128 devices in a mesh: freq: 8 (over z, x_lo), gx: 4 (over y), gy: 4 (over x_hi, core).
Axes of the slice: x: 4 (x_hi: 2, x_lo: 2; x = x_hi * 2 + x_lo), y: 4, z: 4, core: 2. Of those that a mesh axis runs over, the one named last changes fastest.
Arguments:
- wavefield: float32 [32, 2, 512, 512], P('freq', None, 'gx', 'gy'), may hold values from -6 to 6
- velocity: float32 [4, 512, 512], P(None, ('gx', 'freq'), 'gy'), may hold values from 1.5 to 4.5
Outputs:
- image: float32 [4, 512, 512], P(None, 'gx', 'gy')
- extrapolated: float32 [32, 2, 512, 512], P('freq', None, 'gx', 'gy')
The draws below stay inside these ranges and needn't reach their ends.
All inputs are finite; a program needn't handle non-finite values.
Results may differ from the reference program's by a relative error of at most 0.0001.
Values sent between devices are 32-bit elements; how exact they have to be, the bound alone decides.
A program may use at most 128 MiB of HBM per device.

```python
import math
import jax
import jax.numpy as jnp
from jax import lax

ORDER = 8
STEPS = 4
FREQS = 32
NX = 512
NY = 512


def levels(stream_key, extent, shards, least, high):
    loudness = 1.0
    for position, blocks in shards:
        heights = jax.random.uniform(jax.random.fold_in(jax.random.fold_in(stream_key, 6), position), (blocks,), jnp.float32, least / len(shards), high / len(shards))
        loudness = loudness * jnp.repeat(jnp.exp(heights), extent[position] // blocks).reshape((-1,) + (1,) * (len(extent) - 1 - position))
    return loudness


def normal_values(stream_key, shape, deviation, limit, shards=(), dtype=jnp.bfloat16):
    values = jax.random.normal(stream_key, shape, jnp.float32) * deviation
    if len(shards) > 0:
        values = levels(stream_key, shape, shards, -0.22, 0.18) * values
    return jnp.clip(values, min=-limit, max=limit).astype(dtype)


def setup_inputs(seed: int = 0) -> dict:
    keys = jax.random.split(jax.random.key(seed), 3)
    return {
        "wavefield": normal_values(keys[0], (FREQS, 2, NX, NY), 1.0, 6.0, ((0, 8), (2, 4), (3, 4)), jnp.float32),
        "velocity": jnp.clip(jnp.exp(math.log(4.5) - 1.0986123 * jax.random.uniform(keys[1], (STEPS, NX, NY), jnp.float32) ** levels(keys[1], (STEPS, NX, NY), ((1, 32), (2, 4)), -0.2, 0.2)), 1.5, 4.5),
    }


lowest_freq = 2.0
highest_freq = 60.0
depth_interval = 0.01

def stencil(source):
    centre = source[..., 1:-1, 1:-1]
    along_x = source[..., 2:, 1:-1] + source[..., :-2, 1:-1]
    along_y = source[..., 1:-1, 2:] + source[..., 1:-1, :-2]
    diagonal_sum = source[..., 2:, 2:] + source[..., 2:, :-2] + source[..., :-2, 2:] + source[..., :-2, :-2]
    return -0.5 * centre + 0.25 * (along_x + along_y) + 0.125 * diagonal_sum

def padded_stencil(source):
    return stencil(jnp.pad(source, ((0, 0), (0, 0), (1, 1), (1, 1))))

def term_weights(order):
    values = [1.0 / (term + 1) for term in range(order + 1)]
    whole = sum(values)
    return [value / whole for value in values]

def add_term(real_part, imag_part, part, phase_base, term, weight):
    phase = phase_base * ((term + 1) / (ORDER + 1))
    cosine = jnp.cos(phase)
    sine = jnp.sin(phase)
    real_part = real_part + weight * (cosine * part[:, 0] - sine * part[:, 1])
    imag_part = imag_part + weight * (sine * part[:, 0] + cosine * part[:, 1])
    return (real_part, imag_part)

def reference(wavefield, velocity):
    weights = term_weights(ORDER)
    angular = 2.0 * math.pi * (lowest_freq + (highest_freq - lowest_freq) * (jnp.arange(FREQS).astype(jnp.float32) + 0.5) / FREQS)
    wave_now = wavefield
    image_rows = []
    for depth in range(STEPS):
        phase_base = angular[:, None, None] * depth_interval / velocity[depth][None]
        zeros = jnp.zeros(wave_now[:, 0].shape, jnp.float32)
        real_part, imag_part = add_term(zeros, zeros, wave_now, phase_base, 0, weights[0])
        previous = wave_now
        present = padded_stencil(wave_now)
        real_part, imag_part = add_term(real_part, imag_part, present, phase_base, 1, weights[1])
        for term in range(2, ORDER + 1):
            following = 2.0 * padded_stencil(present) - previous
            previous = present
            present = following
            real_part, imag_part = add_term(real_part, imag_part, present, phase_base, term, weights[term])
        wave_now = jnp.stack([real_part, imag_part], axis=1)
        image_rows.append(lax.optimization_barrier(jnp.sum(real_part, axis=0)) / math.sqrt(FREQS))
    return (jnp.stack(image_rows), wave_now)
```

```python
import functools
import math

import jax
import jax.numpy as jnp
from jax import lax
from jax.experimental import pallas as pl
from jax.experimental.pallas import tpu as pltpu
from jax.sharding import PartitionSpec as P

ORDER = 8
LOWEST = 2.0
HIGHEST = 60.0
INTERVAL = 0.01
MESH = pl.DeviceIdType.MESH

SPAN = 2
LANE_BLOCKS = 16
SUB_BLOCKS = 8


def term_weights(order):
    values = [1.0 / (term + 1) for term in range(order + 1)]
    whole = sum(values)
    return [value / whole for value in values]


def kernel(
    dims,
    wave_hbm, vel_hbm, image_hbm, out_hbm,
    terms, pair_sum, quarter, slow, rows_buf, tile, edge_r, edge_l, halo_l, halo_r, natural,
    vel_tile, vel_edge_r, vel_edge_l, vel_halo_l, vel_halo_r,
    part_image, image_in, image_out,
    load_sem, wave_send, wave_recv, vel_send, vel_recv, velh_send, velh_recv,
    red_send, red_recv, cast_send, cast_recv, store_sem,
):
    depths, span, freqs, side, fcount, xcount, ycount = dims
    order = ORDER
    weights = term_weights(order)
    reach = order * span
    extent = side + 2 * reach
    nx = extent // LANE_BLOCKS
    ny = extent // SUB_BLOCKS
    slab_rows = nx * 8
    batch = 2 * freqs
    inner = min(batch, 128 // reach)
    groups = batch // inner
    strip = side // fcount
    rounds = depths // span

    me_f = lax.axis_index("freq")
    me_x = lax.axis_index("gx")
    me_y = lax.axis_index("gy")

    def mod(value, count):
        return lax.rem(value + count, count)

    up, down = mod(me_x - 1, xcount), mod(me_x + 1, xcount)
    left, right = mod(me_y - 1, ycount), mod(me_y + 1, ycount)
    around = [
        {"gx": up, "gy": me_y}, {"gx": down, "gy": me_y}, {"gx": me_x, "gy": right}, {"gx": me_x, "gy": left},
        {"gx": up, "gy": right}, {"gx": down, "gy": right}, {"gx": up, "gy": left}, {"gx": down, "gy": left},
    ]
    peers = [mod(me_f + k, fcount) for k in range(1, fcount)]

    loads = []
    for f in range(freqs):
        for part in range(2):
            loads.append(
                pltpu.make_async_copy(
                    wave_hbm.at[f, part], tile.at[0, part * freqs + f, pl.ds(reach, side)], load_sem.at[f * 2 + part]
                )
            )
    own_rows = pl.multiple_of(reach + me_f * strip, 8)
    vel_load = pltpu.make_async_copy(vel_hbm, vel_tile.at[:, pl.ds(own_rows, strip)], load_sem.at[batch])
    for copy in loads:
        copy.start()
    vel_load.start()

    barrier = pltpu.get_barrier_semaphore()
    for device in around:
        pl.semaphore_signal(barrier, inc=1, device_id=device, device_id_type=MESH)
    for peer in peers:
        pl.semaphore_signal(barrier, inc=1, device_id={"freq": peer}, device_id_type=MESH)

    lane = lax.broadcasted_iota(jnp.int32, (1, 128), 1)
    for copy in loads:
        copy.wait()
    vel_load.wait()

    def build_edges(r):
        def place(source, columns_end):
            for g in range(groups):
                made = None
                for k in range(inner):
                    cells = source(k * groups + g)
                    shift = (k * reach - columns_end) % 128
                    moved = cells if shift == 0 else pltpu.roll(cells, shift, 1)
                    made = moved if made is None else jnp.where(lane >= k * reach, moved, made)
                yield g, made

        def step(i, _):
            rows = pl.ds(pl.multiple_of(i * 32, 32), 32)
            source_rows = pl.ds(pl.multiple_of(reach + i * 32, 8), 32)
            for g, made in place(lambda b: tile[r, b, source_rows, :], side - reach):
                edge_r[r, g, rows, :] = made
            for g, made in place(lambda b: tile[r, b, source_rows, :], 0):
                edge_l[r, g, rows, :] = made
            return 0

        lax.fori_loop(0, side // 32, step, 0)

    def wave_copies(r):
        head, tail = pl.ds(0, reach), pl.ds(side - reach, reach)
        low, mid, high = pl.ds(0, reach), pl.ds(reach, side), pl.ds(reach + side, reach)
        own_head, own_tail = pl.ds(reach, reach), pl.ds(side, reach)
        pairs = [
            (tile.at[r, :, own_head], tile.at[r, :, high]),
            (tile.at[r, :, own_tail], tile.at[r, :, low]),
            (edge_r.at[r], halo_l.at[r, :, mid]),
            (edge_l.at[r], halo_r.at[r, :, mid]),
            (edge_r.at[r, :, head], halo_l.at[r, :, high]),
            (edge_r.at[r, :, tail], halo_l.at[r, :, low]),
            (edge_l.at[r, :, head], halo_r.at[r, :, high]),
            (edge_l.at[r, :, tail], halo_r.at[r, :, low]),
        ]
        return [
            pltpu.make_async_remote_copy(
                src_ref=source, dst_ref=target, send_sem=wave_send.at[r, k], recv_sem=wave_recv.at[r, k],
                device_id=around[k], device_id_type=MESH,
            )
            for k, (source, target) in enumerate(pairs)
        ]

    def vel_copies():
        return [
            pltpu.make_async_remote_copy(
                src_ref=vel_tile.at[:, pl.ds(own_rows, strip)], dst_ref=vel_tile.at[:, pl.ds(own_rows, strip)],
                send_sem=vel_send.at[k], recv_sem=vel_recv.at[k],
                device_id={"freq": peer}, device_id_type=MESH,
            )
            for k, peer in enumerate(peers)
        ]

    def vel_halo_copies():
        head, tail = pl.ds(0, reach), pl.ds(side - reach, reach)
        low, mid, high = pl.ds(0, reach), pl.ds(reach, side), pl.ds(reach + side, reach)
        own_head, own_tail = pl.ds(reach, reach), pl.ds(side, reach)
        pairs = [
            (vel_tile.at[:, own_head], vel_tile.at[:, high]),
            (vel_tile.at[:, own_tail], vel_tile.at[:, low]),
            (vel_edge_r, vel_halo_l.at[mid]),
            (vel_edge_l, vel_halo_r.at[mid]),
            (vel_edge_r.at[head], vel_halo_l.at[high]),
            (vel_edge_r.at[tail], vel_halo_l.at[low]),
            (vel_edge_l.at[head], vel_halo_r.at[high]),
            (vel_edge_l.at[tail], vel_halo_r.at[low]),
        ]
        return [
            pltpu.make_async_remote_copy(
                src_ref=source, dst_ref=target, send_sem=velh_send.at[k], recv_sem=velh_recv.at[k],
                device_id=around[k], device_id_type=MESH,
            )
            for k, (source, target) in enumerate(pairs)
        ]

    build_edges(0)
    pl.semaphore_wait(barrier, len(around) + len(peers))
    first_wave = wave_copies(0)
    for copy in first_wave:
        copy.start()
    vel_sends = vel_copies()
    for copy in vel_sends:
        copy.start()

    lanes8 = lax.broadcasted_iota(jnp.int32, (8, 128), 1)
    subs8 = lax.broadcasted_iota(jnp.int32, (8, 128), 0)
    x_base = me_x * side - reach + lax.rem(lanes8, LANE_BLOCKS) * nx
    y_base = me_y * side - reach + subs8 * ny

    def fill_quarter(yi, _):
        inside_y = jnp.where((y_base + yi >= 0) & (y_base + yi < ycount * side), 0.25, 0.0)
        for xi in range(nx):
            inside = jnp.where((x_base + xi >= 0) & (x_base + xi < xcount * side), inside_y, 0.0)
            quarter[pl.ds(pl.multiple_of(yi * slab_rows + xi * 8, 8), 8), :] = inside
        return 0

    lax.fori_loop(0, ny, fill_quarter, 0)

    per_step = 4 if nx % 4 == 0 else (3 if nx % 3 == 0 else 2)

    def gather_blocks(load):
        pieces = []
        for half in range(LANE_BLOCKS // 8):
            pieces.append(load(half * 8 * nx))
        return pieces

    def assemble_wave(r):
        def some(i, _):
            for j in range(per_step):
                xi = i * per_step + j
                pieces = []
                for b in range(batch):
                    pieces += gather_blocks(lambda start: tile[r, b, pl.ds(xi + start, 8, stride=nx), :])
                rows_buf[xi, pl.ds(reach, side), :] = jnp.concatenate(pieces, axis=0).T
                from_l, from_r = [], []
                for g in range(groups):
                    from_l += gather_blocks(lambda start: halo_l[r, g, pl.ds(xi + start, 8, stride=nx), :])
                    from_r += gather_blocks(lambda start: halo_r[r, g, pl.ds(xi + start, 8, stride=nx), :])
                from_l, from_r = jnp.concatenate(from_l, axis=0), jnp.concatenate(from_r, axis=0)
                pieces = []
                for k in range(inner):
                    moved_l = from_l if k == 0 else pltpu.roll(from_l, 128 - k * reach, 1)
                    shift = (reach - k * reach) % 128
                    moved_r = from_r if shift == 0 else pltpu.roll(from_r, shift, 1)
                    pieces.append(jnp.where(lane < reach, moved_l, moved_r))
                beside = jnp.concatenate(pieces, axis=0).T
                rows_buf[xi, pl.ds(0, reach), :] = beside[:reach]
                rows_buf[xi, pl.ds(reach + side, reach), :] = beside[reach : 2 * reach]
            return 0

        lax.fori_loop(0, nx // per_step, some, 0)

        def pack(xi, _):
            for yi in range(ny):
                rows = pl.ds(pl.multiple_of(yi * slab_rows + xi * 8, 8), 8)
                terms[0, rows, :] = rows_buf[xi, pl.ds(yi, 8, stride=ny), :] * (quarter[rows, :] * 4.0)
            return 0

        lax.fori_loop(0, nx, pack, 0)

    with_vel_halo = span > 1

    def assemble_vel(d):
        def some(i, _):
            for j in range(per_step):
                xi = i * per_step + j
                pieces = gather_blocks(lambda start: vel_tile[d, pl.ds(xi + start, 8, stride=nx), :])
                rows_buf[xi, pl.ds(reach, side), :] = jnp.concatenate(pieces * batch, axis=0).T
                if with_vel_halo:
                    from_l = jnp.concatenate(gather_blocks(lambda start: vel_halo_l[pl.ds(xi + start, 8, stride=nx), :]), axis=0)
                    from_r = jnp.concatenate(gather_blocks(lambda start: vel_halo_r[pl.ds(xi + start, 8, stride=nx), :]), axis=0)
                    shift_l = (-(32 * d + 32 - reach)) % 128
                    shift_r = (reach - 32 * d) % 128
                    moved_l = from_l if shift_l == 0 else pltpu.roll(from_l, shift_l, 1)
                    moved_r = from_r if shift_r == 0 else pltpu.roll(from_r, shift_r, 1)
                    both = jnp.where(lane < reach, moved_l, moved_r)
                    beside = jnp.concatenate([both] * batch, axis=0).T
                    rows_buf[xi, pl.ds(0, reach), :] = beside[:reach]
                    rows_buf[xi, pl.ds(reach + side, reach), :] = beside[reach : 2 * reach]
                else:
                    rows_buf[xi, pl.ds(0, reach), :] = jnp.ones((reach, 128), jnp.float32)
                    rows_buf[xi, pl.ds(reach + side, reach), :] = jnp.ones((reach, 128), jnp.float32)
            return 0

        lax.fori_loop(0, nx // per_step, some, 0)

        def pack(xi, _):
            for yi in range(ny):
                rows = pl.ds(pl.multiple_of(yi * slab_rows + xi * 8, 8), 8)
                slow[d, rows, :] = (INTERVAL / (order + 1)) / rows_buf[xi, pl.ds(yi, 8, stride=ny), :]
            return 0

        lax.fori_loop(0, nx, pack, 0)

    def slab(n, yi):
        return terms[n, pl.ds(yi * slab_rows, slab_rows), :].reshape(nx, 8, 128)

    def x_sum(cells):
        before = pltpu.roll(cells[nx - 1 : nx], 1, 2)
        after = pltpu.roll(cells[0:1], 127, 2)
        wide = jnp.concatenate([before, cells, after], axis=0)
        twos = wide[:-1] + wide[1:]
        return twos[:-1] + twos[1:]

    def next_term(n, first):
        here = slab(n, 0)
        sum_here = x_sum(here)
        sum_first = sum_here
        twos = pltpu.roll(x_sum(slab(n, ny - 1)), 1, 1) + sum_here
        for yi in range(ny):
            if yi + 1 < ny:
                after = slab(n, yi + 1)
                sum_after = x_sum(after)
            else:
                after = None
                sum_after = pltpu.roll(sum_first, 7, 1)
            twos_after = sum_here + sum_after
            nine = twos + twos_after
            rows = pl.ds(yi * slab_rows, slab_rows)
            scale = quarter[rows, :].reshape(nx, 8, 128)
            if first:
                pair = (0.5 * scale) * nine
            else:
                pair = scale * nine - pair_sum[rows, :].reshape(nx, 8, 128)
            pair_sum[rows, :] = pair.reshape(slab_rows, 128)
            terms[n + 1, rows, :] = (pair - here).reshape(slab_rows, 128)
            twos, sum_here, here = twos_after, sum_after, after

    def all_terms():
        next_term(0, True)

        def body(n, _):
            next_term(n, False)
            return 0

        lax.fori_loop(1, order, body, 0)

    frequency = me_f * freqs + lax.rem(lanes8 // LANE_BLOCKS, freqs)
    omega = (2.0 * math.pi) * (
        LOWEST + (HIGHEST - LOWEST) * (frequency.astype(jnp.float32) + 0.5) / (freqs * fcount)
    )
    sign = jnp.where(lanes8 < 64, -1.0, 1.0)

    vregs = nx * ny
    chunk = max(c for c in range(8, 37) if vregs % c == 0)

    def phase_sum(d):
        def body(i, _):
            rows = pl.ds(pl.multiple_of(i * chunk * 8, 8), chunk * 8)

            def term(n):
                return terms[n, rows, :].reshape(chunk, 8, 128)

            angle = omega * slow[d, rows, :].reshape(chunk, 8, 128)
            square = angle * angle
            cosine = 1.0 + square * (-0.5 + square * (1 / 24.0 + square * (-1 / 720.0 + square * (1 / 40320.0))))
            sine = angle * (sign * (1.0 + square * (-1 / 6.0 + square * (1 / 120.0 + square * (-1 / 5040.0)))))
            double = cosine + cosine
            later = weights[order] * term(order)
            now = weights[order - 1] * term(order - 1) + double * later
            for n in range(order - 2, -1, -1):
                now, later = weights[n] * term(n) + double * now - later, now
            new = cosine * now + sine * pltpu.roll(now, 64, 2) - later
            terms[0, rows, :] = new.reshape(chunk * 8, 128)
            return 0

        lax.fori_loop(0, vregs // chunk, body, 0)

    def to_natural(d, whole):
        def unpack(xi, _):
            for yi in range(ny):
                rows = pl.ds(pl.multiple_of(yi * slab_rows + xi * 8, 8), 8)
                rows_buf[xi, pl.ds(yi, 8, stride=ny), :] = terms[0, rows, :]
            return 0

        lax.fori_loop(0, nx, unpack, 0)

        def some(i, _):
            for j in range(per_step):
                xi = i * per_step + j
                turned = rows_buf[xi, pl.ds(reach, side), :].T
                for half in range(LANE_BLOCKS // 8):
                    target = pl.ds(xi + half * 8 * nx, 8, stride=nx)
                    blocks = [turned[b * 16 + half * 8 : b * 16 + half * 8 + 8] for b in range(batch)]
                    if whole:
                        for b in range(batch):
                            natural[b, target, :] = blocks[b]
                    total = blocks[0]
                    for b in range(1, freqs):
                        total = total + blocks[b]
                    part_image[d, target, :] = total
            return 0

        lax.fori_loop(0, nx // per_step, some, 0)

    def reduce_copies(d):
        return [
            pltpu.make_async_remote_copy(
                src_ref=part_image.at[d, pl.ds(pl.multiple_of(reach + peer * strip, 8), strip)],
                dst_ref=image_in.at[d, k],
                send_sem=red_send.at[d, k], recv_sem=red_recv.at[d, k],
                device_id={"freq": peer}, device_id_type=MESH,
            )
            for k, peer in enumerate(peers)
        ]

    image_rows = pl.ds(pl.multiple_of(me_f * strip, 8), strip)

    def cast_copies(d):
        return [
            pltpu.make_async_remote_copy(
                src_ref=image_out.at[d, image_rows], dst_ref=image_out.at[d, image_rows],
                send_sem=cast_send.at[d, k], recv_sem=cast_recv.at[d, k],
                device_id={"freq": peer}, device_id_type=MESH,
            )
            for k, peer in enumerate(peers)
        ]

    sent_images = {}

    def send_image(d):
        sent_images[d] = reduce_copies(d)
        for copy in sent_images[d]:
            copy.start()

    def finish_image(d):
        for copy in sent_images[d]:
            copy.wait()
        total = part_image[d, pl.ds(own_rows, strip), :]
        for k in range(fcount - 1):
            total = total + image_in[d, k]
        image_out[d, image_rows, :] = total * (1.0 / math.sqrt(freqs * fcount))
        casts = cast_copies(d)
        for copy in casts:
            copy.start()
        return casts

    casts = []
    for r in range(rounds):
        if r == 0:
            copies = first_wave
            for copy in vel_sends:
                copy.wait()
            if with_vel_halo:
                for source, target in ((96, vel_edge_r), (0, vel_edge_l)):
                    made = None
                    for d in range(depths):
                        cells = vel_tile[d, pl.ds(reach, side), :]
                        shift = (32 * d - source) % 128
                        moved = cells if shift == 0 else pltpu.roll(cells, shift, 1)
                        made = moved if made is None else jnp.where(lane >= 32 * d, moved, made)
                    target[...] = made
                vel_sends = vel_halo_copies()
                for copy in vel_sends:
                    copy.start()
            else:
                for d in range(depths):
                    vel_tile[d, pl.ds(0, reach), :] = jnp.ones((reach, side), jnp.float32)
                    vel_tile[d, pl.ds(reach + side, reach), :] = jnp.ones((reach, side), jnp.float32)
        else:
            for b in range(batch):
                tile[r, b, pl.ds(reach, side), :] = natural[b, pl.ds(reach, side), :]
            build_edges(r)
            copies = wave_copies(r)
            for copy in copies:
                copy.start()
        if r == 0 and not with_vel_halo:
            for d in range(depths):
                assemble_vel(d)
        for copy in copies:
            copy.wait()
        assemble_wave(r)
        for step in range(span):
            d = r * span + step
            all_terms()
            if d == 0 and with_vel_halo:
                for copy in vel_sends:
                    copy.wait()
                for e in range(depths):
                    assemble_vel(e)
            if d > 0:
                casts += finish_image(d - 1)
            phase_sum(d)
            to_natural(d, step == span - 1)
            send_image(d)
    stores = []
    for f in range(freqs):
        for part in range(2):
            stores.append(
                pltpu.make_async_copy(
                    natural.at[part * freqs + f, pl.ds(reach, side)], out_hbm.at[f, part], store_sem.at[f * 2 + part]
                )
            )
    for copy in stores:
        copy.start()
    casts += finish_image(depths - 1)
    for copy in casts:
        copy.wait()
    last = pltpu.make_async_copy(image_out, image_hbm, store_sem.at[batch])
    last.start()
    for copy in stores:
        copy.wait()
    last.wait()


def per_device(wavefield, velocity):
    freqs, _, side, _ = wavefield.shape
    depths = velocity.shape[0]
    fcount, xcount, ycount = lax.axis_size("freq"), lax.axis_size("gx"), lax.axis_size("gy")
    span = SPAN
    rounds = depths // span
    reach = ORDER * span
    extent = side + 2 * reach
    nx, ny = extent // LANE_BLOCKS, extent // SUB_BLOCKS
    cells = nx * ny * 8
    batch = 2 * freqs
    inner = min(batch, 128 // reach)
    groups = batch // inner
    strip = side // fcount
    dims = (depths, span, freqs, side, fcount, xcount, ycount)
    f32 = jnp.float32
    dma = pltpu.SemaphoreType.DMA
    image, extrapolated = pl.pallas_call(
        functools.partial(kernel, dims),
        out_shape=(
            jax.ShapeDtypeStruct((depths, side, side), f32),
            jax.ShapeDtypeStruct(wavefield.shape, f32),
        ),
        in_specs=[pl.BlockSpec(memory_space=pl.ANY)] * 2,
        out_specs=(pl.BlockSpec(memory_space=pl.ANY),) * 2,
        scratch_shapes=[
            pltpu.VMEM((ORDER + 1, cells, 128), f32),
            pltpu.VMEM((cells, 128), f32),
            pltpu.VMEM((cells, 128), f32),
            pltpu.VMEM((depths, cells, 128), f32),
            pltpu.VMEM((nx, extent, 128), f32),
            pltpu.VMEM((rounds, batch, extent, 128), f32),
            pltpu.VMEM((rounds, groups, side, 128), f32),
            pltpu.VMEM((rounds, groups, side, 128), f32),
            pltpu.VMEM((rounds, groups, extent, 128), f32),
            pltpu.VMEM((rounds, groups, extent, 128), f32),
            pltpu.VMEM((batch, extent, 128), f32),
            pltpu.VMEM((depths, extent, 128), f32),
            pltpu.VMEM((side, 128), f32),
            pltpu.VMEM((side, 128), f32),
            pltpu.VMEM((extent, 128), f32),
            pltpu.VMEM((extent, 128), f32),
            pltpu.VMEM((depths, extent, 128), f32),
            pltpu.VMEM((depths, fcount - 1, strip, 128), f32),
            pltpu.VMEM((depths, side, 128), f32),
            dma((batch + 1,)),
            dma((rounds, 8)),
            dma((rounds, 8)),
            dma((fcount - 1,)),
            dma((fcount - 1,)),
            dma((8,)),
            dma((8,)),
            dma((depths, fcount - 1)),
            dma((depths, fcount - 1)),
            dma((depths, fcount - 1)),
            dma((depths, fcount - 1)),
            dma((batch + 1,)),
        ],
        compiler_params=pltpu.CompilerParams(
            collective_id=0, has_side_effects=True, vmem_limit_bytes=56 * 1024 * 1024
        ),
    )(wavefield, velocity)
    return (image, extrapolated)


def solution(mesh):
    placed = (P("freq", None, "gx", "gy"), P(None, ("gx", "freq"), "gy"))
    return jax.shard_map(
        per_device,
        mesh=mesh,
        in_specs=placed,
        out_specs=(P(None, "gx", "gy"), P("freq", None, "gx", "gy")),
        check_vma=False,
    )
```

```python
import functools
import math

import jax
import jax.numpy as jnp
from jax import lax
from jax.experimental import pallas as pl
from jax.experimental.pallas import tpu as pltpu
from jax.sharding import PartitionSpec as P

ORDER = 8
LOWEST = 2.0
HIGHEST = 60.0
INTERVAL = 0.01
MESH = pl.DeviceIdType.MESH
SUB_BLOCKS = 8


def ratios(order):
    return [1.0 / (term + 1) for term in range(order + 1)]


def shared_weight(order):
    return 1.0 / sum(1.0 / (term + 1) for term in range(order + 1))


def rolled(cells, shift, axis):
    shift = shift % cells.shape[axis]
    return cells if shift == 0 else pltpu.roll(cells, shift, axis)


def kernel(
    dims,
    wave_hbm, vel_hbm, image_hbm, out_hbm,
    terms, pair_sum, quarter, rows_buf, slow_rows, tile, edge_r, edge_l, halo_l, halo_r, natural,
    vel_raw, slow_tile, slow_edge_r, slow_edge_l, slow_halo_l, slow_halo_r,
    part_image, image_in, image_out,
    load_sem, wave_send, wave_recv, vel_send, vel_recv, velh_send, velh_recv,
    red_send, red_recv, cast_send, cast_recv, store_sem,
):
    depths, freqs, side, fcount, xcount, ycount = dims
    order = ORDER
    weights = ratios(order)
    reach = order * depths
    extent = side + 2 * reach
    lane_blocks = 128 // freqs
    octets = lane_blocks // 8
    nx = extent // lane_blocks
    slab_rows = 2 * nx * 8
    batch = 2 * freqs
    inner = 128 // reach
    groups = batch // inner
    strip = side // fcount
    around_y = [reach - order * d for d in range(depths)]
    blocks_y = [(side + 2 * h) // SUB_BLOCKS for h in around_y]

    me_f = lax.axis_index("freq")
    me_x = lax.axis_index("gx")
    me_y = lax.axis_index("gy")

    def mod(value, count):
        return lax.rem(value + count, count)

    up, down = mod(me_x - 1, xcount), mod(me_x + 1, xcount)
    left, right = mod(me_y - 1, ycount), mod(me_y + 1, ycount)
    around = [
        {"gx": up, "gy": me_y}, {"gx": down, "gy": me_y}, {"gx": me_x, "gy": right}, {"gx": me_x, "gy": left},
        {"gx": up, "gy": right}, {"gx": down, "gy": right}, {"gx": up, "gy": left}, {"gx": down, "gy": left},
    ]
    peers = [mod(me_f + k, fcount) for k in range(1, fcount)]

    barrier = pltpu.get_barrier_semaphore()
    for device in around:
        pl.semaphore_signal(barrier, inc=1, device_id=device, device_id_type=MESH)
    for peer in peers:
        pl.semaphore_signal(barrier, inc=1, device_id={"freq": peer}, device_id_type=MESH)

    vel_load = pltpu.make_async_copy(vel_hbm, vel_raw, load_sem.at[batch])
    vel_load.start()
    loads = []
    for f in range(freqs):
        for part in range(2):
            loads.append(
                pltpu.make_async_copy(
                    wave_hbm.at[f, part], tile.at[part * freqs + f, pl.ds(reach, side)], load_sem.at[f * 2 + part]
                )
            )
    for copy in loads:
        copy.start()

    own_rows = pl.ds(pl.multiple_of(reach + me_f * strip, 8), strip)
    vel_load.wait()
    slow_tile[:, own_rows, :] = (INTERVAL / (order + 1)) / vel_raw[...]
    for copy in loads:
        copy.wait()

    lane = lax.broadcasted_iota(jnp.int32, (1, 128), 1)

    def build_edges(i, _):
        rows = pl.ds(pl.multiple_of(i * 32, 32), 32)
        source_rows = pl.ds(pl.multiple_of(reach + i * 32, 8), 32)
        for target, first in ((edge_r, side - reach), (edge_l, 0)):
            for g in range(groups):
                made = None
                for k in range(inner):
                    moved = rolled(tile[k * groups + g, source_rows, :], k * reach - first, 1)
                    made = moved if made is None else jnp.where(lane >= k * reach, moved, made)
                target[g, rows, :] = made
        return 0

    lax.fori_loop(0, side // 32, build_edges, 0)

    head, tail = pl.ds(0, reach), pl.ds(side - reach, reach)
    low, mid, high = pl.ds(0, reach), pl.ds(reach, side), pl.ds(reach + side, reach)
    own_head, own_tail = pl.ds(reach, reach), pl.ds(side, reach)

    def to_neighbours(pairs, send_sem, recv_sem):
        return [
            pltpu.make_async_remote_copy(
                src_ref=source, dst_ref=target, send_sem=send_sem.at[k], recv_sem=recv_sem.at[k],
                device_id=around[k], device_id_type=MESH,
            )
            for k, (source, target) in enumerate(pairs)
        ]

    def to_peers(pairs, send_sem, recv_sem):
        return [
            pltpu.make_async_remote_copy(
                src_ref=source, dst_ref=target, send_sem=send_sem.at[k], recv_sem=recv_sem.at[k],
                device_id={"freq": peers[k]}, device_id_type=MESH,
            )
            for k, (source, target) in enumerate(pairs)
        ]

    def start(copies):
        for copy in copies:
            copy.start()
        return copies

    def wait(copies):
        for copy in copies:
            copy.wait()

    wave_copies = to_neighbours(
        [
            (tile.at[:, own_head], tile.at[:, high]),
            (tile.at[:, own_tail], tile.at[:, low]),
            (edge_r, halo_l.at[:, mid]),
            (edge_l, halo_r.at[:, mid]),
            (edge_r.at[:, head], halo_l.at[:, high]),
            (edge_r.at[:, tail], halo_l.at[:, low]),
            (edge_l.at[:, head], halo_r.at[:, high]),
            (edge_l.at[:, tail], halo_r.at[:, low]),
        ],
        wave_send, wave_recv,
    )
    stages = [(0, 1), (1, depths - 1)]

    def slow_peer_copies(stage):
        first, count = stages[stage]
        block = slow_tile.at[pl.ds(first, count), own_rows]
        return to_peers([(block, block)] * (fcount - 1), vel_send.at[stage], vel_recv.at[stage])

    def slow_halo_copies(stage):
        first, count = stages[stage]
        of = pl.ds(first, count)
        return to_neighbours(
            [
                (slow_tile.at[of, own_head], slow_tile.at[of, high]),
                (slow_tile.at[of, own_tail], slow_tile.at[of, low]),
                (slow_edge_r.at[stage], slow_halo_l.at[stage, mid]),
                (slow_edge_l.at[stage], slow_halo_r.at[stage, mid]),
                (slow_edge_r.at[stage, head], slow_halo_l.at[stage, high]),
                (slow_edge_r.at[stage, tail], slow_halo_l.at[stage, low]),
                (slow_edge_l.at[stage, head], slow_halo_r.at[stage, high]),
                (slow_edge_l.at[stage, tail], slow_halo_r.at[stage, low]),
            ],
            velh_send.at[stage], velh_recv.at[stage],
        )

    def build_slow_edges(stage):
        first, count = stages[stage]
        for target, source in ((slow_edge_r, side - reach), (slow_edge_l, 0)):
            made = None
            for j in range(count):
                moved = rolled(slow_tile[first + j, pl.ds(reach, side), :], reach * j - source, 1)
                made = moved if made is None else jnp.where(lane >= reach * j, moved, made)
            target[stage] = made

    pl.semaphore_wait(barrier, len(around) + len(peers))
    slow_first = start(slow_peer_copies(0))
    start(wave_copies)
    slow_rest = start(slow_peer_copies(1))

    lanes8 = lax.broadcasted_iota(jnp.int32, (8, 128), 1)
    subs8 = lax.broadcasted_iota(jnp.int32, (8, 128), 0)

    def inside_x(xi, lanes):
        x = me_x * side - reach + lax.rem(lanes, lane_blocks) * nx + xi
        return (x >= 0) & (x < xcount * side)

    for d in range(depths):
        def fill_quarter(yi, _):
            y = me_y * side - around_y[d] + subs8 * blocks_y[d] + yi
            inside_y = jnp.where((y >= 0) & (y < ycount * side), 0.25, 0.0)
            for xi in range(nx):
                rows = pl.ds(pl.multiple_of((yi * nx + xi) * 8, 8), 8)
                quarter[d, rows, :] = jnp.where(inside_x(xi, lanes8), inside_y, 0.0)
            return 0

        lax.fori_loop(0, blocks_y[d], fill_quarter, 0)

    def blocks_of(load):
        return jnp.concatenate([load(8 * nx * o) for o in range(octets)], axis=0)

    def place_slow_tile(d):
        for xi in range(nx):
            cells = blocks_of(lambda begin: slow_tile[d, pl.ds(xi + begin, 8, stride=nx), :])
            slow_rows[d, xi, pl.ds(around_y[d], side), :] = jnp.concatenate([cells] * freqs, axis=0).T

    def place_slow_halo(stage):
        first, count = stages[stage]
        for pair in range(0, count, 2):
            for xi in range(nx):
                from_l = blocks_of(lambda begin: slow_halo_l[stage, pl.ds(xi + begin, 8, stride=nx), :])
                from_r = blocks_of(lambda begin: slow_halo_r[stage, pl.ds(xi + begin, 8, stride=nx), :])
                made = jnp.where(lane < reach, rolled(from_l, -reach * pair, 1), rolled(from_r, reach - reach * pair, 1))
                if pair + 1 < count:
                    made = jnp.where(lane < 2 * reach, made, rolled(from_l, reach * (1 - pair), 1))
                    made = jnp.where(lane < 3 * reach, made, rolled(from_r, reach * (2 - pair), 1))
                turned = jnp.concatenate([made] * freqs, axis=0).T
                for j in range(min(2, count - pair)):
                    d = first + pair + j
                    h = around_y[d]
                    base = 2 * reach * j
                    slow_rows[d, xi, pl.ds(0, h), :] = turned[base + reach - h : base + reach]
                    slow_rows[d, xi, pl.ds(h + side, h), :] = turned[base + reach : base + reach + h]

    def assemble_wave():
        ny = blocks_y[0]
        inside_l = jnp.where(me_y > 0, 1.0, 0.0)
        inside_r = jnp.where(me_y < ycount - 1, 1.0, 0.0)

        def put(part, xi, y0, block):
            yb, yi = y0 // ny, y0 % ny
            begin = ((yi * 2 + part) * nx + xi) * 8 + yb
            terms[0, pl.ds(begin, 8, stride=slab_rows), :] = block

        def some(xi, _):
            grid_x = jnp.where(inside_x(xi, lane), 1.0, 0.0)
            for part in range(2):
                cells = jnp.concatenate(
                    [
                        blocks_of(lambda begin: tile[part * freqs + f, pl.ds(xi + begin, 8, stride=nx), :])
                        for f in range(freqs)
                    ],
                    axis=0,
                )
                turned = cells.T * grid_x
                for o in range(side // 8):
                    put(part, xi, reach + 8 * o, turned[8 * o : 8 * o + 8])
                cells = []
                for f in range(freqs):
                    k, g = (part * freqs + f) // groups, (part * freqs + f) % groups
                    from_l = blocks_of(lambda begin: halo_l[g, pl.ds(xi + begin, 8, stride=nx), :])
                    from_r = blocks_of(lambda begin: halo_r[g, pl.ds(xi + begin, 8, stride=nx), :])
                    cells.append(
                        jnp.where(lane < reach, rolled(from_l, -k * reach, 1), rolled(from_r, reach - k * reach, 1))
                    )
                turned = jnp.concatenate(cells, axis=0).T
                beside_l = turned[:reach] * (grid_x * inside_l)
                beside_r = turned[reach : 2 * reach] * (grid_x * inside_r)
                for o in range(reach // 8):
                    put(part, xi, 8 * o, beside_l[8 * o : 8 * o + 8])
                    put(part, xi, reach + side + 8 * o, beside_r[8 * o : 8 * o + 8])
            return 0

        lax.fori_loop(0, nx, some, 0)

    def slab(n, yi):
        return terms[n, pl.ds(yi * slab_rows, slab_rows), :].reshape(2, nx, 8, 128)

    def x_sum(cells):
        before = pltpu.roll(cells[:, nx - 1 : nx], 1, 3)
        after = pltpu.roll(cells[:, 0:1], 127, 3)
        wide = jnp.concatenate([before, cells, after], axis=1)
        twos = wide[:, :-1] + wide[:, 1:]
        return twos[:, :-1] + twos[:, 1:]

    def next_term(d, n, first):
        ny = blocks_y[d]
        here = slab(n, 0)
        sum_here = x_sum(here)
        sum_first = sum_here
        twos = pltpu.roll(x_sum(slab(n, ny - 1)), 1, 2) + sum_here
        for yi in range(ny):
            if yi + 1 < ny:
                after = slab(n, yi + 1)
                sum_after = x_sum(after)
            else:
                after = None
                sum_after = pltpu.roll(sum_first, 7, 2)
            twos_after = sum_here + sum_after
            nine = twos + twos_after
            rows = pl.ds(yi * slab_rows, slab_rows)
            scale = quarter[d, pl.ds(yi * nx * 8, nx * 8), :].reshape(1, nx, 8, 128)
            if first:
                pair = (0.5 * scale) * nine
            else:
                pair = scale * nine - pair_sum[rows, :].reshape(2, nx, 8, 128)
            pair_sum[rows, :] = pair.reshape(slab_rows, 128)
            terms[n + 1, rows, :] = (pair - here).reshape(slab_rows, 128)
            twos, sum_here, here = twos_after, sum_after, after

    def all_terms(d):
        next_term(d, 0, True)

        def body(n, _):
            next_term(d, n, False)
            return 0

        lax.fori_loop(1, order, body, 0)

    frequency = me_f * freqs + lanes8 // lane_blocks
    omega = (2.0 * math.pi) * (
        LOWEST + (HIGHEST - LOWEST) * (frequency.astype(jnp.float32) + 0.5) / (freqs * fcount)
    )

    def phase_sum(d):
        ny = blocks_y[d]

        def chunk(yi0, count):
            rows = pl.ds(pl.multiple_of(yi0 * slab_rows, 8), count * slab_rows)

            def term(n):
                return terms[n, rows, :].reshape(count, 2, nx, 8, 128)

            slow = jnp.concatenate(
                [
                    slow_rows[d, xi, pl.ds(yi0 + j, 8, stride=ny), :][None]
                    for j in range(count)
                    for xi in range(nx)
                ],
                axis=0,
            )
            angle = (omega * slow).reshape(count, 1, nx, 8, 128)
            square = angle * angle
            cosine = 1.0 + square * (-0.5 + square * (1 / 24.0 + square * (-1 / 720.0)))
            sine = angle * (1.0 + square * (-1 / 6.0 + square * (1 / 120.0 + square * (-1 / 5040.0))))
            double = cosine + cosine
            later = weights[order] * term(order)
            now = weights[order - 1] * term(order - 1) + double * later
            for n in range(order - 2, 0, -1):
                now, later = weights[n] * term(n) + double * now - later, now
            now, later = term(0) + double * now - later, now
            straight = cosine * now - later
            real = straight[:, 0] - sine[:, 0] * now[:, 1]
            imag = straight[:, 1] + sine[:, 0] * now[:, 0]
            for j in range(count):
                for xi in range(nx):
                    rows_buf[0, xi, pl.ds(yi0 + j, 8, stride=ny), :] = real[j, xi]
                    rows_buf[1, xi, pl.ds(yi0 + j, 8, stride=ny), :] = imag[j, xi]

        size = 3

        def body(i, _):
            chunk(i * size, size)
            return 0

        lax.fori_loop(0, ny // size, body, 0)
        if ny % size:
            chunk(ny - ny % size, ny % size)

    def turn(part, xi, h):
        return rows_buf[part, xi, pl.ds(h, side), :].T

    def make_image(d):
        def some(i, _):
            for j in range(3):
                xi = i * 3 + j
                turned = turn(0, xi, around_y[d])
                for o in range(octets):
                    total = turned[8 * o : 8 * o + 8]
                    for f in range(1, freqs):
                        total = total + turned[f * lane_blocks + 8 * o : f * lane_blocks + 8 * o + 8]
                    part_image[d, pl.ds(xi + 8 * nx * o, 8, stride=nx), :] = total
                if d + 1 < depths:
                    ny = blocks_y[d + 1]
                    for yi in range(ny):
                        for part in range(2):
                            rows = pl.ds(pl.multiple_of(((yi * 2 + part) * nx + xi) * 8, 8), 8)
                            terms[0, rows, :] = rows_buf[part, xi, pl.ds(order + yi, 8, stride=ny), :]
            return 0

        lax.fori_loop(0, nx // 3, some, 0)

    def make_natural():
        h = around_y[depths - 1]

        def some(i, _):
            for j in range(3):
                xi = i * 3 + j
                for part in range(2):
                    turned = turn(part, xi, h)
                    for f in range(freqs):
                        for o in range(octets):
                            at = f * lane_blocks + 8 * o
                            natural[part * freqs + f, pl.ds(xi + 8 * nx * o, 8, stride=nx), :] = turned[at : at + 8]
            return 0

        lax.fori_loop(0, nx // 3, some, 0)

    image_stages = [(0, depths - 1), (depths - 1, 1)]
    image_rows = pl.ds(pl.multiple_of(me_f * strip, 8), strip)

    def reduce_copies(stage):
        first, count = image_stages[stage]
        of = pl.ds(first, count)
        return to_peers(
            [
                (
                    part_image.at[of, pl.ds(pl.multiple_of(reach + peer * strip, 8), strip)],
                    image_in.at[k, of],
                )
                for k, peer in enumerate(peers)
            ],
            red_send.at[stage], red_recv.at[stage],
        )

    def cast_image(stage):
        first, count = image_stages[stage]
        of = pl.ds(first, count)
        total = part_image[of, own_rows, :]
        for k in range(fcount - 1):
            total = total + image_in[k, of]
        image_out[of, image_rows, :] = total
        block = image_out.at[of, image_rows]
        return start(to_peers([(block, block)] * (fcount - 1), cast_send.at[stage], cast_recv.at[stage]))

    wait(slow_first)
    build_slow_edges(0)
    halo_first = start(slow_halo_copies(0))
    wait(slow_rest)
    build_slow_edges(1)
    halo_rest = start(slow_halo_copies(1))
    wait(halo_first)
    place_slow_tile(0)
    place_slow_halo(0)
    wait(wave_copies)
    assemble_wave()
    casts = []
    for d in range(depths):
        all_terms(d)
        if d == 0:
            wait(halo_rest)
            for e in range(1, depths):
                place_slow_tile(e)
            place_slow_halo(1)
        phase_sum(d)
        make_image(d)
        if d == depths - 2:
            reduced = start(reduce_copies(0))
    last = start(reduce_copies(1))
    wait(reduced)
    casts += cast_image(0)
    make_natural()
    stores = []
    for f in range(freqs):
        for part in range(2):
            stores.append(
                pltpu.make_async_copy(
                    natural.at[part * freqs + f, pl.ds(reach, side)], out_hbm.at[f, part], store_sem.at[f * 2 + part]
                )
            )
    start(stores)
    wait(last)
    casts += cast_image(1)
    wait(casts)
    image_store = pltpu.make_async_copy(image_out, image_hbm, store_sem.at[batch])
    image_store.start()
    wait(stores)
    image_store.wait()


def per_device(wavefield, velocity):
    freqs, _, side, _ = wavefield.shape
    depths = velocity.shape[0]
    fcount, xcount, ycount = lax.axis_size("freq"), lax.axis_size("gx"), lax.axis_size("gy")
    reach = ORDER * depths
    extent = side + 2 * reach
    nx, ny = extent * freqs // 128, extent // SUB_BLOCKS
    cells = nx * ny * 8
    batch = 2 * freqs
    groups = batch * reach // 128
    strip = side // fcount
    dims = (depths, freqs, side, fcount, xcount, ycount)
    f32 = jnp.float32
    dma = pltpu.SemaphoreType.DMA
    image, extrapolated = pl.pallas_call(
        functools.partial(kernel, dims),
        out_shape=(
            jax.ShapeDtypeStruct((depths, side, side), f32),
            jax.ShapeDtypeStruct(wavefield.shape, f32),
        ),
        in_specs=[pl.BlockSpec(memory_space=pl.ANY)] * 2,
        out_specs=(pl.BlockSpec(memory_space=pl.ANY),) * 2,
        scratch_shapes=[
            pltpu.VMEM((ORDER + 1, 2 * cells, 128), f32),
            pltpu.VMEM((2 * cells, 128), f32),
            pltpu.VMEM((depths, cells, 128), f32),
            pltpu.VMEM((2, nx, extent, 128), f32),
            pltpu.VMEM((depths, nx, extent, 128), f32),
            pltpu.VMEM((batch, extent, 128), f32),
            pltpu.VMEM((groups, side, 128), f32),
            pltpu.VMEM((groups, side, 128), f32),
            pltpu.VMEM((groups, extent, 128), f32),
            pltpu.VMEM((groups, extent, 128), f32),
            pltpu.VMEM((batch, extent, 128), f32),
            pltpu.VMEM((depths, strip, 128), f32),
            pltpu.VMEM((depths, extent, 128), f32),
            pltpu.VMEM((2, side, 128), f32),
            pltpu.VMEM((2, side, 128), f32),
            pltpu.VMEM((2, extent, 128), f32),
            pltpu.VMEM((2, extent, 128), f32),
            pltpu.VMEM((depths, extent, 128), f32),
            pltpu.VMEM((fcount - 1, depths, strip, 128), f32),
            pltpu.VMEM((depths, side, 128), f32),
            dma((batch + 1,)),
            dma((8,)),
            dma((8,)),
            dma((2, fcount - 1)),
            dma((2, fcount - 1)),
            dma((2, 8)),
            dma((2, 8)),
            dma((2, fcount - 1)),
            dma((2, fcount - 1)),
            dma((2, fcount - 1)),
            dma((2, fcount - 1)),
            dma((batch + 1,)),
        ],
        compiler_params=pltpu.CompilerParams(
            collective_id=0, has_side_effects=True, vmem_limit_bytes=56 * 1024 * 1024
        ),
    )(wavefield, velocity)
    weight = shared_weight(ORDER)
    scales = jnp.asarray([weight ** (d + 1) / math.sqrt(freqs * fcount) for d in range(depths)], f32)
    return (image * scales[:, None, None], extrapolated * (weight**depths))


def solution(mesh):
    placed = (P("freq", None, "gx", "gy"), P(None, ("gx", "freq"), "gy"))
    return jax.shard_map(
        per_device,
        mesh=mesh,
        in_specs=placed,
        out_specs=(P(None, "gx", "gy"), P("freq", None, "gx", "gy")),
        check_vma=False,
    )
```

```python
import functools
import math

import jax
import jax.numpy as jnp
from jax import lax
from jax.experimental import pallas as pl
from jax.experimental.pallas import tpu as pltpu
from jax.sharding import PartitionSpec as P

ORDER = 8
LOWEST = 2.0
HIGHEST = 60.0
INTERVAL = 0.01
MESH = pl.DeviceIdType.MESH
SUB_BLOCKS = 8


def ratios(order):
    return [1.0 / (term + 1) for term in range(order + 1)]


def shared_weight(order):
    return 1.0 / sum(1.0 / (term + 1) for term in range(order + 1))


def rolled(cells, shift, axis):
    shift = shift % cells.shape[axis]
    return cells if shift == 0 else pltpu.roll(cells, shift, axis)


def kernel(
    dims,
    wave_hbm, vel_hbm, image_ref, out_ref,
    terms, pair_sum, quarter, rows_buf, slow_rows, tile, edge_r, edge_l, halo_l, halo_r, natural,
    vel_raw, slow_tile, slow_edge_r, slow_edge_l, slow_halo_l, slow_halo_r,
    first_edge_r, first_edge_l, first_halo_l, first_halo_r, wide_halo_l, wide_halo_r,
    part_image, image_in, image_out,
    load_sem, wave_send, wave_recv, vel_send, vel_recv, velh_send, velh_recv, rows_send, rows_recv,
    red_send, red_recv, cast_send, cast_recv,
):
    depths, freqs, side, fcount, xcount, ycount = dims
    order = ORDER
    weights = ratios(order)
    reach = order * depths
    extent = side + 2 * reach
    lane_blocks = 128 // freqs
    octets = lane_blocks // 8
    nx = extent // lane_blocks
    slab_rows = 2 * nx * 8
    batch = 2 * freqs
    inner = 128 // reach
    groups = batch // inner
    strip = side // fcount
    around_y = [reach - order * d for d in range(depths)]
    blocks_y = [(side + 2 * h) // SUB_BLOCKS for h in around_y]

    me_f = lax.axis_index("freq")
    me_x = lax.axis_index("gx")
    me_y = lax.axis_index("gy")

    def mod(value, count):
        return lax.rem(value + count, count)

    up, down = mod(me_x - 1, xcount), mod(me_x + 1, xcount)
    left, right = mod(me_y - 1, ycount), mod(me_y + 1, ycount)
    around = [
        {"gx": up, "gy": me_y}, {"gx": down, "gy": me_y}, {"gx": me_x, "gy": right}, {"gx": me_x, "gy": left},
        {"gx": up, "gy": right}, {"gx": down, "gy": right}, {"gx": up, "gy": left}, {"gx": down, "gy": left},
    ]
    peers = [mod(me_f + k, fcount) for k in range(1, fcount)]

    barrier = pltpu.get_barrier_semaphore()
    for device in around:
        pl.semaphore_signal(barrier, inc=1, device_id=device, device_id_type=MESH)
    for peer in peers:
        pl.semaphore_signal(barrier, inc=1, device_id={"freq": peer}, device_id_type=MESH)

    vel_load = pltpu.make_async_copy(vel_hbm, vel_raw, load_sem.at[batch])
    vel_load.start()
    loads = []
    for f in range(freqs):
        for part in range(2):
            loads.append(
                pltpu.make_async_copy(
                    wave_hbm.at[f, part], tile.at[part * freqs + f, pl.ds(reach, side)], load_sem.at[f * 2 + part]
                )
            )
    for copy in loads:
        copy.start()

    own_rows = pl.ds(pl.multiple_of(reach + me_f * strip, 8), strip)
    vel_load.wait()
    slow_tile[:, own_rows, :] = (INTERVAL / (order + 1)) / vel_raw[...]
    for copy in loads:
        copy.wait()

    lane = lax.broadcasted_iota(jnp.int32, (1, 128), 1)

    def build_edges(i, _):
        rows = pl.ds(pl.multiple_of(i * 32, 32), 32)
        source_rows = pl.ds(pl.multiple_of(reach + i * 32, 8), 32)
        for target, first in ((edge_r, side - reach), (edge_l, 0)):
            for g in range(groups):
                made = None
                for k in range(inner):
                    moved = rolled(tile[k * groups + g, source_rows, :], k * reach - first, 1)
                    made = moved if made is None else jnp.where(lane >= k * reach, moved, made)
                target[g, rows, :] = made
        return 0

    lax.fori_loop(0, side // 32, build_edges, 0)

    head, tail = pl.ds(0, reach), pl.ds(side - reach, reach)
    low, mid, high = pl.ds(0, reach), pl.ds(reach, side), pl.ds(reach + side, reach)
    own_head, own_tail = pl.ds(reach, reach), pl.ds(side, reach)

    def to_neighbours(pairs, send_sem, recv_sem):
        return [
            pltpu.make_async_remote_copy(
                src_ref=source, dst_ref=target, send_sem=send_sem.at[k], recv_sem=recv_sem.at[k],
                device_id=around[k], device_id_type=MESH,
            )
            for k, (source, target) in [(k, pair) for k, pair in enumerate(pairs) if pair is not None]
        ]

    def to_peers(pairs, send_sem, recv_sem):
        return [
            pltpu.make_async_remote_copy(
                src_ref=source, dst_ref=target, send_sem=send_sem.at[k], recv_sem=recv_sem.at[k],
                device_id={"freq": peers[k]}, device_id_type=MESH,
            )
            for k, (source, target) in enumerate(pairs)
        ]

    def start(copies):
        for copy in copies:
            copy.start()
        return copies

    def wait(copies):
        for copy in copies:
            copy.wait()

    wave_copies = to_neighbours(
        [
            (tile.at[:, own_head], tile.at[:, high]),
            (tile.at[:, own_tail], tile.at[:, low]),
            (edge_r, halo_l.at[:, mid]),
            (edge_l, halo_r.at[:, mid]),
            (edge_r.at[:, head], halo_l.at[:, high]),
            (edge_r.at[:, tail], halo_l.at[:, low]),
            (edge_l.at[:, head], halo_r.at[:, high]),
            (edge_l.at[:, tail], halo_r.at[:, low]),
        ],
        wave_send, wave_recv,
    )
    stages = [(0, 1), (1, depths - 1)]
    ahead = [reach - order * (d + 1) for d in range(depths)]

    def slow_peer_copies(stage):
        first, count = stages[stage]
        block = slow_tile.at[pl.ds(first, count), own_rows]
        return to_peers([(block, block)] * (fcount - 1), vel_send.at[stage], vel_recv.at[stage])

    def slow_halo_copies(stage):
        copies = []
        for k, d in enumerate([0] if stage == 0 else range(1, depths - 1)):
            w = ahead[d]
            rows = [
                (slow_tile.at[d, pl.ds(reach, w)], slow_tile.at[d, pl.ds(reach + side, w)]),
                (slow_tile.at[d, pl.ds(reach + side - w, w)], slow_tile.at[d, pl.ds(reach - w, w)]),
            ]
            copies += to_neighbours(rows, rows_send.at[stage + k], rows_recv.at[stage + k])
        if stage == 0:
            sides = [(first_edge_r, first_halo_l.at[1]), (first_edge_l, first_halo_r.at[1])]
            for edge, halo in ((first_edge_r, first_halo_l), (first_edge_l, first_halo_r)):
                sides += [(edge, halo.at[2]), (edge, halo.at[0])]
        else:
            w = ahead[1]
            sides = [(slow_edge_r, slow_halo_l.at[mid]), (slow_edge_l, slow_halo_r.at[mid])]
            for edge, halo in ((slow_edge_r, slow_halo_l), (slow_edge_l, slow_halo_r)):
                sides += [
                    (edge.at[pl.ds(0, w)], halo.at[pl.ds(reach + side, w)]),
                    (edge.at[pl.ds(side - w, w)], halo.at[pl.ds(reach - w, w)]),
                ]
        return copies + to_neighbours([None, None] + sides, velh_send.at[stage], velh_recv.at[stage])

    def build_slow_edges(stage):
        if stage == 0:
            for target, source in ((first_edge_r, side - reach), (first_edge_l, 0)):
                made = None
                for j in range(side // reach):
                    moved = rolled(slow_tile[0, pl.ds(reach + reach * j, reach), :], reach * j - source, 1)
                    made = moved if made is None else jnp.where(lane >= reach * j, moved, made)
                target[...] = made
            return
        first, count = stages[stage]
        for target, source in ((slow_edge_r, side - reach), (slow_edge_l, 0)):
            made = None
            for j in range(count):
                moved = rolled(slow_tile[first + j, pl.ds(reach, side), :], reach * j - source, 1)
                made = moved if made is None else jnp.where(lane >= reach * j, moved, made)
            target[...] = made

    def unpack_first_halo():
        for halo, target in ((first_halo_l, wide_halo_l), (first_halo_r, wide_halo_r)):
            target[pl.ds(0, reach), :] = rolled(halo[0], -(side - reach), 1)
            for j in range(side // reach):
                target[pl.ds(reach + reach * j, reach), :] = rolled(halo[1], -reach * j, 1)
            target[pl.ds(reach + side, reach), :] = halo[2]

    for d in range(depths):
        rest = reach - (ahead[d] if d < depths - 1 else 0)
        slow_tile[d, pl.ds(0, rest), :] = jnp.zeros((rest, side), jnp.float32)
        slow_tile[d, pl.ds(extent - rest, rest), :] = jnp.zeros((rest, side), jnp.float32)
    rest = reach - ahead[1]
    for halo in (slow_halo_l, slow_halo_r):
        halo[pl.ds(0, rest), :] = jnp.zeros((rest, side), jnp.float32)
        halo[pl.ds(extent - rest, rest), :] = jnp.zeros((rest, side), jnp.float32)

    pl.semaphore_wait(barrier, len(around) + len(peers))
    slow_first = start(slow_peer_copies(0))
    start(wave_copies)

    lanes8 = lax.broadcasted_iota(jnp.int32, (8, 128), 1)
    subs8 = lax.broadcasted_iota(jnp.int32, (8, 128), 0)

    def inside_x(xi, lanes):
        x = me_x * side - reach + lax.rem(lanes, lane_blocks) * nx + xi
        return (x >= 0) & (x < xcount * side)

    def fill_quarters(d):
        def fill_quarter(yi, _):
            y = me_y * side - around_y[d] + subs8 * blocks_y[d] + yi
            inside_y = jnp.where((y >= 0) & (y < ycount * side), 0.25, 0.0)
            for xi in range(nx):
                rows = pl.ds(pl.multiple_of((yi * nx + xi) * 8, 8), 8)
                quarter[d, rows, :] = jnp.where(inside_x(xi, lanes8), inside_y, 0.0)
            return 0

        lax.fori_loop(0, blocks_y[d], fill_quarter, 0)

    def fill_all_quarters():
        for d in range(depths):
            fill_quarters(d)

    def blocks_of(load):
        return jnp.concatenate([load(8 * nx * o) for o in range(octets)], axis=0)

    def place_slow_tile(d):
        for xi in range(nx):
            cells = blocks_of(lambda begin: slow_tile[d, pl.ds(xi + begin, 8, stride=nx), :])
            slow_rows[d, xi, pl.ds(around_y[d], side), :] = jnp.concatenate([cells] * freqs, axis=0).T

    def place_slow_halo(stage):
        first, count = stages[stage]
        if stage == 0:
            edges_l, edges_r = wide_halo_l, wide_halo_r
        else:
            edges_l, edges_r = slow_halo_l, slow_halo_r
        for pair in range(0, count, 2):
            for xi in range(nx):
                from_l = blocks_of(lambda begin: edges_l[pl.ds(xi + begin, 8, stride=nx), :])
                from_r = blocks_of(lambda begin: edges_r[pl.ds(xi + begin, 8, stride=nx), :])
                made = jnp.where(lane < reach, rolled(from_l, -reach * pair, 1), rolled(from_r, reach - reach * pair, 1))
                if pair + 1 < count:
                    made = jnp.where(lane < 2 * reach, made, rolled(from_l, reach * (1 - pair), 1))
                    made = jnp.where(lane < 3 * reach, made, rolled(from_r, reach * (2 - pair), 1))
                turned = jnp.concatenate([made] * freqs, axis=0).T
                for j in range(min(2, count - pair)):
                    d = first + pair + j
                    h = around_y[d]
                    base = 2 * reach * j
                    slow_rows[d, xi, pl.ds(0, h), :] = turned[base + reach - h : base + reach]
                    slow_rows[d, xi, pl.ds(h + side, h), :] = turned[base + reach : base + reach + h]

    def assemble_wave():
        ny = blocks_y[0]
        inside_l = jnp.where(me_y > 0, 1.0, 0.0)
        inside_r = jnp.where(me_y < ycount - 1, 1.0, 0.0)

        def put(part, xi, y0, block):
            yb, yi = y0 // ny, y0 % ny
            begin = ((yi * 2 + part) * nx + xi) * 8 + yb
            terms[0, pl.ds(begin, 8, stride=slab_rows), :] = block

        def some(xi, _):
            grid_x = jnp.where(inside_x(xi, lane), 1.0, 0.0)
            for part in range(2):
                cells = jnp.concatenate(
                    [
                        blocks_of(lambda begin: tile[part * freqs + f, pl.ds(xi + begin, 8, stride=nx), :])
                        for f in range(freqs)
                    ],
                    axis=0,
                )
                turned = cells.T * grid_x
                for o in range(side // 8):
                    put(part, xi, reach + 8 * o, turned[8 * o : 8 * o + 8])
                cells = []
                for f in range(freqs):
                    k, g = (part * freqs + f) // groups, (part * freqs + f) % groups
                    from_l = blocks_of(lambda begin: halo_l[g, pl.ds(xi + begin, 8, stride=nx), :])
                    from_r = blocks_of(lambda begin: halo_r[g, pl.ds(xi + begin, 8, stride=nx), :])
                    cells.append(
                        jnp.where(lane < reach, rolled(from_l, -k * reach, 1), rolled(from_r, reach - k * reach, 1))
                    )
                turned = jnp.concatenate(cells, axis=0).T
                beside_l = turned[:reach] * (grid_x * inside_l)
                beside_r = turned[reach : 2 * reach] * (grid_x * inside_r)
                for o in range(reach // 8):
                    put(part, xi, 8 * o, beside_l[8 * o : 8 * o + 8])
                    put(part, xi, reach + side + 8 * o, beside_r[8 * o : 8 * o + 8])
            return 0

        lax.fori_loop(0, nx, some, 0)

    def slab(n, yi):
        return terms[n, pl.ds(yi * slab_rows, slab_rows), :].reshape(2, nx, 8, 128)

    def x_sum(cells):
        before = pltpu.roll(cells[:, nx - 1 : nx], 1, 3)
        after = pltpu.roll(cells[:, 0:1], 127, 3)
        wide = jnp.concatenate([before, cells, after], axis=1)
        twos = wide[:, :-1] + wide[:, 1:]
        return twos[:, :-1] + twos[:, 1:]

    def next_term(d, n, first):
        ny = blocks_y[d]
        here = slab(n, 0)
        sum_here = x_sum(here)
        sum_first = sum_here
        twos = pltpu.roll(x_sum(slab(n, ny - 1)), 1, 2) + sum_here
        for yi in range(ny):
            if yi + 1 < ny:
                after = slab(n, yi + 1)
                sum_after = x_sum(after)
            else:
                after = None
                sum_after = pltpu.roll(sum_first, 7, 2)
            twos_after = sum_here + sum_after
            nine = twos + twos_after
            rows = pl.ds(yi * slab_rows, slab_rows)
            scale = quarter[d, pl.ds(yi * nx * 8, nx * 8), :].reshape(1, nx, 8, 128)
            if first:
                pair = (0.5 * scale) * nine
            else:
                pair = scale * nine - pair_sum[rows, :].reshape(2, nx, 8, 128)
            pair_sum[rows, :] = pair.reshape(slab_rows, 128)
            terms[n + 1, rows, :] = (pair - here).reshape(slab_rows, 128)
            twos, sum_here, here = twos_after, sum_after, after

    def all_terms(d):
        next_term(d, 0, True)

        def body(n, _):
            next_term(d, n, False)
            return 0

        lax.fori_loop(1, order, body, 0)

    frequency = me_f * freqs + lanes8 // lane_blocks
    omega = (2.0 * math.pi) * (
        LOWEST + (HIGHEST - LOWEST) * (frequency.astype(jnp.float32) + 0.5) / (freqs * fcount)
    )

    def phase_sum(d):
        ny = blocks_y[d]

        def chunk(yi0, count):
            rows = pl.ds(pl.multiple_of(yi0 * slab_rows, 8), count * slab_rows)

            def term(n):
                return terms[n, rows, :].reshape(count, 2, nx, 8, 128)

            slow = jnp.concatenate(
                [
                    slow_rows[d, xi, pl.ds(yi0 + j, 8, stride=ny), :][None]
                    for j in range(count)
                    for xi in range(nx)
                ],
                axis=0,
            )
            angle = (omega * slow).reshape(count, 1, nx, 8, 128)
            square = angle * angle
            cosine = 1.0 + square * (-0.5 + square * (1 / 24.0 + square * (-1 / 720.0)))
            sine = angle * (1.0 + square * (-1 / 6.0 + square * (1 / 120.0 + square * (-1 / 5040.0))))
            double = cosine + cosine
            later = weights[order] * term(order)
            now = weights[order - 1] * term(order - 1) + double * later
            for n in range(order - 2, 0, -1):
                now, later = weights[n] * term(n) + double * now - later, now
            now, later = term(0) + double * now - later, now
            straight = cosine * now - later
            real = straight[:, 0] - sine[:, 0] * now[:, 1]
            imag = straight[:, 1] + sine[:, 0] * now[:, 0]
            for j in range(count):
                for xi in range(nx):
                    rows_buf[0, xi, pl.ds(yi0 + j, 8, stride=ny), :] = real[j, xi]
                    rows_buf[1, xi, pl.ds(yi0 + j, 8, stride=ny), :] = imag[j, xi]

        size = 3

        def body(i, _):
            chunk(i * size, size)
            return 0

        lax.fori_loop(0, ny // size, body, 0)
        if ny % size:
            chunk(ny - ny % size, ny % size)

    def turn(part, xi, h):
        return rows_buf[part, xi, pl.ds(h, side), :].T

    def make_image(d):
        def some(i, _):
            for j in range(3):
                xi = i * 3 + j
                turned = turn(0, xi, around_y[d])
                for o in range(octets):
                    total = turned[8 * o : 8 * o + 8]
                    for f in range(1, freqs):
                        total = total + turned[f * lane_blocks + 8 * o : f * lane_blocks + 8 * o + 8]
                    part_image[d, pl.ds(xi + 8 * nx * o, 8, stride=nx), :] = total
                if d + 1 < depths:
                    ny = blocks_y[d + 1]
                    for yi in range(ny):
                        for part in range(2):
                            rows = pl.ds(pl.multiple_of(((yi * 2 + part) * nx + xi) * 8, 8), 8)
                            terms[0, rows, :] = rows_buf[part, xi, pl.ds(order + yi, 8, stride=ny), :]
            return 0

        lax.fori_loop(0, nx // 3, some, 0)

    def make_natural():
        h = around_y[depths - 1]

        def some(i, _):
            for j in range(3):
                xi = i * 3 + j
                for part in range(2):
                    turned = turn(part, xi, h)
                    for f in range(freqs):
                        for o in range(octets):
                            at = f * lane_blocks + 8 * o
                            natural[part * freqs + f, pl.ds(xi + 8 * nx * o, 8, stride=nx), :] = turned[at : at + 8]
            return 0

        lax.fori_loop(0, nx // 3, some, 0)
        for f in range(freqs):
            for part in range(2):
                out_ref[f, part] = natural[part * freqs + f, pl.ds(reach, side), :] * shared_weight(order) ** depths

    image_stages = [(0, depths - 1), (depths - 1, 1)]
    image_rows = pl.ds(pl.multiple_of(me_f * strip, 8), strip)

    def reduce_copies(stage):
        first, count = image_stages[stage]
        of = pl.ds(first, count)
        return to_peers(
            [
                (
                    part_image.at[of, pl.ds(pl.multiple_of(reach + peer * strip, 8), strip)],
                    image_in.at[k, of],
                )
                for k, peer in enumerate(peers)
            ],
            red_send.at[stage], red_recv.at[stage],
        )

    def cast_image(stage):
        first, count = image_stages[stage]
        of = pl.ds(first, count)
        total = part_image[of, own_rows, :]
        for k in range(fcount - 1):
            total = total + image_in[k, of]
        for d in range(first, first + count):
            scale = shared_weight(order) ** (d + 1) / math.sqrt(freqs * fcount)
            image_out[d, image_rows, :] = total[d - first] * scale
        block = image_out.at[of, image_rows]
        return start(to_peers([(block, block)] * (fcount - 1), cast_send.at[stage], cast_recv.at[stage]))

    wait(slow_first)
    build_slow_edges(0)
    halo_first = start(slow_halo_copies(0))
    slow_rest = start(slow_peer_copies(1))
    fill_all_quarters()
    wait(halo_first)
    unpack_first_halo()
    place_slow_tile(0)
    place_slow_halo(0)
    wait(wave_copies)
    assemble_wave()
    wait(slow_rest)
    build_slow_edges(1)
    halo_rest = start(slow_halo_copies(1))
    casts = []
    for d in range(depths):
        all_terms(d)
        if d == 1:
            wait(halo_rest)
            for e in range(1, depths):
                place_slow_tile(e)
            place_slow_halo(1)
        phase_sum(d)
        make_image(d)
        if d == depths - 2:
            reduced = start(reduce_copies(0))
    last = start(reduce_copies(1))
    wait(reduced)
    casts += cast_image(0)
    make_natural()
    wait(last)
    casts += cast_image(1)
    wait(casts)
    image_ref[...] = image_out[...]


def per_device(wavefield, velocity):
    freqs, _, side, _ = wavefield.shape
    depths = velocity.shape[0]
    fcount, xcount, ycount = lax.axis_size("freq"), lax.axis_size("gx"), lax.axis_size("gy")
    reach = ORDER * depths
    extent = side + 2 * reach
    nx, ny = extent * freqs // 128, extent // SUB_BLOCKS
    cells = nx * ny * 8
    batch = 2 * freqs
    groups = batch * reach // 128
    strip = side // fcount
    dims = (depths, freqs, side, fcount, xcount, ycount)
    f32 = jnp.float32
    dma = pltpu.SemaphoreType.DMA
    image, extrapolated = pl.pallas_call(
        functools.partial(kernel, dims),
        out_shape=(
            pltpu.VMEM((depths, side, side), f32),
            pltpu.VMEM(wavefield.shape, f32),
        ),
        in_specs=[pl.BlockSpec(memory_space=pltpu.HBM)] * 2,
        out_specs=(pl.BlockSpec(memory_space=pltpu.VMEM),) * 2,
        scratch_shapes=[
            pltpu.VMEM((ORDER + 1, 2 * cells, 128), f32),
            pltpu.VMEM((2 * cells, 128), f32),
            pltpu.VMEM((depths, cells, 128), f32),
            pltpu.VMEM((2, nx, extent, 128), f32),
            pltpu.VMEM((depths, nx, extent, 128), f32),
            pltpu.VMEM((batch, extent, 128), f32),
            pltpu.VMEM((groups, side, 128), f32),
            pltpu.VMEM((groups, side, 128), f32),
            pltpu.VMEM((groups, extent, 128), f32),
            pltpu.VMEM((groups, extent, 128), f32),
            pltpu.VMEM((batch, extent, 128), f32),
            pltpu.VMEM((depths, strip, 128), f32),
            pltpu.VMEM((depths, extent, 128), f32),
            pltpu.VMEM((side, 128), f32),
            pltpu.VMEM((side, 128), f32),
            pltpu.VMEM((extent, 128), f32),
            pltpu.VMEM((extent, 128), f32),
            pltpu.VMEM((reach, 128), f32),
            pltpu.VMEM((reach, 128), f32),
            pltpu.VMEM((3, reach, 128), f32),
            pltpu.VMEM((3, reach, 128), f32),
            pltpu.VMEM((extent, 128), f32),
            pltpu.VMEM((extent, 128), f32),
            pltpu.VMEM((depths, extent, 128), f32),
            pltpu.VMEM((fcount - 1, depths, strip, 128), f32),
            pltpu.VMEM((depths, side, 128), f32),
            dma((batch + 1,)),
            dma((8,)),
            dma((8,)),
            dma((2, fcount - 1)),
            dma((2, fcount - 1)),
            dma((2, 8)),
            dma((2, 8)),
            dma((depths - 1, 2)),
            dma((depths - 1, 2)),
            dma((2, fcount - 1)),
            dma((2, fcount - 1)),
            dma((2, fcount - 1)),
            dma((2, fcount - 1)),
        ],
        compiler_params=pltpu.CompilerParams(
            collective_id=0, has_side_effects=True, vmem_limit_bytes=66_000_000
        ),
    )(wavefield, velocity)
    return (image, extrapolated)


def solution(mesh):
    placed = (P("freq", None, "gx", "gy"), P(None, ("gx", "freq"), "gy"))
    return jax.shard_map(
        per_device,
        mesh=mesh,
        in_specs=placed,
        out_specs=(P(None, "gx", "gy"), P("freq", None, "gx", "gy")),
        check_vma=False,
    )
```

```python
import functools
import math

import jax
import jax.numpy as jnp
from jax import lax
from jax.experimental import pallas as pl
from jax.experimental.pallas import tpu as pltpu
from jax.sharding import PartitionSpec as P

ORDER = 8
LOWEST = 2.0
HIGHEST = 60.0
INTERVAL = 0.01
MESH = pl.DeviceIdType.MESH
SUB_BLOCKS = 8


def ratios(order):
    return [1.0 / (term + 1) for term in range(order + 1)]


def shared_weight(order):
    return 1.0 / sum(1.0 / (term + 1) for term in range(order + 1))


def rolled(cells, shift, axis):
    shift = shift % cells.shape[axis]
    return cells if shift == 0 else pltpu.roll(cells, shift, axis)


def kernel(
    dims,
    wave_hbm, vel_hbm, image_ref, out_ref,
    terms, pair_sum, quarter, rows_buf, slow_rows, tile, edge_r, edge_l, halo_l, halo_r, natural,
    vel_raw, slow_tile, slow_edge_r, slow_edge_l, slow_halo_l, slow_halo_r,
    first_edge_r, first_edge_l, first_halo_l, first_halo_r, wide_halo_l, wide_halo_r,
    part_image, image_in, image_out,
    load_sem, wave_send, wave_recv, vel_send, vel_recv, velh_send, velh_recv, rows_send, rows_recv,
    red_send, red_recv, cast_send, cast_recv,
):
    depths, freqs, side, fcount, xcount, ycount = dims
    order = ORDER
    weights = ratios(order)
    reach = order * depths
    extent = side + 2 * reach
    lane_blocks = 128 // freqs
    octets = lane_blocks // 8
    nx = extent // lane_blocks
    slab_rows = 2 * nx * 8
    batch = 2 * freqs
    inner = 128 // reach
    groups = batch // inner
    strip = side // fcount
    around_y = [reach - order * d for d in range(depths)]
    blocks_y = [(side + 2 * h) // SUB_BLOCKS for h in around_y]

    me_f = lax.axis_index("freq")
    me_x = lax.axis_index("gx")
    me_y = lax.axis_index("gy")

    def mod(value, count):
        return lax.rem(value + count, count)

    up, down = mod(me_x - 1, xcount), mod(me_x + 1, xcount)
    left, right = mod(me_y - 1, ycount), mod(me_y + 1, ycount)
    around = [
        {"gx": up, "gy": me_y}, {"gx": down, "gy": me_y}, {"gx": me_x, "gy": right}, {"gx": me_x, "gy": left},
        {"gx": up, "gy": right}, {"gx": down, "gy": right}, {"gx": up, "gy": left}, {"gx": down, "gy": left},
    ]
    peers = [mod(me_f + k, fcount) for k in range(1, fcount)]

    barrier = pltpu.get_barrier_semaphore()
    for device in around:
        pl.semaphore_signal(barrier, inc=1, device_id=device, device_id_type=MESH)
    for peer in peers:
        pl.semaphore_signal(barrier, inc=1, device_id={"freq": peer}, device_id_type=MESH)

    vel_load = pltpu.make_async_copy(vel_hbm, vel_raw, load_sem.at[batch])
    vel_load.start()
    loads = []
    for f in range(freqs):
        for part in range(2):
            loads.append(
                pltpu.make_async_copy(
                    wave_hbm.at[f, part], tile.at[part * freqs + f, pl.ds(reach, side)], load_sem.at[f * 2 + part]
                )
            )
    for copy in loads:
        copy.start()

    own_rows = pl.ds(pl.multiple_of(reach + me_f * strip, 8), strip)
    vel_load.wait()
    slow_tile[:, own_rows, :] = (INTERVAL / (order + 1)) / vel_raw[...]
    for copy in loads:
        copy.wait()

    lane = lax.broadcasted_iota(jnp.int32, (1, 128), 1)

    def build_edges(i, _):
        rows = pl.ds(pl.multiple_of(i * 32, 32), 32)
        source_rows = pl.ds(pl.multiple_of(reach + i * 32, 8), 32)
        for target, first in ((edge_r, side - reach), (edge_l, 0)):
            for g in range(groups):
                made = None
                for k in range(inner):
                    moved = rolled(tile[k * groups + g, source_rows, :], k * reach - first, 1)
                    made = moved if made is None else jnp.where(lane >= k * reach, moved, made)
                target[g, rows, :] = made
        return 0

    lax.fori_loop(0, side // 32, build_edges, 0)

    head, tail = pl.ds(0, reach), pl.ds(side - reach, reach)
    low, mid, high = pl.ds(0, reach), pl.ds(reach, side), pl.ds(reach + side, reach)
    own_head, own_tail = pl.ds(reach, reach), pl.ds(side, reach)

    def to_neighbours(pairs, send_sem, recv_sem):
        return [
            pltpu.make_async_remote_copy(
                src_ref=source, dst_ref=target, send_sem=send_sem.at[k], recv_sem=recv_sem.at[k],
                device_id=around[k], device_id_type=MESH,
            )
            for k, (source, target) in [(k, pair) for k, pair in enumerate(pairs) if pair is not None]
        ]

    def to_peers(pairs, send_sem, recv_sem):
        return [
            pltpu.make_async_remote_copy(
                src_ref=source, dst_ref=target, send_sem=send_sem.at[k], recv_sem=recv_sem.at[k],
                device_id={"freq": peers[k]}, device_id_type=MESH,
            )
            for k, (source, target) in enumerate(pairs)
        ]

    def start(copies):
        for copy in copies:
            copy.start()
        return copies

    def wait(copies):
        for copy in copies:
            copy.wait()

    wave_copies = to_neighbours(
        [
            (tile.at[:, own_head], tile.at[:, high]),
            (tile.at[:, own_tail], tile.at[:, low]),
            (edge_r, halo_l.at[:, mid]),
            (edge_l, halo_r.at[:, mid]),
            (edge_r.at[:, head], halo_l.at[:, high]),
            (edge_r.at[:, tail], halo_l.at[:, low]),
            (edge_l.at[:, head], halo_r.at[:, high]),
            (edge_l.at[:, tail], halo_r.at[:, low]),
        ],
        wave_send, wave_recv,
    )
    stages = [(0, 1), (1, depths - 1)]
    ahead = [reach - order * (d + 1) for d in range(depths)]

    def slow_peer_copies(stage):
        first, count = stages[stage]
        block = slow_tile.at[pl.ds(first, count), own_rows]
        return to_peers([(block, block)] * (fcount - 1), vel_send.at[stage], vel_recv.at[stage])

    def slow_halo_copies(stage):
        copies = []
        for k, d in enumerate([0] if stage == 0 else range(1, depths - 1)):
            w = ahead[d]
            rows = [
                (slow_tile.at[d, pl.ds(reach, w)], slow_tile.at[d, pl.ds(reach + side, w)]),
                (slow_tile.at[d, pl.ds(reach + side - w, w)], slow_tile.at[d, pl.ds(reach - w, w)]),
            ]
            copies += to_neighbours(rows, rows_send.at[stage + k], rows_recv.at[stage + k])
        if stage == 0:
            sides = [(first_edge_r, first_halo_l.at[1]), (first_edge_l, first_halo_r.at[1])]
            for edge, halo in ((first_edge_r, first_halo_l), (first_edge_l, first_halo_r)):
                sides += [(edge, halo.at[2]), (edge, halo.at[0])]
        else:
            w = ahead[1]
            sides = [(slow_edge_r, slow_halo_l.at[mid]), (slow_edge_l, slow_halo_r.at[mid])]
            for edge, halo in ((slow_edge_r, slow_halo_l), (slow_edge_l, slow_halo_r)):
                sides += [
                    (edge.at[pl.ds(0, w)], halo.at[pl.ds(reach + side, w)]),
                    (edge.at[pl.ds(side - w, w)], halo.at[pl.ds(reach - w, w)]),
                ]
        return copies + to_neighbours([None, None] + sides, velh_send.at[stage], velh_recv.at[stage])

    def build_slow_edges(stage):
        if stage == 0:
            for target, source in ((first_edge_r, side - reach), (first_edge_l, 0)):
                made = None
                for j in range(side // reach):
                    moved = rolled(slow_tile[0, pl.ds(reach + reach * j, reach), :], reach * j - source, 1)
                    made = moved if made is None else jnp.where(lane >= reach * j, moved, made)
                target[...] = made
            return
        first, count = stages[stage]
        for target, source in ((slow_edge_r, side - reach), (slow_edge_l, 0)):
            made = None
            for j in range(count):
                moved = rolled(slow_tile[first + j, pl.ds(reach, side), :], reach * j - source, 1)
                made = moved if made is None else jnp.where(lane >= reach * j, moved, made)
            target[...] = made

    def unpack_first_halo():
        for halo, target in ((first_halo_l, wide_halo_l), (first_halo_r, wide_halo_r)):
            target[pl.ds(0, reach), :] = rolled(halo[0], -(side - reach), 1)
            for j in range(side // reach):
                target[pl.ds(reach + reach * j, reach), :] = rolled(halo[1], -reach * j, 1)
            target[pl.ds(reach + side, reach), :] = halo[2]

    for d in range(depths):
        rest = reach - (ahead[d] if d < depths - 1 else 0)
        slow_tile[d, pl.ds(0, rest), :] = jnp.zeros((rest, side), jnp.float32)
        slow_tile[d, pl.ds(extent - rest, rest), :] = jnp.zeros((rest, side), jnp.float32)
    rest = reach - ahead[1]
    for halo in (slow_halo_l, slow_halo_r):
        halo[pl.ds(0, rest), :] = jnp.zeros((rest, side), jnp.float32)
        halo[pl.ds(extent - rest, rest), :] = jnp.zeros((rest, side), jnp.float32)

    pl.semaphore_wait(barrier, len(around) + len(peers))
    slow_first = start(slow_peer_copies(0))
    start(wave_copies)

    lanes8 = lax.broadcasted_iota(jnp.int32, (8, 128), 1)
    subs8 = lax.broadcasted_iota(jnp.int32, (8, 128), 0)

    def inside_x(xi, lanes):
        x = me_x * side - reach + lax.rem(lanes, lane_blocks) * nx + xi
        return (x >= 0) & (x < xcount * side)

    def fill_quarters(d):
        def fill_quarter(yi, _):
            y = me_y * side - around_y[d] + subs8 * blocks_y[d] + yi
            inside_y = jnp.where((y >= 0) & (y < ycount * side), 0.25, 0.0)
            for xi in range(nx):
                rows = pl.ds(pl.multiple_of((yi * nx + xi) * 8, 8), 8)
                quarter[d, rows, :] = jnp.where(inside_x(xi, lanes8), inside_y, 0.0)
            return 0

        lax.fori_loop(0, blocks_y[d], fill_quarter, 0)

    def fill_all_quarters():
        for d in range(depths):
            fill_quarters(d)

    def blocks_of(load):
        return jnp.concatenate([load(8 * nx * o) for o in range(octets)], axis=0)

    def place_slow_tile(d):
        for xi in range(nx):
            cells = blocks_of(lambda begin: slow_tile[d, pl.ds(xi + begin, 8, stride=nx), :])
            slow_rows[d, xi, pl.ds(around_y[d], side), :] = jnp.concatenate([cells] * freqs, axis=0).T

    def place_slow_halo(stage):
        first, count = stages[stage]
        if stage == 0:
            edges_l, edges_r = wide_halo_l, wide_halo_r
        else:
            edges_l, edges_r = slow_halo_l, slow_halo_r
        for pair in range(0, count, 2):
            for xi in range(nx):
                from_l = blocks_of(lambda begin: edges_l[pl.ds(xi + begin, 8, stride=nx), :])
                from_r = blocks_of(lambda begin: edges_r[pl.ds(xi + begin, 8, stride=nx), :])
                made = jnp.where(lane < reach, rolled(from_l, -reach * pair, 1), rolled(from_r, reach - reach * pair, 1))
                if pair + 1 < count:
                    made = jnp.where(lane < 2 * reach, made, rolled(from_l, reach * (1 - pair), 1))
                    made = jnp.where(lane < 3 * reach, made, rolled(from_r, reach * (2 - pair), 1))
                turned = jnp.concatenate([made] * freqs, axis=0).T
                for j in range(min(2, count - pair)):
                    d = first + pair + j
                    h = around_y[d]
                    base = 2 * reach * j
                    slow_rows[d, xi, pl.ds(0, h), :] = turned[base + reach - h : base + reach]
                    slow_rows[d, xi, pl.ds(h + side, h), :] = turned[base + reach : base + reach + h]

    def assemble_wave():
        ny = blocks_y[0]
        inside_l = jnp.where(me_y > 0, 1.0, 0.0)
        inside_r = jnp.where(me_y < ycount - 1, 1.0, 0.0)

        def put(part, xi, y0, block):
            yb, yi = y0 // ny, y0 % ny
            begin = ((yi * 2 + part) * nx + xi) * 8 + yb
            terms[0, pl.ds(begin, 8, stride=slab_rows), :] = block

        def middle(i, _):
            for j in range(3):
                xi = i * 3 + j
                grid_x = jnp.where(inside_x(xi, lane), 1.0, 0.0)
                for part in range(2):
                    cells = jnp.concatenate(
                        [
                            blocks_of(lambda begin: tile[part * freqs + f, pl.ds(xi + begin, 8, stride=nx), :])
                            for f in range(freqs)
                        ],
                        axis=0,
                    )
                    turned = cells.T * grid_x
                    for o in range(side // 8):
                        put(part, xi, reach + 8 * o, turned[8 * o : 8 * o + 8])
            return 0

        def beside(i, _):
            for j in range(3):
                xi = i * 3 + j
                grid_x = jnp.where(inside_x(xi, lane), 1.0, 0.0)
                cells = []
                for f in range(freqs):
                    both = []
                    for part in range(2):
                        k, g = (part * freqs + f) // groups, (part * freqs + f) % groups
                        from_l = blocks_of(lambda begin: halo_l[g, pl.ds(xi + begin, 8, stride=nx), :])
                        from_r = blocks_of(lambda begin: halo_r[g, pl.ds(xi + begin, 8, stride=nx), :])
                        at = 2 * reach * part
                        both.append(
                            jnp.where(
                                lane < at + reach, rolled(from_l, at - k * reach, 1), rolled(from_r, at + reach - k * reach, 1)
                            )
                        )
                    cells.append(jnp.where(lane < 2 * reach, both[0], both[1]))
                turned = jnp.concatenate(cells, axis=0).T
                for part in range(2):
                    at = 2 * reach * part
                    beside_l = turned[at : at + reach] * (grid_x * inside_l)
                    beside_r = turned[at + reach : at + 2 * reach] * (grid_x * inside_r)
                    for o in range(reach // 8):
                        put(part, xi, 8 * o, beside_l[8 * o : 8 * o + 8])
                        put(part, xi, reach + side + 8 * o, beside_r[8 * o : 8 * o + 8])
            return 0

        wait(wave_copies[:2])
        lax.fori_loop(0, nx // 3, middle, 0)
        wait(wave_copies[2:])
        lax.fori_loop(0, nx // 3, beside, 0)

    def slab(n, yi):
        return terms[n, pl.ds(yi * slab_rows, slab_rows), :].reshape(2, nx, 8, 128)

    def x_sum(cells):
        before = pltpu.roll(cells[:, nx - 1 : nx], 1, 3)
        after = pltpu.roll(cells[:, 0:1], 127, 3)
        wide = jnp.concatenate([before, cells, after], axis=1)
        twos = wide[:, :-1] + wide[:, 1:]
        return twos[:, :-1] + twos[:, 1:]

    def next_term(d, n, first):
        ny = blocks_y[d]
        here = slab(n, 0)
        sum_here = x_sum(here)
        sum_first = sum_here
        twos = pltpu.roll(x_sum(slab(n, ny - 1)), 1, 2) + sum_here
        for yi in range(ny):
            if yi + 1 < ny:
                after = slab(n, yi + 1)
                sum_after = x_sum(after)
            else:
                after = None
                sum_after = pltpu.roll(sum_first, 7, 2)
            twos_after = sum_here + sum_after
            nine = twos + twos_after
            rows = pl.ds(yi * slab_rows, slab_rows)
            scale = quarter[d, pl.ds(yi * nx * 8, nx * 8), :].reshape(1, nx, 8, 128)
            if first:
                pair = (0.5 * scale) * nine
            else:
                pair = scale * nine - pair_sum[rows, :].reshape(2, nx, 8, 128)
            pair_sum[rows, :] = pair.reshape(slab_rows, 128)
            terms[n + 1, rows, :] = (pair - here).reshape(slab_rows, 128)
            twos, sum_here, here = twos_after, sum_after, after

    def all_terms(d):
        next_term(d, 0, True)

        def body(n, _):
            next_term(d, n, False)
            return 0

        lax.fori_loop(1, order, body, 0)

    frequency = me_f * freqs + lanes8 // lane_blocks
    omega = (2.0 * math.pi) * (
        LOWEST + (HIGHEST - LOWEST) * (frequency.astype(jnp.float32) + 0.5) / (freqs * fcount)
    )

    def phase_sum(d):
        ny = blocks_y[d]

        def chunk(yi0, count):
            rows = pl.ds(pl.multiple_of(yi0 * slab_rows, 8), count * slab_rows)

            def term(n):
                return terms[n, rows, :].reshape(count, 2, nx, 8, 128)

            slow = jnp.concatenate(
                [
                    slow_rows[d, xi, pl.ds(yi0 + j, 8, stride=ny), :][None]
                    for j in range(count)
                    for xi in range(nx)
                ],
                axis=0,
            )
            angle = (omega * slow).reshape(count, 1, nx, 8, 128)
            square = angle * angle
            cosine = 1.0 + square * (-0.5 + square * (1 / 24.0 + square * (-1 / 720.0)))
            sine = angle * (1.0 + square * (-1 / 6.0 + square * (1 / 120.0 + square * (-1 / 5040.0))))
            double = cosine + cosine
            later = weights[order] * term(order)
            now = weights[order - 1] * term(order - 1) + double * later
            for n in range(order - 2, 0, -1):
                now, later = weights[n] * term(n) + double * now - later, now
            now, later = term(0) + double * now - later, now
            straight = cosine * now - later
            real = straight[:, 0] - sine[:, 0] * now[:, 1]
            imag = straight[:, 1] + sine[:, 0] * now[:, 0]
            for j in range(count):
                for xi in range(nx):
                    rows_buf[0, xi, pl.ds(yi0 + j, 8, stride=ny), :] = real[j, xi]
                    rows_buf[1, xi, pl.ds(yi0 + j, 8, stride=ny), :] = imag[j, xi]

        size = 3

        def body(i, _):
            chunk(i * size, size)
            return 0

        lax.fori_loop(0, ny // size, body, 0)
        if ny % size:
            chunk(ny - ny % size, ny % size)

    def turn(part, xi, h):
        return rows_buf[part, xi, pl.ds(h, side), :].T

    def make_image(d):
        def some(i, _):
            for j in range(3):
                xi = i * 3 + j
                turned = turn(0, xi, around_y[d])
                for o in range(octets):
                    total = turned[8 * o : 8 * o + 8]
                    for f in range(1, freqs):
                        total = total + turned[f * lane_blocks + 8 * o : f * lane_blocks + 8 * o + 8]
                    part_image[d, pl.ds(xi + 8 * nx * o, 8, stride=nx), :] = total
                if d + 1 < depths:
                    ny = blocks_y[d + 1]
                    for yi in range(ny):
                        for part in range(2):
                            rows = pl.ds(pl.multiple_of(((yi * 2 + part) * nx + xi) * 8, 8), 8)
                            terms[0, rows, :] = rows_buf[part, xi, pl.ds(order + yi, 8, stride=ny), :]
            return 0

        lax.fori_loop(0, nx // 3, some, 0)

    def make_natural():
        h = around_y[depths - 1]

        def some(i, _):
            for j in range(3):
                xi = i * 3 + j
                for part in range(2):
                    turned = turn(part, xi, h)
                    for f in range(freqs):
                        for o in range(octets):
                            at = f * lane_blocks + 8 * o
                            natural[part * freqs + f, pl.ds(xi + 8 * nx * o, 8, stride=nx), :] = turned[at : at + 8]
            return 0

        lax.fori_loop(0, nx // 3, some, 0)
        for f in range(freqs):
            for part in range(2):
                out_ref[f, part] = natural[part * freqs + f, pl.ds(reach, side), :] * shared_weight(order) ** depths

    image_stages = [(0, depths - 1), (depths - 1, 1)]
    image_rows = pl.ds(pl.multiple_of(me_f * strip, 8), strip)

    def reduce_copies(stage):
        first, count = image_stages[stage]
        of = pl.ds(first, count)
        return to_peers(
            [
                (
                    part_image.at[of, pl.ds(pl.multiple_of(reach + peer * strip, 8), strip)],
                    image_in.at[k, of],
                )
                for k, peer in enumerate(peers)
            ],
            red_send.at[stage], red_recv.at[stage],
        )

    def cast_image(stage):
        first, count = image_stages[stage]
        of = pl.ds(first, count)
        total = part_image[of, own_rows, :]
        for k in range(fcount - 1):
            total = total + image_in[k, of]
        for d in range(first, first + count):
            scale = shared_weight(order) ** (d + 1) / math.sqrt(freqs * fcount)
            image_out[d, image_rows, :] = total[d - first] * scale
        block = image_out.at[of, image_rows]
        return start(to_peers([(block, block)] * (fcount - 1), cast_send.at[stage], cast_recv.at[stage]))

    wait(slow_first)
    build_slow_edges(0)
    halo_first = start(slow_halo_copies(0))
    slow_rest = start(slow_peer_copies(1))
    fill_all_quarters()
    assemble_wave()
    casts = []
    for d in range(depths):
        all_terms(d)
        if d == 0:
            wait(halo_first)
            unpack_first_halo()
            place_slow_tile(0)
            place_slow_halo(0)
            wait(slow_rest)
            build_slow_edges(1)
            halo_rest = start(slow_halo_copies(1))
        if d == 1:
            wait(halo_rest)
            for e in range(1, depths):
                place_slow_tile(e)
            place_slow_halo(1)
        phase_sum(d)
        make_image(d)
        if d == depths - 2:
            reduced = start(reduce_copies(0))
    last = start(reduce_copies(1))
    wait(reduced)
    casts += cast_image(0)
    make_natural()
    wait(last)
    casts += cast_image(1)
    wait(casts)
    image_ref[...] = image_out[...]


def per_device(wavefield, velocity):
    freqs, _, side, _ = wavefield.shape
    depths = velocity.shape[0]
    fcount, xcount, ycount = lax.axis_size("freq"), lax.axis_size("gx"), lax.axis_size("gy")
    reach = ORDER * depths
    extent = side + 2 * reach
    nx, ny = extent * freqs // 128, extent // SUB_BLOCKS
    cells = nx * ny * 8
    batch = 2 * freqs
    groups = batch * reach // 128
    strip = side // fcount
    dims = (depths, freqs, side, fcount, xcount, ycount)
    f32 = jnp.float32
    dma = pltpu.SemaphoreType.DMA
    image, extrapolated = pl.pallas_call(
        functools.partial(kernel, dims),
        out_shape=(
            pltpu.VMEM((depths, side, side), f32),
            pltpu.VMEM(wavefield.shape, f32),
        ),
        in_specs=[pl.BlockSpec(memory_space=pltpu.HBM)] * 2,
        out_specs=(pl.BlockSpec(memory_space=pltpu.VMEM),) * 2,
        scratch_shapes=[
            pltpu.VMEM((ORDER + 1, 2 * cells, 128), f32),
            pltpu.VMEM((2 * cells, 128), f32),
            pltpu.VMEM((depths, cells, 128), f32),
            pltpu.VMEM((2, nx, extent, 128), f32),
            pltpu.VMEM((depths, nx, extent, 128), f32),
            pltpu.VMEM((batch, extent, 128), f32),
            pltpu.VMEM((groups, side, 128), f32),
            pltpu.VMEM((groups, side, 128), f32),
            pltpu.VMEM((groups, extent, 128), f32),
            pltpu.VMEM((groups, extent, 128), f32),
            pltpu.VMEM((batch, extent, 128), f32),
            pltpu.VMEM((depths, strip, 128), f32),
            pltpu.VMEM((depths, extent, 128), f32),
            pltpu.VMEM((side, 128), f32),
            pltpu.VMEM((side, 128), f32),
            pltpu.VMEM((extent, 128), f32),
            pltpu.VMEM((extent, 128), f32),
            pltpu.VMEM((reach, 128), f32),
            pltpu.VMEM((reach, 128), f32),
            pltpu.VMEM((3, reach, 128), f32),
            pltpu.VMEM((3, reach, 128), f32),
            pltpu.VMEM((extent, 128), f32),
            pltpu.VMEM((extent, 128), f32),
            pltpu.VMEM((depths, extent, 128), f32),
            pltpu.VMEM((fcount - 1, depths, strip, 128), f32),
            pltpu.VMEM((depths, side, 128), f32),
            dma((batch + 1,)),
            dma((8,)),
            dma((8,)),
            dma((2, fcount - 1)),
            dma((2, fcount - 1)),
            dma((2, 8)),
            dma((2, 8)),
            dma((depths - 1, 2)),
            dma((depths - 1, 2)),
            dma((2, fcount - 1)),
            dma((2, fcount - 1)),
            dma((2, fcount - 1)),
            dma((2, fcount - 1)),
        ],
        compiler_params=pltpu.CompilerParams(
            collective_id=0, has_side_effects=True, vmem_limit_bytes=66_000_000
        ),
    )(wavefield, velocity)
    return (image, extrapolated)


def solution(mesh):
    placed = (P("freq", None, "gx", "gy"), P(None, ("gx", "freq"), "gy"))
    return jax.shard_map(
        per_device,
        mesh=mesh,
        in_specs=placed,
        out_specs=(P(None, "gx", "gy"), P("freq", None, "gx", "gy")),
        check_vma=False,
    )
```

```python
import functools
import math

import jax
import jax.numpy as jnp
from jax import lax
from jax.experimental import pallas as pl
from jax.experimental.pallas import tpu as pltpu
from jax.sharding import PartitionSpec as P

ORDER = 8
LOWEST = 2.0
HIGHEST = 60.0
INTERVAL = 0.01
MESH = pl.DeviceIdType.MESH
SUB_BLOCKS = 8


def ratios(order):
    return [1.0 / (term + 1) for term in range(order + 1)]


def shared_weight(order):
    return 1.0 / sum(1.0 / (term + 1) for term in range(order + 1))


def rolled(cells, shift, axis):
    shift = shift % cells.shape[axis]
    return cells if shift == 0 else pltpu.roll(cells, shift, axis)


def kernel(
    dims,
    wave_hbm, vel_hbm, image_ref, out_ref,
    terms, pair_sum, quarter, rows_buf, slow_rows, tile, edge_r, edge_l, halo_l, halo_r, natural,
    vel_raw, slow_tile, slow_edge_r, slow_edge_l, slow_halo_l, slow_halo_r,
    first_edge_r, first_edge_l, first_halo_l, first_halo_r, wide_halo_l, wide_halo_r,
    part_image, image_in, image_out,
    load_sem, wave_send, wave_recv, vel_send, vel_recv, velh_send, velh_recv, rows_send, rows_recv,
    red_send, red_recv, cast_send, cast_recv,
):
    depths, freqs, side, fcount, xcount, ycount = dims
    order = ORDER
    weights = ratios(order)
    reach = order * depths
    extent = side + 2 * reach
    lane_blocks = 128 // freqs
    octets = lane_blocks // 8
    nx = extent // lane_blocks
    slab_rows = 2 * nx * 8
    batch = 2 * freqs
    inner = 128 // reach
    groups = batch // inner
    strip = side // fcount
    around_y = [reach - order * d for d in range(depths)]
    blocks_y = [(side + 2 * h) // SUB_BLOCKS for h in around_y]

    me_f = lax.axis_index("freq")
    me_x = lax.axis_index("gx")
    me_y = lax.axis_index("gy")

    def mod(value, count):
        return lax.rem(value + count, count)

    up, down = mod(me_x - 1, xcount), mod(me_x + 1, xcount)
    left, right = mod(me_y - 1, ycount), mod(me_y + 1, ycount)
    around = [
        {"gx": up, "gy": me_y}, {"gx": down, "gy": me_y}, {"gx": me_x, "gy": right}, {"gx": me_x, "gy": left},
        {"gx": up, "gy": right}, {"gx": down, "gy": right}, {"gx": up, "gy": left}, {"gx": down, "gy": left},
    ]
    peers = [mod(me_f + k, fcount) for k in range(1, fcount)]

    barrier = pltpu.get_barrier_semaphore()
    for device in around:
        pl.semaphore_signal(barrier, inc=1, device_id=device, device_id_type=MESH)
    for peer in peers:
        pl.semaphore_signal(barrier, inc=1, device_id={"freq": peer}, device_id_type=MESH)

    vel_load = pltpu.make_async_copy(vel_hbm, vel_raw, load_sem.at[batch])
    vel_load.start()
    loads = []
    for f in range(freqs):
        for part in range(2):
            loads.append(
                pltpu.make_async_copy(
                    wave_hbm.at[f, part], tile.at[part * freqs + f, pl.ds(reach, side)], load_sem.at[f * 2 + part]
                )
            )
    for copy in loads:
        copy.start()

    own_rows = pl.ds(pl.multiple_of(reach + me_f * strip, 8), strip)
    vel_load.wait()
    slow_tile[:, own_rows, :] = (INTERVAL / (order + 1)) / vel_raw[...]
    for copy in loads:
        copy.wait()

    lane = lax.broadcasted_iota(jnp.int32, (1, 128), 1)

    def build_edges(i, _):
        rows = pl.ds(pl.multiple_of(i * 32, 32), 32)
        source_rows = pl.ds(pl.multiple_of(reach + i * 32, 8), 32)
        for target, first in ((edge_r, side - reach), (edge_l, 0)):
            for g in range(groups):
                made = None
                for k in range(inner):
                    moved = rolled(tile[k * groups + g, source_rows, :], k * reach - first, 1)
                    made = moved if made is None else jnp.where(lane >= k * reach, moved, made)
                target[g, rows, :] = made
        return 0

    lax.fori_loop(0, side // 32, build_edges, 0)

    head, tail = pl.ds(0, reach), pl.ds(side - reach, reach)
    low, mid, high = pl.ds(0, reach), pl.ds(reach, side), pl.ds(reach + side, reach)
    own_head, own_tail = pl.ds(reach, reach), pl.ds(side, reach)

    def to_neighbours(pairs, send_sem, recv_sem):
        return [
            (k, pltpu.make_async_remote_copy(
                src_ref=source, dst_ref=target, send_sem=send_sem.at[k], recv_sem=recv_sem.at[k],
                device_id=around[k], device_id_type=MESH,
            ))
            for k, (source, target) in [(k, pair) for k, pair in enumerate(pairs) if pair is not None]
        ]

    def to_peers(pairs, send_sem, recv_sem):
        return [
            pltpu.make_async_remote_copy(
                src_ref=source, dst_ref=target, send_sem=send_sem.at[k], recv_sem=recv_sem.at[k],
                device_id={"freq": peers[k]}, device_id_type=MESH,
            )
            for k, (source, target) in enumerate(pairs)
        ]

    def start(copies):
        for copy in copies:
            copy.start()
        return copies

    def wait(copies):
        for copy in copies:
            copy.wait()

    has_left, has_right = me_y > 0, me_y < ycount - 1
    rightwards, leftwards = (2, 4, 5), (3, 6, 7)

    def start_near(copies):
        for k, copy in copies:
            if k < 2:
                copy.start()

        @pl.when(has_right)
        def _():
            for k, copy in copies:
                if k in rightwards:
                    copy.start()

        @pl.when(has_left)
        def _():
            for k, copy in copies:
                if k in leftwards:
                    copy.start()

        return copies

    def wait_near(copies):
        for k, copy in copies:
            if k < 2:
                copy.wait()
        if all(k < 2 for k, _ in copies):
            return

        @pl.when(has_right)
        def _():
            for k, copy in copies:
                if k in rightwards:
                    copy.wait_send()
                if k in leftwards:
                    copy.wait_recv()

        @pl.when(has_left)
        def _():
            for k, copy in copies:
                if k in leftwards:
                    copy.wait_send()
                if k in rightwards:
                    copy.wait_recv()

    def clear(refs):
        for ref in refs:
            ref[...] = jnp.zeros(ref.shape, jnp.float32)

    @pl.when(me_y == 0)
    def _():
        clear((halo_l, first_halo_l, slow_halo_l))

    @pl.when(me_y == ycount - 1)
    def _():
        clear((halo_r, first_halo_r, slow_halo_r))

    wave_copies = to_neighbours(
        [
            (tile.at[:, own_head], tile.at[:, high]),
            (tile.at[:, own_tail], tile.at[:, low]),
            (edge_r, halo_l.at[:, mid]),
            (edge_l, halo_r.at[:, mid]),
            (edge_r.at[:, head], halo_l.at[:, high]),
            (edge_r.at[:, tail], halo_l.at[:, low]),
            (edge_l.at[:, head], halo_r.at[:, high]),
            (edge_l.at[:, tail], halo_r.at[:, low]),
        ],
        wave_send, wave_recv,
    )
    stages = [(0, 1), (1, depths - 1)]
    ahead = [reach - order * (d + 1) for d in range(depths)]

    def slow_peer_copies(stage):
        first, count = stages[stage]
        block = slow_tile.at[pl.ds(first, count), own_rows]
        return to_peers([(block, block)] * (fcount - 1), vel_send.at[stage], vel_recv.at[stage])

    def slow_halo_copies(stage):
        copies = []
        for k, d in enumerate([0] if stage == 0 else range(1, depths - 1)):
            w = ahead[d]
            rows = [
                (slow_tile.at[d, pl.ds(reach, w)], slow_tile.at[d, pl.ds(reach + side, w)]),
                (slow_tile.at[d, pl.ds(reach + side - w, w)], slow_tile.at[d, pl.ds(reach - w, w)]),
            ]
            copies += to_neighbours(rows, rows_send.at[stage + k], rows_recv.at[stage + k])
        if stage == 0:
            sides = [(first_edge_r, first_halo_l.at[1]), (first_edge_l, first_halo_r.at[1])]
            for edge, halo in ((first_edge_r, first_halo_l), (first_edge_l, first_halo_r)):
                sides += [(edge, halo.at[2]), (edge, halo.at[0])]
        else:
            w = ahead[1]
            sides = [(slow_edge_r, slow_halo_l.at[mid]), (slow_edge_l, slow_halo_r.at[mid])]
            for edge, halo in ((slow_edge_r, slow_halo_l), (slow_edge_l, slow_halo_r)):
                sides += [
                    (edge.at[pl.ds(0, w)], halo.at[pl.ds(reach + side, w)]),
                    (edge.at[pl.ds(side - w, w)], halo.at[pl.ds(reach - w, w)]),
                ]
        return copies + to_neighbours([None, None] + sides, velh_send.at[stage], velh_recv.at[stage])

    def build_slow_edges(stage):
        if stage == 0:
            for target, source in ((first_edge_r, side - reach), (first_edge_l, 0)):
                made = None
                for j in range(side // reach):
                    moved = rolled(slow_tile[0, pl.ds(reach + reach * j, reach), :], reach * j - source, 1)
                    made = moved if made is None else jnp.where(lane >= reach * j, moved, made)
                target[...] = made
            return
        first, count = stages[stage]
        for target, source in ((slow_edge_r, side - reach), (slow_edge_l, 0)):
            made = None
            for j in range(count):
                moved = rolled(slow_tile[first + j, pl.ds(reach, side), :], reach * j - source, 1)
                made = moved if made is None else jnp.where(lane >= reach * j, moved, made)
            target[...] = made

    def unpack_first_halo():
        for halo, target in ((first_halo_l, wide_halo_l), (first_halo_r, wide_halo_r)):
            target[pl.ds(0, reach), :] = rolled(halo[0], -(side - reach), 1)
            for j in range(side // reach):
                target[pl.ds(reach + reach * j, reach), :] = rolled(halo[1], -reach * j, 1)
            target[pl.ds(reach + side, reach), :] = halo[2]

    for d in range(depths):
        rest = reach - (ahead[d] if d < depths - 1 else 0)
        slow_tile[d, pl.ds(0, rest), :] = jnp.zeros((rest, side), jnp.float32)
        slow_tile[d, pl.ds(extent - rest, rest), :] = jnp.zeros((rest, side), jnp.float32)
    rest = reach - ahead[1]
    for halo in (slow_halo_l, slow_halo_r):
        halo[pl.ds(0, rest), :] = jnp.zeros((rest, side), jnp.float32)
        halo[pl.ds(extent - rest, rest), :] = jnp.zeros((rest, side), jnp.float32)

    pl.semaphore_wait(barrier, len(around) + len(peers))
    slow_first = start(slow_peer_copies(0))
    start_near(wave_copies)

    lanes8 = lax.broadcasted_iota(jnp.int32, (8, 128), 1)
    subs8 = lax.broadcasted_iota(jnp.int32, (8, 128), 0)

    def inside_x(xi, lanes):
        x = me_x * side - reach + lax.rem(lanes, lane_blocks) * nx + xi
        return (x >= 0) & (x < xcount * side)

    def fill_quarters(d):
        def fill_quarter(yi, _):
            y = me_y * side - around_y[d] + subs8 * blocks_y[d] + yi
            inside_y = jnp.where((y >= 0) & (y < ycount * side), 0.25, 0.0)
            for xi in range(nx):
                rows = pl.ds(pl.multiple_of((yi * nx + xi) * 8, 8), 8)
                quarter[d, rows, :] = jnp.where(inside_x(xi, lanes8), inside_y, 0.0)
            return 0

        lax.fori_loop(0, blocks_y[d], fill_quarter, 0)

    def fill_all_quarters():
        for d in range(depths):
            fill_quarters(d)

    def blocks_of(load):
        return jnp.concatenate([load(8 * nx * o) for o in range(octets)], axis=0)

    def place_slow_tile(d):
        for xi in range(nx):
            cells = blocks_of(lambda begin: slow_tile[d, pl.ds(xi + begin, 8, stride=nx), :])
            slow_rows[d, xi, pl.ds(around_y[d], side), :] = jnp.concatenate([cells] * freqs, axis=0).T

    def place_slow_halo(stage):
        first, count = stages[stage]
        if stage == 0:
            edges_l, edges_r = wide_halo_l, wide_halo_r
        else:
            edges_l, edges_r = slow_halo_l, slow_halo_r
        for pair in range(0, count, 2):
            for xi in range(nx):
                from_l = blocks_of(lambda begin: edges_l[pl.ds(xi + begin, 8, stride=nx), :])
                from_r = blocks_of(lambda begin: edges_r[pl.ds(xi + begin, 8, stride=nx), :])
                made = jnp.where(lane < reach, rolled(from_l, -reach * pair, 1), rolled(from_r, reach - reach * pair, 1))
                if pair + 1 < count:
                    made = jnp.where(lane < 2 * reach, made, rolled(from_l, reach * (1 - pair), 1))
                    made = jnp.where(lane < 3 * reach, made, rolled(from_r, reach * (2 - pair), 1))
                turned = jnp.concatenate([made] * freqs, axis=0).T
                for j in range(min(2, count - pair)):
                    d = first + pair + j
                    h = around_y[d]
                    base = 2 * reach * j
                    slow_rows[d, xi, pl.ds(0, h), :] = turned[base + reach - h : base + reach]
                    slow_rows[d, xi, pl.ds(h + side, h), :] = turned[base + reach : base + reach + h]

    def assemble_wave():
        ny = blocks_y[0]
        inside_l = jnp.where(me_y > 0, 1.0, 0.0)
        inside_r = jnp.where(me_y < ycount - 1, 1.0, 0.0)

        def put(part, xi, y0, block):
            yb, yi = y0 // ny, y0 % ny
            begin = ((yi * 2 + part) * nx + xi) * 8 + yb
            terms[0, pl.ds(begin, 8, stride=slab_rows), :] = block

        def middle(i, _):
            for j in range(3):
                xi = i * 3 + j
                grid_x = jnp.where(inside_x(xi, lane), 1.0, 0.0)
                for part in range(2):
                    cells = jnp.concatenate(
                        [
                            blocks_of(lambda begin: tile[part * freqs + f, pl.ds(xi + begin, 8, stride=nx), :])
                            for f in range(freqs)
                        ],
                        axis=0,
                    )
                    turned = cells.T * grid_x
                    for o in range(side // 8):
                        put(part, xi, reach + 8 * o, turned[8 * o : 8 * o + 8])
            return 0

        def beside(i, _):
            for j in range(3):
                xi = i * 3 + j
                grid_x = jnp.where(inside_x(xi, lane), 1.0, 0.0)
                cells = []
                for f in range(freqs):
                    both = []
                    for part in range(2):
                        k, g = (part * freqs + f) // groups, (part * freqs + f) % groups
                        from_l = blocks_of(lambda begin: halo_l[g, pl.ds(xi + begin, 8, stride=nx), :])
                        from_r = blocks_of(lambda begin: halo_r[g, pl.ds(xi + begin, 8, stride=nx), :])
                        at = 2 * reach * part
                        both.append(
                            jnp.where(
                                lane < at + reach, rolled(from_l, at - k * reach, 1), rolled(from_r, at + reach - k * reach, 1)
                            )
                        )
                    cells.append(jnp.where(lane < 2 * reach, both[0], both[1]))
                turned = jnp.concatenate(cells, axis=0).T
                for part in range(2):
                    at = 2 * reach * part
                    beside_l = turned[at : at + reach] * (grid_x * inside_l)
                    beside_r = turned[at + reach : at + 2 * reach] * (grid_x * inside_r)
                    for o in range(reach // 8):
                        put(part, xi, 8 * o, beside_l[8 * o : 8 * o + 8])
                        put(part, xi, reach + side + 8 * o, beside_r[8 * o : 8 * o + 8])
            return 0

        wait_near(wave_copies[:2])
        lax.fori_loop(0, nx // 3, middle, 0)
        wait_near(wave_copies[2:])
        lax.fori_loop(0, nx // 3, beside, 0)

    def slab(n, yi):
        return terms[n, pl.ds(yi * slab_rows, slab_rows), :].reshape(2, nx, 8, 128)

    def x_sum(cells):
        before = pltpu.roll(cells[:, nx - 1 : nx], 1, 3)
        after = pltpu.roll(cells[:, 0:1], 127, 3)
        wide = jnp.concatenate([before, cells, after], axis=1)
        twos = wide[:, :-1] + wide[:, 1:]
        return twos[:, :-1] + twos[:, 1:]

    def next_term(d, n, first):
        ny = blocks_y[d]
        here = slab(n, 0)
        sum_here = x_sum(here)
        sum_first = sum_here
        twos = pltpu.roll(x_sum(slab(n, ny - 1)), 1, 2) + sum_here
        for yi in range(ny):
            if yi + 1 < ny:
                after = slab(n, yi + 1)
                sum_after = x_sum(after)
            else:
                after = None
                sum_after = pltpu.roll(sum_first, 7, 2)
            twos_after = sum_here + sum_after
            nine = twos + twos_after
            rows = pl.ds(yi * slab_rows, slab_rows)
            scale = quarter[d, pl.ds(yi * nx * 8, nx * 8), :].reshape(1, nx, 8, 128)
            if first:
                pair = (0.5 * scale) * nine
            else:
                pair = scale * nine - pair_sum[rows, :].reshape(2, nx, 8, 128)
            pair_sum[rows, :] = pair.reshape(slab_rows, 128)
            terms[n + 1, rows, :] = (pair - here).reshape(slab_rows, 128)
            twos, sum_here, here = twos_after, sum_after, after

    def all_terms(d):
        next_term(d, 0, True)

        def body(n, _):
            next_term(d, n, False)
            return 0

        lax.fori_loop(1, order, body, 0)

    frequency = me_f * freqs + lanes8 // lane_blocks
    omega = (2.0 * math.pi) * (
        LOWEST + (HIGHEST - LOWEST) * (frequency.astype(jnp.float32) + 0.5) / (freqs * fcount)
    )

    def phase_sum(d):
        ny = blocks_y[d]

        def chunk(yi0, count):
            rows = pl.ds(pl.multiple_of(yi0 * slab_rows, 8), count * slab_rows)

            def term(n):
                return terms[n, rows, :].reshape(count, 2, nx, 8, 128)

            slow = jnp.concatenate(
                [
                    slow_rows[d, xi, pl.ds(yi0 + j, 8, stride=ny), :][None]
                    for j in range(count)
                    for xi in range(nx)
                ],
                axis=0,
            )
            angle = (omega * slow).reshape(count, 1, nx, 8, 128)
            square = angle * angle
            cosine = 1.0 + square * (-0.5 + square * (1 / 24.0 + square * (-1 / 720.0)))
            sine = angle * (1.0 + square * (-1 / 6.0 + square * (1 / 120.0 + square * (-1 / 5040.0))))
            double = cosine + cosine
            later = weights[order] * term(order)
            now = weights[order - 1] * term(order - 1) + double * later
            for n in range(order - 2, 0, -1):
                now, later = weights[n] * term(n) + double * now - later, now
            now, later = term(0) + double * now - later, now
            straight = cosine * now - later
            real = straight[:, 0] - sine[:, 0] * now[:, 1]
            imag = straight[:, 1] + sine[:, 0] * now[:, 0]
            for j in range(count):
                for xi in range(nx):
                    rows_buf[0, xi, pl.ds(yi0 + j, 8, stride=ny), :] = real[j, xi]
                    rows_buf[1, xi, pl.ds(yi0 + j, 8, stride=ny), :] = imag[j, xi]

        size = 3

        def body(i, _):
            chunk(i * size, size)
            return 0

        lax.fori_loop(0, ny // size, body, 0)
        if ny % size:
            chunk(ny - ny % size, ny % size)

    def turn(part, xi, h):
        return rows_buf[part, xi, pl.ds(h, side), :].T

    def make_image(d):
        def some(i, _):
            for j in range(3):
                xi = i * 3 + j
                turned = turn(0, xi, around_y[d])
                for o in range(octets):
                    total = turned[8 * o : 8 * o + 8]
                    for f in range(1, freqs):
                        total = total + turned[f * lane_blocks + 8 * o : f * lane_blocks + 8 * o + 8]
                    part_image[d, pl.ds(xi + 8 * nx * o, 8, stride=nx), :] = total
                if d + 1 < depths:
                    ny = blocks_y[d + 1]
                    for yi in range(ny):
                        for part in range(2):
                            rows = pl.ds(pl.multiple_of(((yi * 2 + part) * nx + xi) * 8, 8), 8)
                            terms[0, rows, :] = rows_buf[part, xi, pl.ds(order + yi, 8, stride=ny), :]
            return 0

        lax.fori_loop(0, nx // 3, some, 0)

    def make_natural():
        h = around_y[depths - 1]

        def some(i, _):
            for j in range(3):
                xi = i * 3 + j
                for part in range(2):
                    turned = turn(part, xi, h)
                    for f in range(freqs):
                        for o in range(octets):
                            at = f * lane_blocks + 8 * o
                            natural[part * freqs + f, pl.ds(xi + 8 * nx * o, 8, stride=nx), :] = turned[at : at + 8]
            return 0

        lax.fori_loop(0, nx // 3, some, 0)
        for f in range(freqs):
            for part in range(2):
                out_ref[f, part] = natural[part * freqs + f, pl.ds(reach, side), :] * shared_weight(order) ** depths

    image_stages = [(0, depths - 1), (depths - 1, 1)]
    image_rows = pl.ds(pl.multiple_of(me_f * strip, 8), strip)

    def reduce_copies(stage):
        first, count = image_stages[stage]
        of = pl.ds(first, count)
        return to_peers(
            [
                (
                    part_image.at[of, pl.ds(pl.multiple_of(reach + peer * strip, 8), strip)],
                    image_in.at[k, of],
                )
                for k, peer in enumerate(peers)
            ],
            red_send.at[stage], red_recv.at[stage],
        )

    def cast_image(stage):
        first, count = image_stages[stage]
        of = pl.ds(first, count)
        total = part_image[of, own_rows, :]
        for k in range(fcount - 1):
            total = total + image_in[k, of]
        for d in range(first, first + count):
            scale = shared_weight(order) ** (d + 1) / math.sqrt(freqs * fcount)
            image_out[d, image_rows, :] = total[d - first] * scale
        block = image_out.at[of, image_rows]
        return start(to_peers([(block, block)] * (fcount - 1), cast_send.at[stage], cast_recv.at[stage]))

    wait(slow_first)
    build_slow_edges(0)
    halo_first = start_near(slow_halo_copies(0))
    slow_rest = start(slow_peer_copies(1))
    fill_all_quarters()
    assemble_wave()
    casts = []
    for d in range(depths):
        all_terms(d)
        if d == 0:
            wait_near(halo_first)
            unpack_first_halo()
            place_slow_tile(0)
            place_slow_halo(0)
            wait(slow_rest)
            build_slow_edges(1)
            halo_rest = start_near(slow_halo_copies(1))
        if d == 1:
            wait_near(halo_rest)
            for e in range(1, depths):
                place_slow_tile(e)
            place_slow_halo(1)
        phase_sum(d)
        make_image(d)
        if d == depths - 2:
            reduced = start(reduce_copies(0))
    last = start(reduce_copies(1))
    wait(reduced)
    casts += cast_image(0)
    make_natural()
    wait(last)
    casts += cast_image(1)
    wait(casts)
    image_ref[...] = image_out[...]


def per_device(wavefield, velocity):
    freqs, _, side, _ = wavefield.shape
    depths = velocity.shape[0]
    fcount, xcount, ycount = lax.axis_size("freq"), lax.axis_size("gx"), lax.axis_size("gy")
    reach = ORDER * depths
    extent = side + 2 * reach
    nx, ny = extent * freqs // 128, extent // SUB_BLOCKS
    cells = nx * ny * 8
    batch = 2 * freqs
    groups = batch * reach // 128
    strip = side // fcount
    dims = (depths, freqs, side, fcount, xcount, ycount)
    f32 = jnp.float32
    dma = pltpu.SemaphoreType.DMA
    image, extrapolated = pl.pallas_call(
        functools.partial(kernel, dims),
        out_shape=(
            pltpu.VMEM((depths, side, side), f32),
            pltpu.VMEM(wavefield.shape, f32),
        ),
        in_specs=[pl.BlockSpec(memory_space=pltpu.HBM)] * 2,
        out_specs=(pl.BlockSpec(memory_space=pltpu.VMEM),) * 2,
        scratch_shapes=[
            pltpu.VMEM((ORDER + 1, 2 * cells, 128), f32),
            pltpu.VMEM((2 * cells, 128), f32),
            pltpu.VMEM((depths, cells, 128), f32),
            pltpu.VMEM((2, nx, extent, 128), f32),
            pltpu.VMEM((depths, nx, extent, 128), f32),
            pltpu.VMEM((batch, extent, 128), f32),
            pltpu.VMEM((groups, side, 128), f32),
            pltpu.VMEM((groups, side, 128), f32),
            pltpu.VMEM((groups, extent, 128), f32),
            pltpu.VMEM((groups, extent, 128), f32),
            pltpu.VMEM((batch, extent, 128), f32),
            pltpu.VMEM((depths, strip, 128), f32),
            pltpu.VMEM((depths, extent, 128), f32),
            pltpu.VMEM((side, 128), f32),
            pltpu.VMEM((side, 128), f32),
            pltpu.VMEM((extent, 128), f32),
            pltpu.VMEM((extent, 128), f32),
            pltpu.VMEM((reach, 128), f32),
            pltpu.VMEM((reach, 128), f32),
            pltpu.VMEM((3, reach, 128), f32),
            pltpu.VMEM((3, reach, 128), f32),
            pltpu.VMEM((extent, 128), f32),
            pltpu.VMEM((extent, 128), f32),
            pltpu.VMEM((depths, extent, 128), f32),
            pltpu.VMEM((fcount - 1, depths, strip, 128), f32),
            pltpu.VMEM((depths, side, 128), f32),
            dma((batch + 1,)),
            dma((8,)),
            dma((8,)),
            dma((2, fcount - 1)),
            dma((2, fcount - 1)),
            dma((2, 8)),
            dma((2, 8)),
            dma((depths - 1, 2)),
            dma((depths - 1, 2)),
            dma((2, fcount - 1)),
            dma((2, fcount - 1)),
            dma((2, fcount - 1)),
            dma((2, fcount - 1)),
        ],
        compiler_params=pltpu.CompilerParams(
            collective_id=0, has_side_effects=True, vmem_limit_bytes=66_000_000
        ),
    )(wavefield, velocity)
    return (image, extrapolated)


def solution(mesh):
    placed = (P("freq", None, "gx", "gy"), P(None, ("gx", "freq"), "gy"))
    return jax.shard_map(
        per_device,
        mesh=mesh,
        in_specs=placed,
        out_specs=(P(None, "gx", "gy"), P("freq", None, "gx", "gy")),
        check_vma=False,
    )
```

```python
import functools
import math

import jax
import jax.numpy as jnp
from jax import lax
from jax.experimental import pallas as pl
from jax.experimental.pallas import tpu as pltpu
from jax.sharding import PartitionSpec as P

ORDER = 8
LOWEST = 2.0
HIGHEST = 60.0
INTERVAL = 0.01
MESH = pl.DeviceIdType.MESH
SUB_BLOCKS = 8


def ratios(order):
    return [1.0 / (term + 1) for term in range(order + 1)]


def shared_weight(order):
    return 1.0 / sum(1.0 / (term + 1) for term in range(order + 1))


def rolled(cells, shift, axis):
    shift = shift % cells.shape[axis]
    return cells if shift == 0 else pltpu.roll(cells, shift, axis)


def kernel(
    dims,
    wave_hbm, vel_hbm, image_ref, out_ref,
    terms, pair_sum, quarter, rows_buf, slow_rows, tile, edge_r, edge_l, halo_l, halo_r, natural,
    vel_raw, slow_tile, slow_edge_r, slow_edge_l, slow_halo_l, slow_halo_r,
    first_edge_r, first_edge_l, first_halo_l, first_halo_r, wide_halo_l, wide_halo_r,
    part_image, image_in, image_out,
    load_sem, wave_send, wave_recv, vel_send, vel_recv, velh_send, velh_recv, rows_send, rows_recv,
    red_send, red_recv, cast_send, cast_recv,
):
    depths, freqs, side, fcount, xcount, ycount = dims
    order = ORDER
    weights = ratios(order)
    reach = order * depths
    extent = side + 2 * reach
    lane_blocks = 128 // freqs
    octets = lane_blocks // 8
    nx = extent // lane_blocks
    slab_rows = 2 * nx * 8
    batch = 2 * freqs
    inner = 128 // reach
    groups = batch // inner
    strip = side // fcount
    around_y = [reach - order * d for d in range(depths)]
    blocks_y = [(side + 2 * h) // SUB_BLOCKS for h in around_y]

    me_f = lax.axis_index("freq")
    me_x = lax.axis_index("gx")
    me_y = lax.axis_index("gy")

    def mod(value, count):
        return lax.rem(value + count, count)

    up, down = mod(me_x - 1, xcount), mod(me_x + 1, xcount)
    left, right = mod(me_y - 1, ycount), mod(me_y + 1, ycount)
    around = [
        {"gx": up, "gy": me_y}, {"gx": down, "gy": me_y}, {"gx": me_x, "gy": right}, {"gx": me_x, "gy": left},
        {"gx": up, "gy": right}, {"gx": down, "gy": right}, {"gx": up, "gy": left}, {"gx": down, "gy": left},
    ]
    peers = [mod(me_f + k, fcount) for k in range(1, fcount)]

    has_up, has_down = me_x > 0, me_x < xcount - 1
    has_left, has_right = me_y > 0, me_y < ycount - 1
    present = [
        has_up, has_down, has_right, has_left,
        has_up & has_right, has_down & has_right, has_up & has_left, has_down & has_left,
    ]
    opposite = [1, 0, 3, 2, 7, 6, 5, 4]

    barrier = pltpu.get_barrier_semaphore()
    greeted = jnp.int32(fcount - 1)
    for way, device in enumerate(around):
        greeted = greeted + jnp.where(present[way], 1, 0)

        @pl.when(present[way])
        def _():
            pl.semaphore_signal(barrier, inc=1, device_id=device, device_id_type=MESH)

    for peer in peers:
        pl.semaphore_signal(barrier, inc=1, device_id={"freq": peer}, device_id_type=MESH)

    vel_load = pltpu.make_async_copy(vel_hbm, vel_raw, load_sem.at[batch])
    vel_load.start()
    loads = []
    for f in range(freqs):
        for part in range(2):
            loads.append(
                pltpu.make_async_copy(
                    wave_hbm.at[f, part], tile.at[part * freqs + f, pl.ds(reach, side)], load_sem.at[f * 2 + part]
                )
            )
    for copy in loads:
        copy.start()

    own_rows = pl.ds(pl.multiple_of(reach + me_f * strip, 8), strip)
    vel_load.wait()
    slow_tile[:, own_rows, :] = (INTERVAL / (order + 1)) / vel_raw[...]
    for copy in loads:
        copy.wait()

    lane = lax.broadcasted_iota(jnp.int32, (1, 128), 1)

    def build_edges(i, _):
        rows = pl.ds(pl.multiple_of(i * 32, 32), 32)
        source_rows = pl.ds(pl.multiple_of(reach + i * 32, 8), 32)
        for target, first in ((edge_r, side - reach), (edge_l, 0)):
            for g in range(groups):
                made = None
                for k in range(inner):
                    moved = rolled(tile[k * groups + g, source_rows, :], k * reach - first, 1)
                    made = moved if made is None else jnp.where(lane >= k * reach, moved, made)
                target[g, rows, :] = made
        return 0

    lax.fori_loop(0, side // 32, build_edges, 0)

    head, tail = pl.ds(0, reach), pl.ds(side - reach, reach)
    low, mid, high = pl.ds(0, reach), pl.ds(reach, side), pl.ds(reach + side, reach)
    own_head, own_tail = pl.ds(reach, reach), pl.ds(side, reach)

    def to_neighbours(pairs, send_sem, recv_sem):
        return [
            (k, pltpu.make_async_remote_copy(
                src_ref=source, dst_ref=target, send_sem=send_sem.at[k], recv_sem=recv_sem.at[k],
                device_id=around[k], device_id_type=MESH,
            ))
            for k, (source, target) in [(k, pair) for k, pair in enumerate(pairs) if pair is not None]
        ]

    def to_peers(pairs, send_sem, recv_sem):
        return [
            pltpu.make_async_remote_copy(
                src_ref=source, dst_ref=target, send_sem=send_sem.at[k], recv_sem=recv_sem.at[k],
                device_id={"freq": peers[k]}, device_id_type=MESH,
            )
            for k, (source, target) in enumerate(pairs)
        ]

    def start(copies):
        for copy in copies:
            copy.start()
        return copies

    def wait(copies):
        for copy in copies:
            copy.wait()

    def start_near(copies):
        for way in range(8):
            here = [copy for k, copy in copies if k == way]
            if here:

                @pl.when(present[way])
                def _():
                    for copy in here:
                        copy.start()

        return copies

    def wait_near(copies):
        for way in range(8):
            sent = [copy for k, copy in copies if k == way]
            received = [copy for k, copy in copies if k == opposite[way]]
            if sent or received:

                @pl.when(present[way])
                def _():
                    for copy in sent:
                        copy.wait_send()
                    for copy in received:
                        copy.wait_recv()

    def clear(refs):
        for ref in refs:
            ref[...] = jnp.zeros(ref.shape, jnp.float32)

    @pl.when(me_y == 0)
    def _():
        clear((halo_l, first_halo_l, slow_halo_l))

    @pl.when(me_y == ycount - 1)
    def _():
        clear((halo_r, first_halo_r, slow_halo_r))

    @pl.when(me_x == 0)
    def _():
        clear((tile.at[:, low], slow_tile.at[:, low]))
        for wide, first, later in ((halo_l, first_halo_l, slow_halo_l), (halo_r, first_halo_r, slow_halo_r)):
            clear((wide.at[:, low], first.at[0], later.at[low]))

    @pl.when(me_x == xcount - 1)
    def _():
        clear((tile.at[:, high], slow_tile.at[:, high]))
        for wide, first, later in ((halo_l, first_halo_l, slow_halo_l), (halo_r, first_halo_r, slow_halo_r)):
            clear((wide.at[:, high], first.at[2], later.at[high]))

    wave_copies = to_neighbours(
        [
            (tile.at[:, own_head], tile.at[:, high]),
            (tile.at[:, own_tail], tile.at[:, low]),
            (edge_r, halo_l.at[:, mid]),
            (edge_l, halo_r.at[:, mid]),
            (edge_r.at[:, head], halo_l.at[:, high]),
            (edge_r.at[:, tail], halo_l.at[:, low]),
            (edge_l.at[:, head], halo_r.at[:, high]),
            (edge_l.at[:, tail], halo_r.at[:, low]),
        ],
        wave_send, wave_recv,
    )
    stages = [(0, 1), (1, depths - 1)]
    ahead = [reach - order * (d + 1) for d in range(depths)]

    def slow_peer_copies(stage):
        first, count = stages[stage]
        block = slow_tile.at[pl.ds(first, count), own_rows]
        return to_peers([(block, block)] * (fcount - 1), vel_send.at[stage], vel_recv.at[stage])

    def slow_halo_copies(stage):
        copies = []
        for k, d in enumerate([0] if stage == 0 else range(1, depths - 1)):
            w = ahead[d]
            rows = [
                (slow_tile.at[d, pl.ds(reach, w)], slow_tile.at[d, pl.ds(reach + side, w)]),
                (slow_tile.at[d, pl.ds(reach + side - w, w)], slow_tile.at[d, pl.ds(reach - w, w)]),
            ]
            copies += to_neighbours(rows, rows_send.at[stage + k], rows_recv.at[stage + k])
        if stage == 0:
            sides = [(first_edge_r, first_halo_l.at[1]), (first_edge_l, first_halo_r.at[1])]
            for edge, halo in ((first_edge_r, first_halo_l), (first_edge_l, first_halo_r)):
                sides += [(edge, halo.at[2]), (edge, halo.at[0])]
        else:
            w = ahead[1]
            sides = [(slow_edge_r, slow_halo_l.at[mid]), (slow_edge_l, slow_halo_r.at[mid])]
            for edge, halo in ((slow_edge_r, slow_halo_l), (slow_edge_l, slow_halo_r)):
                sides += [
                    (edge.at[pl.ds(0, w)], halo.at[pl.ds(reach + side, w)]),
                    (edge.at[pl.ds(side - w, w)], halo.at[pl.ds(reach - w, w)]),
                ]
        return copies + to_neighbours([None, None] + sides, velh_send.at[stage], velh_recv.at[stage])

    def build_slow_edges(stage):
        if stage == 0:
            for target, source in ((first_edge_r, side - reach), (first_edge_l, 0)):
                made = None
                for j in range(side // reach):
                    moved = rolled(slow_tile[0, pl.ds(reach + reach * j, reach), :], reach * j - source, 1)
                    made = moved if made is None else jnp.where(lane >= reach * j, moved, made)
                target[...] = made
            return
        first, count = stages[stage]
        for target, source in ((slow_edge_r, side - reach), (slow_edge_l, 0)):
            made = None
            for j in range(count):
                moved = rolled(slow_tile[first + j, pl.ds(reach, side), :], reach * j - source, 1)
                made = moved if made is None else jnp.where(lane >= reach * j, moved, made)
            target[...] = made

    def unpack_first_halo():
        for halo, target in ((first_halo_l, wide_halo_l), (first_halo_r, wide_halo_r)):
            target[pl.ds(0, reach), :] = rolled(halo[0], -(side - reach), 1)
            for j in range(side // reach):
                target[pl.ds(reach + reach * j, reach), :] = rolled(halo[1], -reach * j, 1)
            target[pl.ds(reach + side, reach), :] = halo[2]

    for d in range(depths):
        rest = reach - (ahead[d] if d < depths - 1 else 0)
        slow_tile[d, pl.ds(0, rest), :] = jnp.zeros((rest, side), jnp.float32)
        slow_tile[d, pl.ds(extent - rest, rest), :] = jnp.zeros((rest, side), jnp.float32)
    rest = reach - ahead[1]
    for halo in (slow_halo_l, slow_halo_r):
        halo[pl.ds(0, rest), :] = jnp.zeros((rest, side), jnp.float32)
        halo[pl.ds(extent - rest, rest), :] = jnp.zeros((rest, side), jnp.float32)

    pl.semaphore_wait(barrier, greeted)
    slow_first = start(slow_peer_copies(0))
    start_near(wave_copies)

    lanes8 = lax.broadcasted_iota(jnp.int32, (8, 128), 1)
    subs8 = lax.broadcasted_iota(jnp.int32, (8, 128), 0)

    def inside_x(xi, lanes):
        x = me_x * side - reach + lax.rem(lanes, lane_blocks) * nx + xi
        return (x >= 0) & (x < xcount * side)

    def fill_quarters(d):
        def fill_quarter(yi, _):
            y = me_y * side - around_y[d] + subs8 * blocks_y[d] + yi
            inside_y = jnp.where((y >= 0) & (y < ycount * side), 0.25, 0.0)
            for xi in range(nx):
                rows = pl.ds(pl.multiple_of((yi * nx + xi) * 8, 8), 8)
                quarter[d, rows, :] = jnp.where(inside_x(xi, lanes8), inside_y, 0.0)
            return 0

        lax.fori_loop(0, blocks_y[d], fill_quarter, 0)

    def fill_all_quarters():
        for d in range(depths):
            fill_quarters(d)

    def blocks_of(load):
        return jnp.concatenate([load(8 * nx * o) for o in range(octets)], axis=0)

    def place_slow_tile(d):
        for xi in range(nx):
            cells = blocks_of(lambda begin: slow_tile[d, pl.ds(xi + begin, 8, stride=nx), :])
            slow_rows[d, xi, pl.ds(around_y[d], side), :] = jnp.concatenate([cells] * freqs, axis=0).T

    def place_slow_halo(stage):
        first, count = stages[stage]
        if stage == 0:
            edges_l, edges_r = wide_halo_l, wide_halo_r
        else:
            edges_l, edges_r = slow_halo_l, slow_halo_r
        for pair in range(0, count, 2):
            for xi in range(nx):
                from_l = blocks_of(lambda begin: edges_l[pl.ds(xi + begin, 8, stride=nx), :])
                from_r = blocks_of(lambda begin: edges_r[pl.ds(xi + begin, 8, stride=nx), :])
                made = jnp.where(lane < reach, rolled(from_l, -reach * pair, 1), rolled(from_r, reach - reach * pair, 1))
                if pair + 1 < count:
                    made = jnp.where(lane < 2 * reach, made, rolled(from_l, reach * (1 - pair), 1))
                    made = jnp.where(lane < 3 * reach, made, rolled(from_r, reach * (2 - pair), 1))
                turned = jnp.concatenate([made] * freqs, axis=0).T
                for j in range(min(2, count - pair)):
                    d = first + pair + j
                    h = around_y[d]
                    base = 2 * reach * j
                    slow_rows[d, xi, pl.ds(0, h), :] = turned[base + reach - h : base + reach]
                    slow_rows[d, xi, pl.ds(h + side, h), :] = turned[base + reach : base + reach + h]

    def assemble_wave():
        ny = blocks_y[0]
        inside_l = jnp.where(me_y > 0, 1.0, 0.0)
        inside_r = jnp.where(me_y < ycount - 1, 1.0, 0.0)

        def put(part, xi, y0, block):
            yb, yi = y0 // ny, y0 % ny
            begin = ((yi * 2 + part) * nx + xi) * 8 + yb
            terms[0, pl.ds(begin, 8, stride=slab_rows), :] = block

        def middle(i, _):
            for j in range(3):
                xi = i * 3 + j
                grid_x = jnp.where(inside_x(xi, lane), 1.0, 0.0)
                for part in range(2):
                    cells = jnp.concatenate(
                        [
                            blocks_of(lambda begin: tile[part * freqs + f, pl.ds(xi + begin, 8, stride=nx), :])
                            for f in range(freqs)
                        ],
                        axis=0,
                    )
                    turned = cells.T * grid_x
                    for o in range(side // 8):
                        put(part, xi, reach + 8 * o, turned[8 * o : 8 * o + 8])
            return 0

        def beside(i, _):
            for j in range(3):
                xi = i * 3 + j
                grid_x = jnp.where(inside_x(xi, lane), 1.0, 0.0)
                cells = []
                for f in range(freqs):
                    both = []
                    for part in range(2):
                        k, g = (part * freqs + f) // groups, (part * freqs + f) % groups
                        from_l = blocks_of(lambda begin: halo_l[g, pl.ds(xi + begin, 8, stride=nx), :])
                        from_r = blocks_of(lambda begin: halo_r[g, pl.ds(xi + begin, 8, stride=nx), :])
                        at = 2 * reach * part
                        both.append(
                            jnp.where(
                                lane < at + reach, rolled(from_l, at - k * reach, 1), rolled(from_r, at + reach - k * reach, 1)
                            )
                        )
                    cells.append(jnp.where(lane < 2 * reach, both[0], both[1]))
                turned = jnp.concatenate(cells, axis=0).T
                for part in range(2):
                    at = 2 * reach * part
                    beside_l = turned[at : at + reach] * (grid_x * inside_l)
                    beside_r = turned[at + reach : at + 2 * reach] * (grid_x * inside_r)
                    for o in range(reach // 8):
                        put(part, xi, 8 * o, beside_l[8 * o : 8 * o + 8])
                        put(part, xi, reach + side + 8 * o, beside_r[8 * o : 8 * o + 8])
            return 0

        wait_near(wave_copies[:2])
        lax.fori_loop(0, nx // 3, middle, 0)
        wait_near(wave_copies[2:])
        lax.fori_loop(0, nx // 3, beside, 0)

    def slab(n, yi):
        return terms[n, pl.ds(yi * slab_rows, slab_rows), :].reshape(2, nx, 8, 128)

    def x_sum(cells):
        before = pltpu.roll(cells[:, nx - 1 : nx], 1, 3)
        after = pltpu.roll(cells[:, 0:1], 127, 3)
        wide = jnp.concatenate([before, cells, after], axis=1)
        twos = wide[:, :-1] + wide[:, 1:]
        return twos[:, :-1] + twos[:, 1:]

    def next_term(d, n, first):
        ny = blocks_y[d]
        here = slab(n, 0)
        sum_here = x_sum(here)
        sum_first = sum_here
        twos = pltpu.roll(x_sum(slab(n, ny - 1)), 1, 2) + sum_here
        for yi in range(ny):
            if yi + 1 < ny:
                after = slab(n, yi + 1)
                sum_after = x_sum(after)
            else:
                after = None
                sum_after = pltpu.roll(sum_first, 7, 2)
            twos_after = sum_here + sum_after
            nine = twos + twos_after
            rows = pl.ds(yi * slab_rows, slab_rows)
            scale = quarter[d, pl.ds(yi * nx * 8, nx * 8), :].reshape(1, nx, 8, 128)
            if first:
                pair = (0.5 * scale) * nine
            else:
                pair = scale * nine - pair_sum[rows, :].reshape(2, nx, 8, 128)
            pair_sum[rows, :] = pair.reshape(slab_rows, 128)
            terms[n + 1, rows, :] = (pair - here).reshape(slab_rows, 128)
            twos, sum_here, here = twos_after, sum_after, after

    def all_terms(d):
        next_term(d, 0, True)

        def body(n, _):
            next_term(d, n, False)
            return 0

        lax.fori_loop(1, order, body, 0)

    frequency = me_f * freqs + lanes8 // lane_blocks
    omega = (2.0 * math.pi) * (
        LOWEST + (HIGHEST - LOWEST) * (frequency.astype(jnp.float32) + 0.5) / (freqs * fcount)
    )

    def phase_sum(d):
        ny = blocks_y[d]

        def chunk(yi0, count):
            rows = pl.ds(pl.multiple_of(yi0 * slab_rows, 8), count * slab_rows)

            def term(n):
                return terms[n, rows, :].reshape(count, 2, nx, 8, 128)

            slow = jnp.concatenate(
                [
                    slow_rows[d, xi, pl.ds(yi0 + j, 8, stride=ny), :][None]
                    for j in range(count)
                    for xi in range(nx)
                ],
                axis=0,
            )
            angle = (omega * slow).reshape(count, 1, nx, 8, 128)
            square = angle * angle
            cosine = 1.0 + square * (-0.5 + square * (1 / 24.0 + square * (-1 / 720.0)))
            sine = angle * (1.0 + square * (-1 / 6.0 + square * (1 / 120.0 + square * (-1 / 5040.0))))
            double = cosine + cosine
            later = weights[order] * term(order)
            now = weights[order - 1] * term(order - 1) + double * later
            for n in range(order - 2, 0, -1):
                now, later = weights[n] * term(n) + double * now - later, now
            now, later = term(0) + double * now - later, now
            straight = cosine * now - later
            real = straight[:, 0] - sine[:, 0] * now[:, 1]
            imag = straight[:, 1] + sine[:, 0] * now[:, 0]
            for j in range(count):
                for xi in range(nx):
                    rows_buf[0, xi, pl.ds(yi0 + j, 8, stride=ny), :] = real[j, xi]
                    rows_buf[1, xi, pl.ds(yi0 + j, 8, stride=ny), :] = imag[j, xi]

        size = 3

        def body(i, _):
            chunk(i * size, size)
            return 0

        lax.fori_loop(0, ny // size, body, 0)
        if ny % size:
            chunk(ny - ny % size, ny % size)

    def turn(part, xi, h):
        return rows_buf[part, xi, pl.ds(h, side), :].T

    def make_image(d):
        def some(i, _):
            for j in range(3):
                xi = i * 3 + j
                turned = turn(0, xi, around_y[d])
                for o in range(octets):
                    total = turned[8 * o : 8 * o + 8]
                    for f in range(1, freqs):
                        total = total + turned[f * lane_blocks + 8 * o : f * lane_blocks + 8 * o + 8]
                    part_image[d, pl.ds(xi + 8 * nx * o, 8, stride=nx), :] = total
                if d + 1 < depths:
                    ny = blocks_y[d + 1]
                    for yi in range(ny):
                        for part in range(2):
                            rows = pl.ds(pl.multiple_of(((yi * 2 + part) * nx + xi) * 8, 8), 8)
                            terms[0, rows, :] = rows_buf[part, xi, pl.ds(order + yi, 8, stride=ny), :]
            return 0

        lax.fori_loop(0, nx // 3, some, 0)

    def make_natural():
        h = around_y[depths - 1]

        def some(i, _):
            for j in range(3):
                xi = i * 3 + j
                for part in range(2):
                    turned = turn(part, xi, h)
                    for f in range(freqs):
                        for o in range(octets):
                            at = f * lane_blocks + 8 * o
                            natural[part * freqs + f, pl.ds(xi + 8 * nx * o, 8, stride=nx), :] = turned[at : at + 8]
            return 0

        lax.fori_loop(0, nx // 3, some, 0)
        for f in range(freqs):
            for part in range(2):
                out_ref[f, part] = natural[part * freqs + f, pl.ds(reach, side), :] * shared_weight(order) ** depths

    image_stages = [(0, depths - 1), (depths - 1, 1)]
    image_rows = pl.ds(pl.multiple_of(me_f * strip, 8), strip)

    def reduce_copies(stage):
        first, count = image_stages[stage]
        of = pl.ds(first, count)
        return to_peers(
            [
                (
                    part_image.at[of, pl.ds(pl.multiple_of(reach + peer * strip, 8), strip)],
                    image_in.at[k, of],
                )
                for k, peer in enumerate(peers)
            ],
            red_send.at[stage], red_recv.at[stage],
        )

    def cast_image(stage):
        first, count = image_stages[stage]
        of = pl.ds(first, count)
        total = part_image[of, own_rows, :]
        for k in range(fcount - 1):
            total = total + image_in[k, of]
        for d in range(first, first + count):
            scale = shared_weight(order) ** (d + 1) / math.sqrt(freqs * fcount)
            image_out[d, image_rows, :] = total[d - first] * scale
        block = image_out.at[of, image_rows]
        return start(to_peers([(block, block)] * (fcount - 1), cast_send.at[stage], cast_recv.at[stage]))

    wait(slow_first)
    build_slow_edges(0)
    halo_first = start_near(slow_halo_copies(0))
    slow_rest = start(slow_peer_copies(1))
    fill_all_quarters()
    assemble_wave()
    casts = []
    for d in range(depths):
        all_terms(d)
        if d == 0:
            wait_near(halo_first)
            unpack_first_halo()
            place_slow_tile(0)
            place_slow_halo(0)
            wait(slow_rest)
            build_slow_edges(1)
            halo_rest = start_near(slow_halo_copies(1))
        if d == 1:
            wait_near(halo_rest)
            for e in range(1, depths):
                place_slow_tile(e)
            place_slow_halo(1)
        phase_sum(d)
        make_image(d)
        if d == depths - 2:
            reduced = start(reduce_copies(0))
    last = start(reduce_copies(1))
    wait(reduced)
    casts += cast_image(0)
    make_natural()
    wait(last)
    casts += cast_image(1)
    wait(casts)
    image_ref[...] = image_out[...]


def per_device(wavefield, velocity):
    freqs, _, side, _ = wavefield.shape
    depths = velocity.shape[0]
    fcount, xcount, ycount = lax.axis_size("freq"), lax.axis_size("gx"), lax.axis_size("gy")
    reach = ORDER * depths
    extent = side + 2 * reach
    nx, ny = extent * freqs // 128, extent // SUB_BLOCKS
    cells = nx * ny * 8
    batch = 2 * freqs
    groups = batch * reach // 128
    strip = side // fcount
    dims = (depths, freqs, side, fcount, xcount, ycount)
    f32 = jnp.float32
    dma = pltpu.SemaphoreType.DMA
    image, extrapolated = pl.pallas_call(
        functools.partial(kernel, dims),
        out_shape=(
            pltpu.VMEM((depths, side, side), f32),
            pltpu.VMEM(wavefield.shape, f32),
        ),
        in_specs=[pl.BlockSpec(memory_space=pltpu.HBM)] * 2,
        out_specs=(pl.BlockSpec(memory_space=pltpu.VMEM),) * 2,
        scratch_shapes=[
            pltpu.VMEM((ORDER + 1, 2 * cells, 128), f32),
            pltpu.VMEM((2 * cells, 128), f32),
            pltpu.VMEM((depths, cells, 128), f32),
            pltpu.VMEM((2, nx, extent, 128), f32),
            pltpu.VMEM((depths, nx, extent, 128), f32),
            pltpu.VMEM((batch, extent, 128), f32),
            pltpu.VMEM((groups, side, 128), f32),
            pltpu.VMEM((groups, side, 128), f32),
            pltpu.VMEM((groups, extent, 128), f32),
            pltpu.VMEM((groups, extent, 128), f32),
            pltpu.VMEM((batch, extent, 128), f32),
            pltpu.VMEM((depths, strip, 128), f32),
            pltpu.VMEM((depths, extent, 128), f32),
            pltpu.VMEM((side, 128), f32),
            pltpu.VMEM((side, 128), f32),
            pltpu.VMEM((extent, 128), f32),
            pltpu.VMEM((extent, 128), f32),
            pltpu.VMEM((reach, 128), f32),
            pltpu.VMEM((reach, 128), f32),
            pltpu.VMEM((3, reach, 128), f32),
            pltpu.VMEM((3, reach, 128), f32),
            pltpu.VMEM((extent, 128), f32),
            pltpu.VMEM((extent, 128), f32),
            pltpu.VMEM((depths, extent, 128), f32),
            pltpu.VMEM((fcount - 1, depths, strip, 128), f32),
            pltpu.VMEM((depths, side, 128), f32),
            dma((batch + 1,)),
            dma((8,)),
            dma((8,)),
            dma((2, fcount - 1)),
            dma((2, fcount - 1)),
            dma((2, 8)),
            dma((2, 8)),
            dma((depths - 1, 2)),
            dma((depths - 1, 2)),
            dma((2, fcount - 1)),
            dma((2, fcount - 1)),
            dma((2, fcount - 1)),
            dma((2, fcount - 1)),
        ],
        compiler_params=pltpu.CompilerParams(
            collective_id=0, has_side_effects=True, vmem_limit_bytes=66_000_000
        ),
    )(wavefield, velocity)
    return (image, extrapolated)


def solution(mesh):
    placed = (P("freq", None, "gx", "gy"), P(None, ("gx", "freq"), "gy"))
    return jax.shard_map(
        per_device,
        mesh=mesh,
        in_specs=placed,
        out_specs=(P(None, "gx", "gy"), P("freq", None, "gx", "gy")),
        check_vma=False,
    )
```

```python
import functools
import math

import jax
import jax.numpy as jnp
from jax import lax
from jax.experimental import pallas as pl
from jax.experimental.pallas import tpu as pltpu
from jax.sharding import PartitionSpec as P

ORDER = 8
LOWEST = 2.0
HIGHEST = 60.0
INTERVAL = 0.01
MESH = pl.DeviceIdType.MESH
SUB_BLOCKS = 8


def ratios(order):
    return [1.0 / (term + 1) for term in range(order + 1)]


def shared_weight(order):
    return 1.0 / sum(1.0 / (term + 1) for term in range(order + 1))


def rolled(cells, shift, axis):
    shift = shift % cells.shape[axis]
    return cells if shift == 0 else pltpu.roll(cells, shift, axis)


def kernel(
    dims,
    wave_hbm, vel_hbm, image_ref, out_ref,
    terms, pair_sum, quarter, rows_buf, slow_rows, tile, edge_r, edge_l, halo_l, halo_r, natural,
    vel_raw, slow_tile, slow_edge_r, slow_edge_l, slow_halo_l, slow_halo_r,
    first_edge_r, first_edge_l, first_halo_l, first_halo_r, wide_halo_l, wide_halo_r,
    part_image, image_in, image_out,
    load_sem, wave_send, wave_recv, vel_send, vel_recv, velh_send, velh_recv, rows_send, rows_recv,
    red_send, red_recv, cast_send, cast_recv,
):
    depths, freqs, side, fcount, xcount, ycount = dims
    order = ORDER
    weights = ratios(order)
    reach = order * depths
    extent = side + 2 * reach
    lane_blocks = 128 // freqs
    octets = lane_blocks // 8
    nx = extent // lane_blocks
    slab_rows = 2 * nx * 8
    batch = 2 * freqs
    inner = 128 // reach
    groups = batch // inner
    strip = side // fcount
    around_y = [reach - order * d for d in range(depths)]
    blocks_y = [(side + 2 * h) // SUB_BLOCKS for h in around_y]

    me_f = lax.axis_index("freq")
    me_x = lax.axis_index("gx")
    me_y = lax.axis_index("gy")

    def mod(value, count):
        return lax.rem(value + count, count)

    up, down = mod(me_x - 1, xcount), mod(me_x + 1, xcount)
    left, right = mod(me_y - 1, ycount), mod(me_y + 1, ycount)
    around = [
        {"gx": up, "gy": me_y}, {"gx": down, "gy": me_y}, {"gx": me_x, "gy": right}, {"gx": me_x, "gy": left},
        {"gx": up, "gy": right}, {"gx": down, "gy": right}, {"gx": up, "gy": left}, {"gx": down, "gy": left},
    ]
    peers = [mod(me_f + k, fcount) for k in range(1, fcount)]

    has_up, has_down = me_x > 0, me_x < xcount - 1
    has_left, has_right = me_y > 0, me_y < ycount - 1
    present = [
        has_up, has_down, has_right, has_left,
        has_up & has_right, has_down & has_right, has_up & has_left, has_down & has_left,
    ]
    opposite = [1, 0, 3, 2, 7, 6, 5, 4]

    barrier = pltpu.get_barrier_semaphore()
    greeted = jnp.int32(fcount - 1)
    for way, device in enumerate(around):
        greeted = greeted + jnp.where(present[way], 1, 0)

        @pl.when(present[way])
        def _():
            pl.semaphore_signal(barrier, inc=1, device_id=device, device_id_type=MESH)

    for peer in peers:
        pl.semaphore_signal(barrier, inc=1, device_id={"freq": peer}, device_id_type=MESH)

    vel_load = pltpu.make_async_copy(vel_hbm, vel_raw, load_sem.at[batch])
    vel_load.start()
    loads = []
    for f in range(freqs):
        for part in range(2):
            loads.append(
                pltpu.make_async_copy(
                    wave_hbm.at[f, part], tile.at[part * freqs + f, pl.ds(reach, side)], load_sem.at[f * 2 + part]
                )
            )
    for copy in loads:
        copy.start()

    own_rows = pl.ds(pl.multiple_of(reach + me_f * strip, 8), strip)
    vel_load.wait()
    slow_tile[:, own_rows, :] = (INTERVAL / (order + 1)) / vel_raw[...]
    for copy in loads:
        copy.wait()

    lane = lax.broadcasted_iota(jnp.int32, (1, 128), 1)

    def build_edges(i, _):
        rows = pl.ds(pl.multiple_of(i * 32, 32), 32)
        source_rows = pl.ds(pl.multiple_of(reach + i * 32, 8), 32)
        for target, first in ((edge_r, side - reach), (edge_l, 0)):
            for g in range(groups):
                made = None
                for k in range(inner):
                    moved = rolled(tile[k * groups + g, source_rows, :], k * reach - first, 1)
                    made = moved if made is None else jnp.where(lane >= k * reach, moved, made)
                target[g, rows, :] = made
        return 0

    lax.fori_loop(0, side // 32, build_edges, 0)

    head, tail = pl.ds(0, reach), pl.ds(side - reach, reach)
    low, mid, high = pl.ds(0, reach), pl.ds(reach, side), pl.ds(reach + side, reach)
    own_head, own_tail = pl.ds(reach, reach), pl.ds(side, reach)

    def to_neighbours(pairs, send_sem, recv_sem):
        return [
            (k, pltpu.make_async_remote_copy(
                src_ref=source, dst_ref=target, send_sem=send_sem.at[k], recv_sem=recv_sem.at[k],
                device_id=around[k], device_id_type=MESH,
            ))
            for k, (source, target) in [(k, pair) for k, pair in enumerate(pairs) if pair is not None]
        ]

    def to_peers(pairs, send_sem, recv_sem):
        return [
            pltpu.make_async_remote_copy(
                src_ref=source, dst_ref=target, send_sem=send_sem.at[k], recv_sem=recv_sem.at[k],
                device_id={"freq": peers[k]}, device_id_type=MESH,
            )
            for k, (source, target) in enumerate(pairs)
        ]

    def start(copies):
        for copy in copies:
            copy.start()
        return copies

    def wait(copies):
        for copy in copies:
            copy.wait()

    def start_near(copies):
        for way in range(8):
            here = [copy for k, copy in copies if k == way]
            if here:

                @pl.when(present[way])
                def _():
                    for copy in here:
                        copy.start()

        return copies

    def wait_near(copies):
        for way in range(8):
            sent = [copy for k, copy in copies if k == way]
            received = [copy for k, copy in copies if k == opposite[way]]
            if sent or received:

                @pl.when(present[way])
                def _():
                    for copy in sent:
                        copy.wait_send()
                    for copy in received:
                        copy.wait_recv()

    def clear(refs):
        for ref in refs:
            ref[...] = jnp.zeros(ref.shape, jnp.float32)

    @pl.when(me_y == 0)
    def _():
        clear((halo_l, first_halo_l, slow_halo_l))

    @pl.when(me_y == ycount - 1)
    def _():
        clear((halo_r, first_halo_r, slow_halo_r))

    @pl.when(me_x == 0)
    def _():
        clear((tile.at[:, low], slow_tile.at[:, low]))
        for wide, first, later in ((halo_l, first_halo_l, slow_halo_l), (halo_r, first_halo_r, slow_halo_r)):
            clear((wide.at[:, low], first.at[0], later.at[low]))

    @pl.when(me_x == xcount - 1)
    def _():
        clear((tile.at[:, high], slow_tile.at[:, high]))
        for wide, first, later in ((halo_l, first_halo_l, slow_halo_l), (halo_r, first_halo_r, slow_halo_r)):
            clear((wide.at[:, high], first.at[2], later.at[high]))

    wave_copies = to_neighbours(
        [
            (tile.at[:, own_head], tile.at[:, high]),
            (tile.at[:, own_tail], tile.at[:, low]),
            (edge_r, halo_l.at[:, mid]),
            (edge_l, halo_r.at[:, mid]),
            (edge_r.at[:, head], halo_l.at[:, high]),
            (edge_r.at[:, tail], halo_l.at[:, low]),
            (edge_l.at[:, head], halo_r.at[:, high]),
            (edge_l.at[:, tail], halo_r.at[:, low]),
        ],
        wave_send, wave_recv,
    )
    stages = [(0, 1), (1, depths - 1)]
    ahead = [reach - order * (d + 1) for d in range(depths)]

    def slow_peer_copies(stage):
        first, count = stages[stage]
        block = slow_tile.at[pl.ds(first, count), own_rows]
        return to_peers([(block, block)] * (fcount - 1), vel_send.at[stage], vel_recv.at[stage])

    def slow_halo_copies(stage):
        copies = []
        for k, d in enumerate([0] if stage == 0 else range(1, depths - 1)):
            w = ahead[d]
            rows = [
                (slow_tile.at[d, pl.ds(reach, w)], slow_tile.at[d, pl.ds(reach + side, w)]),
                (slow_tile.at[d, pl.ds(reach + side - w, w)], slow_tile.at[d, pl.ds(reach - w, w)]),
            ]
            copies += to_neighbours(rows, rows_send.at[stage + k], rows_recv.at[stage + k])
        if stage == 0:
            sides = [(first_edge_r, first_halo_l.at[1]), (first_edge_l, first_halo_r.at[1])]
            for edge, halo in ((first_edge_r, first_halo_l), (first_edge_l, first_halo_r)):
                sides += [(edge, halo.at[2]), (edge, halo.at[0])]
        else:
            w = ahead[1]
            sides = [(slow_edge_r, slow_halo_l.at[mid]), (slow_edge_l, slow_halo_r.at[mid])]
            for edge, halo in ((slow_edge_r, slow_halo_l), (slow_edge_l, slow_halo_r)):
                sides += [
                    (edge.at[pl.ds(0, w)], halo.at[pl.ds(reach + side, w)]),
                    (edge.at[pl.ds(side - w, w)], halo.at[pl.ds(reach - w, w)]),
                ]
        return copies + to_neighbours([None, None] + sides, velh_send.at[stage], velh_recv.at[stage])

    def build_slow_edges(stage):
        if stage == 0:
            for target, source in ((first_edge_r, side - reach), (first_edge_l, 0)):
                made = None
                for j in range(side // reach):
                    moved = rolled(slow_tile[0, pl.ds(reach + reach * j, reach), :], reach * j - source, 1)
                    made = moved if made is None else jnp.where(lane >= reach * j, moved, made)
                target[...] = made
            return
        first, count = stages[stage]
        for target, source in ((slow_edge_r, side - reach), (slow_edge_l, 0)):
            made = None
            for j in range(count):
                moved = rolled(slow_tile[first + j, pl.ds(reach, side), :], reach * j - source, 1)
                made = moved if made is None else jnp.where(lane >= reach * j, moved, made)
            target[...] = made

    def unpack_first_halo():
        for halo, target in ((first_halo_l, wide_halo_l), (first_halo_r, wide_halo_r)):
            target[pl.ds(0, reach), :] = rolled(halo[0], -(side - reach), 1)
            for j in range(side // reach):
                target[pl.ds(reach + reach * j, reach), :] = rolled(halo[1], -reach * j, 1)
            target[pl.ds(reach + side, reach), :] = halo[2]

    for d in range(depths):
        rest = reach - (ahead[d] if d < depths - 1 else 0)
        slow_tile[d, pl.ds(0, rest), :] = jnp.zeros((rest, side), jnp.float32)
        slow_tile[d, pl.ds(extent - rest, rest), :] = jnp.zeros((rest, side), jnp.float32)
    rest = reach - ahead[1]
    for halo in (slow_halo_l, slow_halo_r):
        halo[pl.ds(0, rest), :] = jnp.zeros((rest, side), jnp.float32)
        halo[pl.ds(extent - rest, rest), :] = jnp.zeros((rest, side), jnp.float32)

    pl.semaphore_wait(barrier, greeted)
    slow_first = start(slow_peer_copies(0))
    start_near(wave_copies)

    lanes8 = lax.broadcasted_iota(jnp.int32, (8, 128), 1)
    subs8 = lax.broadcasted_iota(jnp.int32, (8, 128), 0)

    def inside_x(xi, lanes):
        x = me_x * side - reach + lax.rem(lanes, lane_blocks) * nx + xi
        return (x >= 0) & (x < xcount * side)

    def fill_quarters(d):
        def fill_quarter(yi, _):
            y = me_y * side - around_y[d] + subs8 * blocks_y[d] + yi
            inside_y = jnp.where((y >= 0) & (y < ycount * side), 0.25, 0.0)
            for xi in range(nx):
                rows = pl.ds(pl.multiple_of((yi * nx + xi) * 8, 8), 8)
                quarter[d, rows, :] = jnp.where(inside_x(xi, lanes8), inside_y, 0.0)
            return 0

        lax.fori_loop(0, blocks_y[d], fill_quarter, 0)

    def fill_all_quarters():
        for d in range(depths):
            fill_quarters(d)

    def blocks_of(load):
        return jnp.concatenate([load(8 * nx * o) for o in range(octets)], axis=0)

    def place_slow_tile(d):
        for xi in range(nx):
            cells = blocks_of(lambda begin: slow_tile[d, pl.ds(xi + begin, 8, stride=nx), :])
            slow_rows[d, xi, pl.ds(around_y[d], side), :] = jnp.concatenate([cells] * freqs, axis=0).T

    def place_slow_halo(stage):
        first, count = stages[stage]
        if stage == 0:
            edges_l, edges_r = wide_halo_l, wide_halo_r
        else:
            edges_l, edges_r = slow_halo_l, slow_halo_r
        for pair in range(0, count, 2):
            for xi in range(nx):
                from_l = blocks_of(lambda begin: edges_l[pl.ds(xi + begin, 8, stride=nx), :])
                from_r = blocks_of(lambda begin: edges_r[pl.ds(xi + begin, 8, stride=nx), :])
                made = jnp.where(lane < reach, rolled(from_l, -reach * pair, 1), rolled(from_r, reach - reach * pair, 1))
                if pair + 1 < count:
                    made = jnp.where(lane < 2 * reach, made, rolled(from_l, reach * (1 - pair), 1))
                    made = jnp.where(lane < 3 * reach, made, rolled(from_r, reach * (2 - pair), 1))
                turned = jnp.concatenate([made] * freqs, axis=0).T
                for j in range(min(2, count - pair)):
                    d = first + pair + j
                    h = around_y[d]
                    base = 2 * reach * j
                    slow_rows[d, xi, pl.ds(0, h), :] = turned[base + reach - h : base + reach]
                    slow_rows[d, xi, pl.ds(h + side, h), :] = turned[base + reach : base + reach + h]

    def assemble_wave():
        ny = blocks_y[0]
        inside_l = jnp.where(me_y > 0, 1.0, 0.0)
        inside_r = jnp.where(me_y < ycount - 1, 1.0, 0.0)

        def put(part, xi, y0, block):
            yb, yi = y0 // ny, y0 % ny
            begin = ((yi * 2 + part) * nx + xi) * 8 + yb
            terms[0, pl.ds(begin, 8, stride=slab_rows), :] = block

        def middle(i, _):
            for j in range(3):
                xi = i * 3 + j
                grid_x = jnp.where(inside_x(xi, lane), 1.0, 0.0)
                for part in range(2):
                    cells = jnp.concatenate(
                        [
                            blocks_of(lambda begin: tile[part * freqs + f, pl.ds(xi + begin, 8, stride=nx), :])
                            for f in range(freqs)
                        ],
                        axis=0,
                    )
                    turned = cells.T * grid_x
                    for o in range(side // 8):
                        put(part, xi, reach + 8 * o, turned[8 * o : 8 * o + 8])
            return 0

        def beside(i, _):
            for j in range(3):
                xi = i * 3 + j
                grid_x = jnp.where(inside_x(xi, lane), 1.0, 0.0)
                cells = []
                for f in range(freqs):
                    both = []
                    for part in range(2):
                        k, g = (part * freqs + f) // groups, (part * freqs + f) % groups
                        from_l = blocks_of(lambda begin: halo_l[g, pl.ds(xi + begin, 8, stride=nx), :])
                        from_r = blocks_of(lambda begin: halo_r[g, pl.ds(xi + begin, 8, stride=nx), :])
                        at = 2 * reach * part
                        both.append(
                            jnp.where(
                                lane < at + reach, rolled(from_l, at - k * reach, 1), rolled(from_r, at + reach - k * reach, 1)
                            )
                        )
                    cells.append(jnp.where(lane < 2 * reach, both[0], both[1]))
                turned = jnp.concatenate(cells, axis=0).T
                for part in range(2):
                    at = 2 * reach * part
                    beside_l = turned[at : at + reach] * (grid_x * inside_l)
                    beside_r = turned[at + reach : at + 2 * reach] * (grid_x * inside_r)
                    for o in range(reach // 8):
                        put(part, xi, 8 * o, beside_l[8 * o : 8 * o + 8])
                        put(part, xi, reach + side + 8 * o, beside_r[8 * o : 8 * o + 8])
            return 0

        wait_near(wave_copies[:2])
        lax.fori_loop(0, nx // 3, middle, 0)
        wait_near(wave_copies[2:])
        lax.fori_loop(0, nx // 3, beside, 0)

    def slab(n, yi):
        return terms[n, pl.ds(yi * slab_rows, slab_rows), :].reshape(2, nx, 8, 128)

    def x_sum(cells):
        before = pltpu.roll(cells[:, nx - 1 : nx], 1, 3)
        after = pltpu.roll(cells[:, 0:1], 127, 3)
        wide = jnp.concatenate([before, cells, after], axis=1)
        twos = wide[:, :-1] + wide[:, 1:]
        return twos[:, :-1] + twos[:, 1:]

    def next_term(d, n, first):
        ny = blocks_y[d]
        here = slab(n, 0)
        sum_here = x_sum(here)
        sum_first = sum_here
        twos = pltpu.roll(x_sum(slab(n, ny - 1)), 1, 2) + sum_here
        for yi in range(ny):
            if yi + 1 < ny:
                after = slab(n, yi + 1)
                sum_after = x_sum(after)
            else:
                after = None
                sum_after = pltpu.roll(sum_first, 7, 2)
            twos_after = sum_here + sum_after
            nine = twos + twos_after
            rows = pl.ds(yi * slab_rows, slab_rows)
            scale = quarter[d, pl.ds(yi * nx * 8, nx * 8), :].reshape(1, nx, 8, 128)
            if first:
                pair = (0.5 * scale) * nine
            else:
                pair = scale * nine - pair_sum[rows, :].reshape(2, nx, 8, 128)
            pair_sum[rows, :] = pair.reshape(slab_rows, 128)
            terms[n + 1, rows, :] = (pair - here).reshape(slab_rows, 128)
            twos, sum_here, here = twos_after, sum_after, after

    def all_terms(d):
        next_term(d, 0, True)

        def body(n, _):
            next_term(d, n, False)
            return 0

        lax.fori_loop(1, order, body, 0)

    frequency = me_f * freqs + lanes8 // lane_blocks
    omega = (2.0 * math.pi) * (
        LOWEST + (HIGHEST - LOWEST) * (frequency.astype(jnp.float32) + 0.5) / (freqs * fcount)
    )

    def phase_sum(d):
        ny = blocks_y[d]

        def chunk(yi0, count):
            rows = pl.ds(pl.multiple_of(yi0 * slab_rows, 8), count * slab_rows)

            def term(n):
                return terms[n, rows, :].reshape(count, 2, nx, 8, 128)

            slow = jnp.concatenate(
                [
                    slow_rows[d, xi, pl.ds(yi0 + j, 8, stride=ny), :][None]
                    for j in range(count)
                    for xi in range(nx)
                ],
                axis=0,
            )
            angle = (omega * slow).reshape(count, 1, nx, 8, 128)
            square = angle * angle
            cosine = 1.0 + square * (-0.5 + square * (1 / 24.0 + square * (-1 / 720.0)))
            sine = angle * (1.0 + square * (-0.16666656 + square * 0.00831999))
            double = cosine + cosine
            later = weights[order] * term(order)
            now = weights[order - 1] * term(order - 1) + double * later
            for n in range(order - 2, 0, -1):
                now, later = weights[n] * term(n) + double * now - later, now
            now, later = term(0) + double * now - later, now
            straight = cosine * now - later
            real = straight[:, 0] - sine[:, 0] * now[:, 1]
            imag = straight[:, 1] + sine[:, 0] * now[:, 0]
            for j in range(count):
                for xi in range(nx):
                    rows_buf[0, xi, pl.ds(yi0 + j, 8, stride=ny), :] = real[j, xi]
                    rows_buf[1, xi, pl.ds(yi0 + j, 8, stride=ny), :] = imag[j, xi]

        size = 4

        def body(i, _):
            chunk(i * size, size)
            return 0

        lax.fori_loop(0, ny // size, body, 0)
        if ny % size:
            chunk(ny - ny % size, ny % size)

    def turn(part, xi, h):
        return rows_buf[part, xi, pl.ds(h, side), :].T

    def make_image(d):
        def some(i, _):
            for j in range(3):
                xi = i * 3 + j
                turned = turn(0, xi, around_y[d])
                for o in range(octets):
                    total = turned[8 * o : 8 * o + 8]
                    for f in range(1, freqs):
                        total = total + turned[f * lane_blocks + 8 * o : f * lane_blocks + 8 * o + 8]
                    part_image[d, pl.ds(xi + 8 * nx * o, 8, stride=nx), :] = total
                if d + 1 < depths:
                    ny = blocks_y[d + 1]
                    for yi in range(ny):
                        for part in range(2):
                            rows = pl.ds(pl.multiple_of(((yi * 2 + part) * nx + xi) * 8, 8), 8)
                            terms[0, rows, :] = rows_buf[part, xi, pl.ds(order + yi, 8, stride=ny), :]
            return 0

        lax.fori_loop(0, nx // 3, some, 0)

    def make_natural():
        h = around_y[depths - 1]

        def some(i, _):
            for j in range(3):
                xi = i * 3 + j
                for part in range(2):
                    turned = turn(part, xi, h)
                    for f in range(freqs):
                        for o in range(octets):
                            at = f * lane_blocks + 8 * o
                            natural[part * freqs + f, pl.ds(xi + 8 * nx * o, 8, stride=nx), :] = turned[at : at + 8]
            return 0

        lax.fori_loop(0, nx // 3, some, 0)
        for f in range(freqs):
            for part in range(2):
                out_ref[f, part] = natural[part * freqs + f, pl.ds(reach, side), :] * shared_weight(order) ** depths

    image_stages = [(0, depths - 1), (depths - 1, 1)]
    image_rows = pl.ds(pl.multiple_of(me_f * strip, 8), strip)

    def reduce_copies(stage):
        first, count = image_stages[stage]
        of = pl.ds(first, count)
        return to_peers(
            [
                (
                    part_image.at[of, pl.ds(pl.multiple_of(reach + peer * strip, 8), strip)],
                    image_in.at[k, of],
                )
                for k, peer in enumerate(peers)
            ],
            red_send.at[stage], red_recv.at[stage],
        )

    def cast_image(stage):
        first, count = image_stages[stage]
        of = pl.ds(first, count)
        total = part_image[of, own_rows, :]
        for k in range(fcount - 1):
            total = total + image_in[k, of]
        for d in range(first, first + count):
            scale = shared_weight(order) ** (d + 1) / math.sqrt(freqs * fcount)
            image_out[d, image_rows, :] = total[d - first] * scale
        block = image_out.at[of, image_rows]
        return start(to_peers([(block, block)] * (fcount - 1), cast_send.at[stage], cast_recv.at[stage]))

    wait(slow_first)
    build_slow_edges(0)
    halo_first = start_near(slow_halo_copies(0))
    slow_rest = start(slow_peer_copies(1))
    fill_all_quarters()
    assemble_wave()
    casts = []
    for d in range(depths):
        all_terms(d)
        if d == 0:
            wait_near(halo_first)
            unpack_first_halo()
            place_slow_tile(0)
            place_slow_halo(0)
            wait(slow_rest)
            build_slow_edges(1)
            halo_rest = start_near(slow_halo_copies(1))
        if d == 1:
            wait_near(halo_rest)
            for e in range(1, depths):
                place_slow_tile(e)
            place_slow_halo(1)
        phase_sum(d)
        make_image(d)
        if d == depths - 2:
            reduced = start(reduce_copies(0))
    last = start(reduce_copies(1))
    make_natural()
    wait(reduced)
    casts += cast_image(0)
    wait(last)
    casts += cast_image(1)
    wait(casts)
    image_ref[...] = image_out[...]


def per_device(wavefield, velocity):
    freqs, _, side, _ = wavefield.shape
    depths = velocity.shape[0]
    fcount, xcount, ycount = lax.axis_size("freq"), lax.axis_size("gx"), lax.axis_size("gy")
    reach = ORDER * depths
    extent = side + 2 * reach
    nx, ny = extent * freqs // 128, extent // SUB_BLOCKS
    cells = nx * ny * 8
    batch = 2 * freqs
    groups = batch * reach // 128
    strip = side // fcount
    dims = (depths, freqs, side, fcount, xcount, ycount)
    f32 = jnp.float32
    dma = pltpu.SemaphoreType.DMA
    image, extrapolated = pl.pallas_call(
        functools.partial(kernel, dims),
        out_shape=(
            pltpu.VMEM((depths, side, side), f32),
            pltpu.VMEM(wavefield.shape, f32),
        ),
        in_specs=[pl.BlockSpec(memory_space=pltpu.HBM)] * 2,
        out_specs=(pl.BlockSpec(memory_space=pltpu.VMEM),) * 2,
        scratch_shapes=[
            pltpu.VMEM((ORDER + 1, 2 * cells, 128), f32),
            pltpu.VMEM((2 * cells, 128), f32),
            pltpu.VMEM((depths, cells, 128), f32),
            pltpu.VMEM((2, nx, extent, 128), f32),
            pltpu.VMEM((depths, nx, extent, 128), f32),
            pltpu.VMEM((batch, extent, 128), f32),
            pltpu.VMEM((groups, side, 128), f32),
            pltpu.VMEM((groups, side, 128), f32),
            pltpu.VMEM((groups, extent, 128), f32),
            pltpu.VMEM((groups, extent, 128), f32),
            pltpu.VMEM((batch, extent, 128), f32),
            pltpu.VMEM((depths, strip, 128), f32),
            pltpu.VMEM((depths, extent, 128), f32),
            pltpu.VMEM((side, 128), f32),
            pltpu.VMEM((side, 128), f32),
            pltpu.VMEM((extent, 128), f32),
            pltpu.VMEM((extent, 128), f32),
            pltpu.VMEM((reach, 128), f32),
            pltpu.VMEM((reach, 128), f32),
            pltpu.VMEM((3, reach, 128), f32),
            pltpu.VMEM((3, reach, 128), f32),
            pltpu.VMEM((extent, 128), f32),
            pltpu.VMEM((extent, 128), f32),
            pltpu.VMEM((depths, extent, 128), f32),
            pltpu.VMEM((fcount - 1, depths, strip, 128), f32),
            pltpu.VMEM((depths, side, 128), f32),
            dma((batch + 1,)),
            dma((8,)),
            dma((8,)),
            dma((2, fcount - 1)),
            dma((2, fcount - 1)),
            dma((2, 8)),
            dma((2, 8)),
            dma((depths - 1, 2)),
            dma((depths - 1, 2)),
            dma((2, fcount - 1)),
            dma((2, fcount - 1)),
            dma((2, fcount - 1)),
            dma((2, fcount - 1)),
        ],
        compiler_params=pltpu.CompilerParams(
            collective_id=0, has_side_effects=True, vmem_limit_bytes=66_000_000
        ),
    )(wavefield, velocity)
    return (image, extrapolated)


def solution(mesh):
    placed = (P("freq", None, "gx", "gy"), P(None, ("gx", "freq"), "gy"))
    return jax.shard_map(
        per_device,
        mesh=mesh,
        in_specs=placed,
        out_specs=(P(None, "gx", "gy"), P("freq", None, "gx", "gy")),
        check_vma=False,
    )
```

```python
import functools
import math

import jax
import jax.numpy as jnp
from jax import lax
from jax.experimental import pallas as pl
from jax.experimental.pallas import tpu as pltpu
from jax.sharding import PartitionSpec as P

ORDER = 8
LOWEST = 2.0
HIGHEST = 60.0
INTERVAL = 0.01
MESH = pl.DeviceIdType.MESH
SUB_BLOCKS = 8


def ratios(order):
    return [1.0 / (term + 1) for term in range(order + 1)]


def shared_weight(order):
    return 1.0 / sum(1.0 / (term + 1) for term in range(order + 1))


def rolled(cells, shift, axis):
    shift = shift % cells.shape[axis]
    return cells if shift == 0 else pltpu.roll(cells, shift, axis)


def kernel(
    dims,
    wave_hbm, vel_hbm, image_ref, out_ref,
    terms, pair_sum, quarter, rows_buf, slow_rows, tile, edge_r, edge_l, halo_l, halo_r, natural,
    vel_raw, slow_tile, slow_edge_r, slow_edge_l, slow_halo_l, slow_halo_r,
    first_edge_r, first_edge_l, first_halo_l, first_halo_r, wide_halo_l, wide_halo_r,
    part_image, image_in, image_out,
    load_sem, wave_send, wave_recv, vel_send, vel_recv, velh_send, velh_recv, rows_send, rows_recv,
    red_send, red_recv, cast_send, cast_recv,
):
    depths, freqs, side, fcount, xcount, ycount = dims
    order = ORDER
    weights = ratios(order)
    reach = order * depths
    extent = side + 2 * reach
    lane_blocks = 128 // freqs
    octets = lane_blocks // 8
    nx = extent // lane_blocks
    slab_rows = 2 * nx * 8
    batch = 2 * freqs
    inner = 128 // reach
    groups = batch // inner
    strip = side // fcount
    around_y = [reach - order * d for d in range(depths)]
    blocks_y = [(side + 2 * h) // SUB_BLOCKS for h in around_y]

    me_f = lax.axis_index("freq")
    me_x = lax.axis_index("gx")
    me_y = lax.axis_index("gy")

    def mod(value, count):
        return lax.rem(value + count, count)

    up, down = mod(me_x - 1, xcount), mod(me_x + 1, xcount)
    left, right = mod(me_y - 1, ycount), mod(me_y + 1, ycount)
    around = [
        {"gx": up, "gy": me_y}, {"gx": down, "gy": me_y}, {"gx": me_x, "gy": right}, {"gx": me_x, "gy": left},
        {"gx": up, "gy": right}, {"gx": down, "gy": right}, {"gx": up, "gy": left}, {"gx": down, "gy": left},
    ]
    peers = [mod(me_f + k, fcount) for k in range(1, fcount)]

    has_up, has_down = me_x > 0, me_x < xcount - 1
    has_left, has_right = me_y > 0, me_y < ycount - 1
    present = [
        has_up, has_down, has_right, has_left,
        has_up & has_right, has_down & has_right, has_up & has_left, has_down & has_left,
    ]
    opposite = [1, 0, 3, 2, 7, 6, 5, 4]

    barrier = pltpu.get_barrier_semaphore()
    greeted = jnp.int32(fcount - 1)
    for way, device in enumerate(around):
        greeted = greeted + jnp.where(present[way], 1, 0)

        @pl.when(present[way])
        def _():
            pl.semaphore_signal(barrier, inc=1, device_id=device, device_id_type=MESH)

    for peer in peers:
        pl.semaphore_signal(barrier, inc=1, device_id={"freq": peer}, device_id_type=MESH)

    vel_load = pltpu.make_async_copy(vel_hbm, vel_raw, load_sem.at[batch])
    vel_load.start()
    loads = []
    for f in range(freqs):
        for part in range(2):
            loads.append(
                pltpu.make_async_copy(
                    wave_hbm.at[f, part], tile.at[part * freqs + f, pl.ds(reach, side)], load_sem.at[f * 2 + part]
                )
            )
    for copy in loads:
        copy.start()

    own_rows = pl.ds(pl.multiple_of(reach + me_f * strip, 8), strip)
    vel_load.wait()
    slow_tile[:, own_rows, :] = (INTERVAL / (order + 1)) / vel_raw[...]
    for copy in loads:
        copy.wait()

    lane = lax.broadcasted_iota(jnp.int32, (1, 128), 1)

    def build_edges(i, _):
        rows = pl.ds(pl.multiple_of(i * 32, 32), 32)
        source_rows = pl.ds(pl.multiple_of(reach + i * 32, 8), 32)
        for target, first in ((edge_r, side - reach), (edge_l, 0)):
            for g in range(groups):
                made = None
                for k in range(inner):
                    moved = rolled(tile[k * groups + g, source_rows, :], k * reach - first, 1)
                    made = moved if made is None else jnp.where(lane >= k * reach, moved, made)
                target[g, rows, :] = made
        return 0

    lax.fori_loop(0, side // 32, build_edges, 0)

    head, tail = pl.ds(0, reach), pl.ds(side - reach, reach)
    low, mid, high = pl.ds(0, reach), pl.ds(reach, side), pl.ds(reach + side, reach)
    own_head, own_tail = pl.ds(reach, reach), pl.ds(side, reach)

    def to_neighbours(pairs, send_sem, recv_sem):
        return [
            (k, pltpu.make_async_remote_copy(
                src_ref=source, dst_ref=target, send_sem=send_sem.at[k], recv_sem=recv_sem.at[k],
                device_id=around[k], device_id_type=MESH,
            ))
            for k, (source, target) in [(k, pair) for k, pair in enumerate(pairs) if pair is not None]
        ]

    def to_peers(pairs, send_sem, recv_sem):
        return [
            pltpu.make_async_remote_copy(
                src_ref=source, dst_ref=target, send_sem=send_sem.at[k], recv_sem=recv_sem.at[k],
                device_id={"freq": peers[k]}, device_id_type=MESH,
            )
            for k, (source, target) in enumerate(pairs)
        ]

    def start(copies):
        for copy in copies:
            copy.start()
        return copies

    def wait(copies):
        for copy in copies:
            copy.wait()

    def start_near(copies):
        for way in range(8):
            here = [copy for k, copy in copies if k == way]
            if here:

                @pl.when(present[way])
                def _():
                    for copy in here:
                        copy.start()

        return copies

    def wait_near(copies):
        for way in range(8):
            sent = [copy for k, copy in copies if k == way]
            received = [copy for k, copy in copies if k == opposite[way]]
            if sent or received:

                @pl.when(present[way])
                def _():
                    for copy in sent:
                        copy.wait_send()
                    for copy in received:
                        copy.wait_recv()

    def clear(refs):
        for ref in refs:
            ref[...] = jnp.zeros(ref.shape, jnp.float32)

    @pl.when(me_y == 0)
    def _():
        clear((halo_l, first_halo_l, slow_halo_l))

    @pl.when(me_y == ycount - 1)
    def _():
        clear((halo_r, first_halo_r, slow_halo_r))

    @pl.when(me_x == 0)
    def _():
        clear((tile.at[:, low], slow_tile.at[:, low]))
        for wide, first, later in ((halo_l, first_halo_l, slow_halo_l), (halo_r, first_halo_r, slow_halo_r)):
            clear((wide.at[:, low], first.at[0], later.at[low]))

    @pl.when(me_x == xcount - 1)
    def _():
        clear((tile.at[:, high], slow_tile.at[:, high]))
        for wide, first, later in ((halo_l, first_halo_l, slow_halo_l), (halo_r, first_halo_r, slow_halo_r)):
            clear((wide.at[:, high], first.at[2], later.at[high]))

    wave_copies = to_neighbours(
        [
            (tile.at[:, own_head], tile.at[:, high]),
            (tile.at[:, own_tail], tile.at[:, low]),
            (edge_r, halo_l.at[:, mid]),
            (edge_l, halo_r.at[:, mid]),
            (edge_r.at[:, head], halo_l.at[:, high]),
            (edge_r.at[:, tail], halo_l.at[:, low]),
            (edge_l.at[:, head], halo_r.at[:, high]),
            (edge_l.at[:, tail], halo_r.at[:, low]),
        ],
        wave_send, wave_recv,
    )
    stages = [(0, 1), (1, depths - 1)]
    ahead = [reach - order * (d + 1) for d in range(depths)]

    def slow_peer_copies(stage):
        first, count = stages[stage]
        block = slow_tile.at[pl.ds(first, count), own_rows]
        return to_peers([(block, block)] * (fcount - 1), vel_send.at[stage], vel_recv.at[stage])

    def slow_halo_copies(stage):
        copies = []
        for k, d in enumerate([0] if stage == 0 else range(1, depths - 1)):
            w = ahead[d]
            rows = [
                (slow_tile.at[d, pl.ds(reach, w)], slow_tile.at[d, pl.ds(reach + side, w)]),
                (slow_tile.at[d, pl.ds(reach + side - w, w)], slow_tile.at[d, pl.ds(reach - w, w)]),
            ]
            copies += to_neighbours(rows, rows_send.at[stage + k], rows_recv.at[stage + k])
        if stage == 0:
            sides = [(first_edge_r, first_halo_l.at[1]), (first_edge_l, first_halo_r.at[1])]
            for edge, halo in ((first_edge_r, first_halo_l), (first_edge_l, first_halo_r)):
                sides += [(edge, halo.at[2]), (edge, halo.at[0])]
        else:
            w = ahead[1]
            sides = [(slow_edge_r, slow_halo_l.at[mid]), (slow_edge_l, slow_halo_r.at[mid])]
            for edge, halo in ((slow_edge_r, slow_halo_l), (slow_edge_l, slow_halo_r)):
                sides += [
                    (edge.at[pl.ds(0, w)], halo.at[pl.ds(reach + side, w)]),
                    (edge.at[pl.ds(side - w, w)], halo.at[pl.ds(reach - w, w)]),
                ]
        return copies + to_neighbours([None, None] + sides, velh_send.at[stage], velh_recv.at[stage])

    def build_slow_edges(stage):
        if stage == 0:
            for target, source in ((first_edge_r, side - reach), (first_edge_l, 0)):
                made = None
                for j in range(side // reach):
                    moved = rolled(slow_tile[0, pl.ds(reach + reach * j, reach), :], reach * j - source, 1)
                    made = moved if made is None else jnp.where(lane >= reach * j, moved, made)
                target[...] = made
            return
        first, count = stages[stage]
        for target, source in ((slow_edge_r, side - reach), (slow_edge_l, 0)):
            made = None
            for j in range(count):
                moved = rolled(slow_tile[first + j, pl.ds(reach, side), :], reach * j - source, 1)
                made = moved if made is None else jnp.where(lane >= reach * j, moved, made)
            target[...] = made

    def unpack_first_halo():
        for halo, target in ((first_halo_l, wide_halo_l), (first_halo_r, wide_halo_r)):
            target[pl.ds(0, reach), :] = rolled(halo[0], -(side - reach), 1)
            for j in range(side // reach):
                target[pl.ds(reach + reach * j, reach), :] = rolled(halo[1], -reach * j, 1)
            target[pl.ds(reach + side, reach), :] = halo[2]

    for d in range(depths):
        rest = reach - (ahead[d] if d < depths - 1 else 0)
        slow_tile[d, pl.ds(0, rest), :] = jnp.zeros((rest, side), jnp.float32)
        slow_tile[d, pl.ds(extent - rest, rest), :] = jnp.zeros((rest, side), jnp.float32)
    rest = reach - ahead[1]
    for halo in (slow_halo_l, slow_halo_r):
        halo[pl.ds(0, rest), :] = jnp.zeros((rest, side), jnp.float32)
        halo[pl.ds(extent - rest, rest), :] = jnp.zeros((rest, side), jnp.float32)

    pl.semaphore_wait(barrier, greeted)
    slow_first = start(slow_peer_copies(0))
    start_near(wave_copies)

    lanes8 = lax.broadcasted_iota(jnp.int32, (8, 128), 1)
    subs8 = lax.broadcasted_iota(jnp.int32, (8, 128), 0)

    def inside_x(xi, lanes):
        x = me_x * side - reach + lax.rem(lanes, lane_blocks) * nx + xi
        return (x >= 0) & (x < xcount * side)

    def fill_quarters(d):
        def fill_quarter(yi, _):
            y = me_y * side - around_y[d] + subs8 * blocks_y[d] + yi
            inside_y = jnp.where((y >= 0) & (y < ycount * side), 0.25, 0.0)
            for xi in range(nx):
                rows = pl.ds(pl.multiple_of((yi * nx + xi) * 8, 8), 8)
                quarter[d, rows, :] = jnp.where(inside_x(xi, lanes8), inside_y, 0.0)
            return 0

        lax.fori_loop(0, blocks_y[d], fill_quarter, 0)

    def fill_all_quarters():
        for d in range(depths):
            fill_quarters(d)

    def blocks_of(load):
        return jnp.concatenate([load(8 * nx * o) for o in range(octets)], axis=0)

    def place_slow_tile(d):
        for xi in range(nx):
            cells = blocks_of(lambda begin: slow_tile[d, pl.ds(xi + begin, 8, stride=nx), :])
            slow_rows[d, xi, pl.ds(around_y[d], side), :] = jnp.concatenate([cells] * freqs, axis=0).T

    def place_slow_halo(stage):
        first, count = stages[stage]
        if stage == 0:
            edges_l, edges_r = wide_halo_l, wide_halo_r
        else:
            edges_l, edges_r = slow_halo_l, slow_halo_r
        for pair in range(0, count, 2):
            for xi in range(nx):
                from_l = blocks_of(lambda begin: edges_l[pl.ds(xi + begin, 8, stride=nx), :])
                from_r = blocks_of(lambda begin: edges_r[pl.ds(xi + begin, 8, stride=nx), :])
                made = jnp.where(lane < reach, rolled(from_l, -reach * pair, 1), rolled(from_r, reach - reach * pair, 1))
                if pair + 1 < count:
                    made = jnp.where(lane < 2 * reach, made, rolled(from_l, reach * (1 - pair), 1))
                    made = jnp.where(lane < 3 * reach, made, rolled(from_r, reach * (2 - pair), 1))
                turned = jnp.concatenate([made] * freqs, axis=0).T
                for j in range(min(2, count - pair)):
                    d = first + pair + j
                    h = around_y[d]
                    base = 2 * reach * j
                    slow_rows[d, xi, pl.ds(0, h), :] = turned[base + reach - h : base + reach]
                    slow_rows[d, xi, pl.ds(h + side, h), :] = turned[base + reach : base + reach + h]

    def assemble_wave():
        ny = blocks_y[0]
        inside_l = jnp.where(me_y > 0, 1.0, 0.0)
        inside_r = jnp.where(me_y < ycount - 1, 1.0, 0.0)

        def put(part, xi, y0, block):
            yb, yi = y0 // ny, y0 % ny
            begin = ((yi * 2 + part) * nx + xi) * 8 + yb
            terms[0, pl.ds(begin, 8, stride=slab_rows), :] = block

        def middle(i, _):
            for j in range(3):
                xi = i * 3 + j
                grid_x = jnp.where(inside_x(xi, lane), 1.0, 0.0)
                for part in range(2):
                    cells = jnp.concatenate(
                        [
                            blocks_of(lambda begin: tile[part * freqs + f, pl.ds(xi + begin, 8, stride=nx), :])
                            for f in range(freqs)
                        ],
                        axis=0,
                    )
                    turned = cells.T * grid_x
                    for o in range(side // 8):
                        put(part, xi, reach + 8 * o, turned[8 * o : 8 * o + 8])
            return 0

        def beside(i, _):
            for j in range(3):
                xi = i * 3 + j
                grid_x = jnp.where(inside_x(xi, lane), 1.0, 0.0)
                cells = []
                for f in range(freqs):
                    both = []
                    for part in range(2):
                        k, g = (part * freqs + f) // groups, (part * freqs + f) % groups
                        from_l = blocks_of(lambda begin: halo_l[g, pl.ds(xi + begin, 8, stride=nx), :])
                        from_r = blocks_of(lambda begin: halo_r[g, pl.ds(xi + begin, 8, stride=nx), :])
                        at = 2 * reach * part
                        both.append(
                            jnp.where(
                                lane < at + reach, rolled(from_l, at - k * reach, 1), rolled(from_r, at + reach - k * reach, 1)
                            )
                        )
                    cells.append(jnp.where(lane < 2 * reach, both[0], both[1]))
                turned = jnp.concatenate(cells, axis=0).T
                for part in range(2):
                    at = 2 * reach * part
                    beside_l = turned[at : at + reach] * (grid_x * inside_l)
                    beside_r = turned[at + reach : at + 2 * reach] * (grid_x * inside_r)
                    for o in range(reach // 8):
                        put(part, xi, 8 * o, beside_l[8 * o : 8 * o + 8])
                        put(part, xi, reach + side + 8 * o, beside_r[8 * o : 8 * o + 8])
            return 0

        wait_near(wave_copies[:2])
        lax.fori_loop(0, nx // 3, middle, 0)
        wait_near(wave_copies[2:])
        lax.fori_loop(0, nx // 3, beside, 0)

    def slab(n, yi):
        return terms[n, pl.ds(yi * slab_rows, slab_rows), :].reshape(2, nx, 8, 128)

    def x_sum(cells):
        before = pltpu.roll(cells[:, nx - 1 : nx], 1, 3)
        after = pltpu.roll(cells[:, 0:1], 127, 3)
        wide = jnp.concatenate([before, cells, after], axis=1)
        twos = wide[:, :-1] + wide[:, 1:]
        return twos[:, :-1] + twos[:, 1:]

    def next_term(d, n, first):
        ny = blocks_y[d]
        here = slab(n, 0)
        sum_here = x_sum(here)
        sum_first = sum_here
        twos = pltpu.roll(x_sum(slab(n, ny - 1)), 1, 2) + sum_here
        for yi in range(ny):
            if yi + 1 < ny:
                after = slab(n, yi + 1)
                sum_after = x_sum(after)
            else:
                after = None
                sum_after = pltpu.roll(sum_first, 7, 2)
            twos_after = sum_here + sum_after
            nine = twos + twos_after
            rows = pl.ds(yi * slab_rows, slab_rows)
            scale = quarter[d, pl.ds(yi * nx * 8, nx * 8), :].reshape(1, nx, 8, 128)
            if first:
                pair = (0.5 * scale) * nine
            else:
                pair = scale * nine - pair_sum[rows, :].reshape(2, nx, 8, 128)
            pair_sum[rows, :] = pair.reshape(slab_rows, 128)
            terms[n + 1, rows, :] = (pair - here).reshape(slab_rows, 128)
            twos, sum_here, here = twos_after, sum_after, after

    def all_terms(d):
        next_term(d, 0, True)

        def body(n, _):
            next_term(d, n, False)
            return 0

        lax.fori_loop(1, order, body, 0)

    frequency = me_f * freqs + lanes8 // lane_blocks
    omega = (2.0 * math.pi) * (
        LOWEST + (HIGHEST - LOWEST) * (frequency.astype(jnp.float32) + 0.5) / (freqs * fcount)
    )

    def phase_sum(d):
        ny = blocks_y[d]

        def chunk(yi0, count):
            rows = pl.ds(pl.multiple_of(yi0 * slab_rows, 8), count * slab_rows)

            def term(n):
                return terms[n, rows, :].reshape(count, 2, nx, 8, 128)

            slow = jnp.concatenate(
                [
                    slow_rows[d, xi, pl.ds(yi0 + j, 8, stride=ny), :][None]
                    for j in range(count)
                    for xi in range(nx)
                ],
                axis=0,
            )
            angle = (omega * slow).reshape(count, 1, nx, 8, 128)
            square = angle * angle
            cosine = 1.0 + square * (-0.5 + square * (1 / 24.0 + square * (-1 / 720.0)))
            sine = angle * (1.0 + square * (-0.16666656 + square * 0.00831999))
            double = cosine + cosine
            later = weights[order] * term(order)
            now = weights[order - 1] * term(order - 1) + double * later
            for n in range(order - 2, 0, -1):
                now, later = weights[n] * term(n) + double * now - later, now
            now, later = term(0) + double * now - later, now
            straight = cosine * now - later
            real = straight[:, 0] - sine[:, 0] * now[:, 1]
            imag = straight[:, 1] + sine[:, 0] * now[:, 0]
            for j in range(count):
                for xi in range(nx):
                    rows_buf[0, xi, pl.ds(yi0 + j, 8, stride=ny), :] = real[j, xi]
                    rows_buf[1, xi, pl.ds(yi0 + j, 8, stride=ny), :] = imag[j, xi]

        size = 6

        def body(i, _):
            chunk(i * size, size)
            return 0

        lax.fori_loop(0, ny // size, body, 0)
        if ny % size:
            chunk(ny - ny % size, ny % size)

    def turn(part, xi, h):
        return rows_buf[part, xi, pl.ds(h, side), :].T

    def make_image(d):
        def some(i, _):
            for j in range(3):
                xi = i * 3 + j
                turned = turn(0, xi, around_y[d])
                for o in range(octets):
                    total = turned[8 * o : 8 * o + 8]
                    for f in range(1, freqs):
                        total = total + turned[f * lane_blocks + 8 * o : f * lane_blocks + 8 * o + 8]
                    part_image[d, pl.ds(xi + 8 * nx * o, 8, stride=nx), :] = total
                if d + 1 < depths:
                    ny = blocks_y[d + 1]
                    for yi in range(ny):
                        for part in range(2):
                            rows = pl.ds(pl.multiple_of(((yi * 2 + part) * nx + xi) * 8, 8), 8)
                            terms[0, rows, :] = rows_buf[part, xi, pl.ds(order + yi, 8, stride=ny), :]
            return 0

        lax.fori_loop(0, nx // 3, some, 0)

    def make_natural():
        h = around_y[depths - 1]

        def some(i, _):
            for j in range(3):
                xi = i * 3 + j
                for part in range(2):
                    turned = turn(part, xi, h)
                    for f in range(freqs):
                        for o in range(octets):
                            at = f * lane_blocks + 8 * o
                            natural[part * freqs + f, pl.ds(xi + 8 * nx * o, 8, stride=nx), :] = turned[at : at + 8]
            return 0

        lax.fori_loop(0, nx // 3, some, 0)
        for f in range(freqs):
            for part in range(2):
                out_ref[f, part] = natural[part * freqs + f, pl.ds(reach, side), :] * shared_weight(order) ** depths

    image_stages = [(0, depths - 1), (depths - 1, 1)]
    image_rows = pl.ds(pl.multiple_of(me_f * strip, 8), strip)

    def reduce_copies(stage):
        first, count = image_stages[stage]
        of = pl.ds(first, count)
        return to_peers(
            [
                (
                    part_image.at[of, pl.ds(pl.multiple_of(reach + peer * strip, 8), strip)],
                    image_in.at[k, of],
                )
                for k, peer in enumerate(peers)
            ],
            red_send.at[stage], red_recv.at[stage],
        )

    def cast_image(stage):
        first, count = image_stages[stage]
        of = pl.ds(first, count)
        total = part_image[of, own_rows, :]
        for k in range(fcount - 1):
            total = total + image_in[k, of]
        for d in range(first, first + count):
            scale = shared_weight(order) ** (d + 1) / math.sqrt(freqs * fcount)
            image_out[d, image_rows, :] = total[d - first] * scale
        block = image_out.at[of, image_rows]
        return start(to_peers([(block, block)] * (fcount - 1), cast_send.at[stage], cast_recv.at[stage]))

    wait(slow_first)
    build_slow_edges(0)
    halo_first = start_near(slow_halo_copies(0))
    slow_rest = start(slow_peer_copies(1))
    fill_all_quarters()
    assemble_wave()
    casts = []
    for d in range(depths):
        all_terms(d)
        if d == 0:
            wait_near(halo_first)
            unpack_first_halo()
            place_slow_tile(0)
            place_slow_halo(0)
            wait(slow_rest)
            build_slow_edges(1)
            halo_rest = start_near(slow_halo_copies(1))
        if d == 1:
            wait_near(halo_rest)
            for e in range(1, depths):
                place_slow_tile(e)
            place_slow_halo(1)
        phase_sum(d)
        make_image(d)
        if d == depths - 2:
            reduced = start(reduce_copies(0))
    last = start(reduce_copies(1))
    make_natural()
    wait(reduced)
    casts += cast_image(0)
    wait(last)
    casts += cast_image(1)
    wait(casts)
    image_ref[...] = image_out[...]


def per_device(wavefield, velocity):
    freqs, _, side, _ = wavefield.shape
    depths = velocity.shape[0]
    fcount, xcount, ycount = lax.axis_size("freq"), lax.axis_size("gx"), lax.axis_size("gy")
    reach = ORDER * depths
    extent = side + 2 * reach
    nx, ny = extent * freqs // 128, extent // SUB_BLOCKS
    cells = nx * ny * 8
    batch = 2 * freqs
    groups = batch * reach // 128
    strip = side // fcount
    dims = (depths, freqs, side, fcount, xcount, ycount)
    f32 = jnp.float32
    dma = pltpu.SemaphoreType.DMA
    image, extrapolated = pl.pallas_call(
        functools.partial(kernel, dims),
        out_shape=(
            pltpu.VMEM((depths, side, side), f32),
            pltpu.VMEM(wavefield.shape, f32),
        ),
        in_specs=[pl.BlockSpec(memory_space=pltpu.HBM)] * 2,
        out_specs=(pl.BlockSpec(memory_space=pltpu.VMEM),) * 2,
        scratch_shapes=[
            pltpu.VMEM((ORDER + 1, 2 * cells, 128), f32),
            pltpu.VMEM((2 * cells, 128), f32),
            pltpu.VMEM((depths, cells, 128), f32),
            pltpu.VMEM((2, nx, extent, 128), f32),
            pltpu.VMEM((depths, nx, extent, 128), f32),
            pltpu.VMEM((batch, extent, 128), f32),
            pltpu.VMEM((groups, side, 128), f32),
            pltpu.VMEM((groups, side, 128), f32),
            pltpu.VMEM((groups, extent, 128), f32),
            pltpu.VMEM((groups, extent, 128), f32),
            pltpu.VMEM((batch, extent, 128), f32),
            pltpu.VMEM((depths, strip, 128), f32),
            pltpu.VMEM((depths, extent, 128), f32),
            pltpu.VMEM((side, 128), f32),
            pltpu.VMEM((side, 128), f32),
            pltpu.VMEM((extent, 128), f32),
            pltpu.VMEM((extent, 128), f32),
            pltpu.VMEM((reach, 128), f32),
            pltpu.VMEM((reach, 128), f32),
            pltpu.VMEM((3, reach, 128), f32),
            pltpu.VMEM((3, reach, 128), f32),
            pltpu.VMEM((extent, 128), f32),
            pltpu.VMEM((extent, 128), f32),
            pltpu.VMEM((depths, extent, 128), f32),
            pltpu.VMEM((fcount - 1, depths, strip, 128), f32),
            pltpu.VMEM((depths, side, 128), f32),
            dma((batch + 1,)),
            dma((8,)),
            dma((8,)),
            dma((2, fcount - 1)),
            dma((2, fcount - 1)),
            dma((2, 8)),
            dma((2, 8)),
            dma((depths - 1, 2)),
            dma((depths - 1, 2)),
            dma((2, fcount - 1)),
            dma((2, fcount - 1)),
            dma((2, fcount - 1)),
            dma((2, fcount - 1)),
        ],
        compiler_params=pltpu.CompilerParams(
            collective_id=0, has_side_effects=True, vmem_limit_bytes=66_000_000
        ),
    )(wavefield, velocity)
    return (image, extrapolated)


def solution(mesh):
    placed = (P("freq", None, "gx", "gy"), P(None, ("gx", "freq"), "gy"))
    return jax.shard_map(
        per_device,
        mesh=mesh,
        in_specs=placed,
        out_specs=(P(None, "gx", "gy"), P("freq", None, "gx", "gy")),
        check_vma=False,
    )
```
